32 devices in a mesh: section: 8 (over z, x), ctx: 4 (over y, core).
Axes of the slice: x: 2, y: 2, z: 4, core: 2. Of those that a mesh axis runs over, the one named last changes fastest.
Arguments:
- queries: bfloat16 [8, 1024, 16, 128], P('section', 'ctx'), may hold values from -12 to 12
- keys: bfloat16 [8, 1024, 128], P('section', 'ctx'), may hold values from -6 to 6
- values: bfloat16 [8, 1024, 128], P('section', 'ctx'), may hold values from -6 to 6
- outputs: bfloat16 [8, 1024, 16, 128], P('section', 'ctx'), may hold values from -6 to 6, as said below
- grad_held: bfloat16 [8, 1024, 16, 128], P('section', 'ctx'), may hold values from -24 to 24
- lse: float32 [8, 16, 1024], P('section', None, 'ctx'), as said below
- span_start: int32 [8], replicated, may hold values from 0 to 896, as said below
Outputs:
- query_grad: bfloat16 [8, 1024, 16, 128], P('section', 'ctx')
- key_grad: bfloat16 [8, 1024, 128], P('section', 'ctx')
- value_grad: bfloat16 [8, 1024, 128], P('section', 'ctx')
The draws below stay inside these ranges and needn't reach their ends.
Inputs may be any that keep to these rules, and one draw needn't show every extreme that they name: `span_start`: each multiple of 128 below 1024 appears once. Entries 2 k and 2 k + 1 are the spans held by index k of ctx; they add up to 896, the smaller first. lse[s, h, i] is the log of the sum of exp(scores[s, h, i, j]) over the j with positions[j] <= positions[i]. outputs[s, i, h] is the sum over j of probs[s, h, i, j] values[s, j], rounded once.
All inputs are finite; a program needn't handle non-finite values.
Results may differ from the reference program's by a relative error of at most 0.014.
Values may be sent and summed in bfloat16 or wider, within the bound.
No kernel may reach another device: no remote copies, remote signals or barrier semaphores. Data moves between devices by JAX's collectives and lax.ppermute only.
A program may use at most 64 MiB of HBM per device.

```python
import jax
import jax.numpy as jnp
from jax import lax

HQ = 16
HD = 128
TOK_DEV = 256
SECTIONS = 8
SPANS = 8
CH = 128
SEQ = 1024
N_CTX = 4


def span_layout(key):
    order = jax.random.permutation(jax.random.fold_in(key, 11), SPANS // 2)
    lower_start = order * CH
    upper_start = (SPANS - 1 - order) * CH
    return jnp.stack([lower_start, upper_start], axis=1).reshape(SPANS).astype(jnp.int32)


def draw_span_start(key, part):
    return span_layout(key)


def draw_queries(key, part):
    key_values = jax.random.fold_in(jax.random.fold_in(key, 21), 0)
    full_shape = (SECTIONS, SEQ, HQ, HD)
    result = 2.0 * jax.random.normal(key_values, full_shape, jnp.float32)
    return jnp.clip(result, -12.0, 12.0).astype(jnp.bfloat16)


def draw_keys(key, part):
    key_values = jax.random.fold_in(jax.random.fold_in(key, 22), 0)
    full_shape = (SECTIONS, SEQ, HD)
    result = jax.random.normal(key_values, full_shape, jnp.float32)
    return jnp.clip(result, -6.0, 6.0).astype(jnp.bfloat16)


def draw_values(key, part):
    key_values = jax.random.fold_in(jax.random.fold_in(key, 23), 0)
    full_shape = (SECTIONS, SEQ, HD)
    result = jax.random.normal(key_values, full_shape, jnp.float32)
    return jnp.clip(result, -6.0, 6.0).astype(jnp.bfloat16)


def attention_forward(key, part):
    all_queries = draw_queries(key, part).astype(jnp.float32)
    all_keys = draw_keys(key, part).astype(jnp.float32)
    all_values = draw_values(key, part).astype(jnp.float32)
    starts = span_layout(key)
    positions = (starts[:, None] + jnp.arange(CH, dtype=jnp.int32)[None, :]).reshape(SEQ)
    score_scale = HD ** (-0.5)
    blocks = SPANS // 2

    def one_section(section_items):
        section_q, section_k, section_v = section_items

        def one_block(block_items):
            block_q, block_pos = block_items
            scores = jnp.einsum('rhd,cd->hrc', block_q, section_k, precision=lax.Precision.HIGHEST) * score_scale
            allowed = positions[None, None, :] <= block_pos[None, :, None]
            scores = jnp.where(allowed, scores, -jnp.inf)
            block_lse = jax.scipy.special.logsumexp(scores, axis=-1)
            probs = jnp.where(allowed, jnp.exp(scores - block_lse[:, :, None]), 0.0)
            block_out = jnp.einsum('hrc,cd->rhd', probs, section_v, precision=lax.Precision.HIGHEST)
            return (block_lse, block_out)
        block_lse, block_out = lax.map(one_block, (section_q.reshape(blocks, TOK_DEV, HQ, HD), positions.reshape(blocks, TOK_DEV)))
        return (block_lse.transpose(1, 0, 2).reshape(HQ, SEQ), block_out.reshape(SEQ, HQ, HD))
    return lax.map(one_section, (all_queries, all_keys, all_values))


def draw_lse(key, part):
    return attention_forward(key, part)[0]


def draw_outputs(key, part):
    return jnp.clip(attention_forward(key, part)[1], -6.0, 6.0).astype(jnp.bfloat16)


def shard_levels(key, shape, pieces, low, top_value):
    level = 1.0
    for dim, blocks in pieces:
        steps = jax.random.uniform(jax.random.fold_in(jax.random.fold_in(key, 6), dim), (blocks,), jnp.float32, low / len(pieces), top_value / len(pieces))
        level = level * jnp.repeat(jnp.exp(steps), shape[dim] // blocks).reshape((-1,) + (1,) * (len(shape) - 1 - dim))
    return level


def noise(own_key, dims, scale, bound, cuts=(), kind=jnp.bfloat16):
    values = jax.random.normal(own_key, dims, jnp.float32) * scale
    if len(cuts) > 0:
        values = shard_levels(own_key, dims, cuts, -0.22, 0.18) * values
    return jnp.clip(values, min=-bound, max=bound).astype(kind)


def setup_inputs(seed: int = 0) -> dict:
    key_of = jax.random.split(jax.random.key(seed), 8)
    queries = draw_queries(jax.random.fold_in(key_of[7], 71), 0)
    keys = draw_keys(jax.random.fold_in(key_of[7], 71), 0)
    values = draw_values(jax.random.fold_in(key_of[7], 71), 0)
    outputs = draw_outputs(jax.random.fold_in(key_of[7], 71), 0)
    grad_held = noise(key_of[4], (SECTIONS, SEQ, HQ, HD), 4.0, 24.0, ((0, 8), (1, 4)))
    lse = draw_lse(jax.random.fold_in(key_of[7], 71), 0)
    span_start = draw_span_start(jax.random.fold_in(key_of[7], 71), 0)
    return dict(queries=queries, keys=keys, values=values, outputs=outputs, grad_held=grad_held, lse=lse, span_start=span_start)


def block_reference(query_rows, grad_rows, lse_rows, delta_rows, query_pos, key_rows, value_rows, key_pos):
    score_scale = HD ** -0.5
    query_float = query_rows.astype(jnp.float32)
    grad_float = grad_rows.astype(jnp.float32)
    key_float = key_rows.astype(jnp.float32)
    value_float = value_rows.astype(jnp.float32)
    highest = lax.Precision.HIGHEST
    scores = jnp.einsum("rhd,cd->hrc", query_float, key_float, precision=highest) * score_scale
    allowed = key_pos[None, :] <= query_pos[:, None]
    probs = jnp.where(allowed[None], jnp.exp(scores - lse_rows[:, :, None]), 0.0)
    probs_low = lax.optimization_barrier(probs.astype(jnp.bfloat16)).astype(jnp.float32)
    grad_probs = jnp.einsum("rhd,cd->hrc", grad_float, value_float, precision=highest)
    grad_scores = lax.optimization_barrier((probs * (grad_probs - delta_rows[:, :, None])).astype(jnp.bfloat16)).astype(jnp.float32)
    query_grad = jnp.einsum("hrc,cd->rhd", grad_scores, key_float, precision=highest) * score_scale
    key_grad = jnp.einsum("hrc,rhd->cd", grad_scores, query_float, precision=highest) * score_scale
    value_grad = jnp.einsum("hrc,rhd->cd", probs_low, grad_float, precision=highest)
    return query_grad, key_grad, value_grad


def reference(queries, keys, values, outputs, grad_held, lse, span_start):
    positions = (span_start[:, None] + jnp.arange(CH, dtype=jnp.int32)[None, :]).reshape(SEQ).astype(jnp.int32)
    grad_next = jnp.roll(grad_held, -1, axis=0)

    def one_section(section_items):
        section_q, section_k, section_v, section_o, section_g, section_lse = section_items
        delta_rows = jnp.sum(section_g.astype(jnp.float32) * section_o.astype(jnp.float32), axis=-1).T
        blocks = N_CTX
        block_items = (
            section_q.reshape(blocks, TOK_DEV, HQ, HD),
            section_g.reshape(blocks, TOK_DEV, HQ, HD),
            section_lse.reshape(HQ, blocks, TOK_DEV).transpose(1, 0, 2),
            delta_rows.reshape(HQ, blocks, TOK_DEV).transpose(1, 0, 2),
            positions.reshape(blocks, TOK_DEV),
        )

        def block_step(totals, scan_items):
            block_q, block_g, block_lse, block_delta, block_pos = scan_items
            query_grad, key_grad, value_grad = block_reference(block_q, block_g, block_lse, block_delta, block_pos, section_k, section_v, positions)
            return (totals[0] + key_grad, totals[1] + value_grad), query_grad.astype(jnp.bfloat16)

        zero_rows = jnp.zeros((SEQ, HD), jnp.float32)
        (key_total, value_total), query_blocks = lax.scan(block_step, (zero_rows, zero_rows), block_items)
        return query_blocks.reshape(SEQ, HQ, HD), key_total.astype(jnp.bfloat16), value_total.astype(jnp.bfloat16)

    query_grad, key_grad, value_grad = lax.map(one_section, (queries, keys, values, outputs, grad_next, lse))
    return query_grad, key_grad, value_grad
```

```python
import functools
import math

import jax
import jax.numpy as jnp
from jax import lax
from jax.experimental import pallas as pl
from jax.experimental.pallas import tpu as pltpu
from jax.sharding import PartitionSpec as P

KEY_BLOCK = 256
ROW_TILE = 1024
VMEM_LIMIT = 48 * 1024 * 1024

WHOLE = pl.BlockSpec(memory_space=pltpu.VMEM)
SCALARS = pl.BlockSpec(memory_space=pltpu.SMEM)


def from_behind(shard, axis, by):
    length = lax.axis_size(axis)
    return lax.ppermute(shard, axis, [(i, (i + by) % length) for i in range(length)])


def params():
    return pltpu.CompilerParams(vmem_limit_bytes=VMEM_LIMIT)


def sort_keys_kernel(count, span_rows, head_size, starts_ref, *refs):
    blocks = refs[:count]
    keys_ref, values_ref, keys_t_ref = refs[count:]
    me = lax.axis_index("ctx")
    values_ref[:, head_size:] = jnp.full(
        (values_ref.shape[0], values_ref.shape[1] - head_size), -1.0, values_ref.dtype
    )
    for step in range(count):
        owner = lax.rem(me - step + count, count)
        for half in range(2):
            start = pl.multiple_of(starts_ref[2 * owner + half], span_rows)
            rows = pl.ds(start, span_rows)
            part = blocks[step][half * span_rows : (half + 1) * span_rows, :]
            keys_ref[rows, :] = part[:, :head_size]
            values_ref[rows, :head_size] = part[:, head_size:]
            keys_t_ref[:, rows] = part[:, :head_size].astype(jnp.float32).T.astype(jnp.bfloat16)


def sort_keys(span_start, blocks, span_rows, head_size):
    count = len(blocks)
    total = count * 2 * span_rows
    return pl.pallas_call(
        functools.partial(sort_keys_kernel, count, span_rows, head_size),
        out_shape=(
            jax.ShapeDtypeStruct((total, head_size), jnp.bfloat16),
            jax.ShapeDtypeStruct((total, 2 * head_size), jnp.bfloat16),
            jax.ShapeDtypeStruct((head_size, total), jnp.bfloat16),
        ),
        in_specs=[SCALARS] + [WHOLE] * count,
        out_specs=(WHOLE,) * 3,
        compiler_params=params(),
    )(span_start, *blocks)


def span_grads(
    half, heads, span_rows, head_size, starts_ref, q_ref, g_ref, o_ref, lse_ref, keys_ref, values_ref,
    keys_t_ref, dq_ref, total_ref, dq_acc,
):
    scale = head_size**-0.5
    to_log2 = math.log2(math.e)
    me = lax.axis_index("ctx")
    start = starts_ref[2 * me + half]
    rows_all = span_rows * heads
    row_tile = min(ROW_TILE, rows_all)
    full_blocks = start // KEY_BLOCK

    for tile in range(rows_all // row_tile):
        rows = slice(tile * row_tile, (tile + 1) * row_tile)
        q = q_ref[rows, :]
        g = g_ref[rows, :]
        products = (g.astype(jnp.float32) * o_ref[rows, :].astype(jnp.float32)).astype(jnp.bfloat16)
        g_wide = jnp.concatenate([g, products], axis=1)
        lse2 = lse_ref[0:1, rows] * to_log2
        dq_acc[...] = jnp.zeros_like(dq_acc)
        query_pos = (
            start
            + tile * (row_tile // heads)
            + lax.broadcasted_iota(jnp.int32, (KEY_BLOCK, row_tile), 1) // heads
        )

        def block(index, masked):
            base = pl.multiple_of(index * KEY_BLOCK, KEY_BLOCK)
            at = pl.ds(base, KEY_BLOCK)
            nt = (((1,), (1,)), ((), ()))
            scores = lax.dot_general(keys_ref[at, :], q, nt, preferred_element_type=jnp.float32)
            probs = jnp.exp2(scores * (scale * to_log2) - lse2)
            if masked:
                key_pos = base + lax.broadcasted_iota(jnp.int32, (KEY_BLOCK, row_tile), 0)
                probs = jnp.where(key_pos <= query_pos, probs, 0.0)
            centred = lax.dot_general(
                values_ref[at, :], g_wide, nt, preferred_element_type=jnp.float32
            )
            grad_scores = (probs * centred).astype(jnp.bfloat16)
            probs_low = probs.astype(jnp.bfloat16)
            total_ref[at, :head_size] += jnp.dot(
                grad_scores, q, preferred_element_type=jnp.float32
            )
            total_ref[at, head_size:] += jnp.dot(probs_low, g, preferred_element_type=jnp.float32)
            dq_acc[...] += jnp.dot(
                keys_t_ref[:, at], grad_scores, preferred_element_type=jnp.float32
            )

        def dense(index, carry):
            block(index, False)
            return carry

        lax.fori_loop(0, full_blocks, dense, 0)
        block(full_blocks, True)
        dq_ref[rows, :] = (dq_acc[...] * scale).T.astype(jnp.bfloat16)


def hand_out(half, count, span_rows, head_size, starts_ref, total_ref, own_ref, send_refs):
    scale = head_size**-0.5
    me = lax.axis_index("ctx")
    for step in range(count):
        owner = lax.rem(me + step, count)
        start = pl.multiple_of(starts_ref[2 * owner + half], span_rows)
        rows = pl.ds(start, span_rows)
        target = own_ref if step == 0 else send_refs[step - 1]
        target[:, :head_size] = (total_ref[rows, :head_size] * scale).astype(target.dtype)
        target[:, head_size:] = total_ref[rows, head_size:].astype(target.dtype)


def upper_kernel(
    count, heads, span_rows, head_size, starts_ref, q_ref, g_ref, o_ref, lse_ref, keys_ref, values_ref,
    keys_t_ref, dq_ref, lower_ref, own_ref, *rest,
):
    send_refs, (total_ref, dq_acc) = rest[: count - 1], rest[count - 1 :]
    total_ref[...] = jnp.zeros_like(total_ref)
    span_grads(
        1, heads, span_rows, head_size, starts_ref, q_ref, g_ref, o_ref, lse_ref, keys_ref, values_ref,
        keys_t_ref, dq_ref, total_ref, dq_acc,
    )
    lower_ref[...] = total_ref[: lower_ref.shape[0], :]
    hand_out(1, count, span_rows, head_size, starts_ref, total_ref, own_ref, send_refs)


def lower_kernel(
    count, heads, span_rows, head_size, starts_ref, q_ref, g_ref, o_ref, lse_ref, keys_ref, values_ref,
    keys_t_ref, lower_ref, dq_in_ref, dq_ref, own_ref, *rest,
):
    send_refs, (total_ref, dq_acc) = rest[: count - 1], rest[count - 1 :]
    total_ref[...] = lower_ref[...]
    span_grads(
        0, heads, span_rows, head_size, starts_ref, q_ref, g_ref, o_ref, lse_ref, keys_ref, values_ref,
        keys_t_ref, dq_ref, total_ref, dq_acc,
    )
    hand_out(0, count, span_rows, head_size, starts_ref, total_ref, own_ref, send_refs)


def add_kernel(count, span_rows, head_size, *refs):
    key_ref, value_ref = refs[2 * count :]
    for half in range(2):
        own_ref, *term_refs = refs[half * count : (half + 1) * count]
        total = own_ref[...]
        for term_ref in term_refs:
            total = total + term_ref[...].astype(jnp.float32)
        rows = slice(half * span_rows, (half + 1) * span_rows)
        key_ref[rows, :] = total[:, :head_size].astype(jnp.bfloat16)
        value_ref[rows, :] = total[:, head_size:].astype(jnp.bfloat16)


def body(queries, keys, values, outputs, grad_held, lse, span_start):
    count = lax.axis_size("ctx")
    row_count, heads, head_size = queries.shape[1:]
    span_rows = row_count // 2
    total = count * row_count
    rows_span = span_rows * heads

    upper_grad = from_behind(grad_held[0, span_rows:], "section", -1)
    lower_grad = from_behind(grad_held[0, :span_rows], "section", -1)

    pair = jnp.concatenate([keys[0], values[0]], axis=1)
    blocks = [pair] + [from_behind(pair, "ctx", step) for step in range(1, count)]
    sorted_keys = sort_keys(span_start, blocks, span_rows, head_size)

    q_flat = queries.reshape(row_count * heads, head_size)
    o_flat = outputs.reshape(row_count * heads, head_size)
    lse_flat = lse[0].T.reshape(1, row_count * heads)
    row_spec = lambda half: pl.BlockSpec((rows_span, head_size), lambda i: (half, 0))
    lse_spec = lambda half: pl.BlockSpec((1, rows_span), lambda i: (0, half))
    fixed = lambda shape: pl.BlockSpec(shape, lambda i: (0,) * len(shape))
    sorted_specs = [
        fixed((total, head_size)), fixed((total, 2 * head_size)), fixed((head_size, total))
    ]
    span_wide = (span_rows, 2 * head_size)
    dq_shape = jax.ShapeDtypeStruct((row_count * heads, head_size), jnp.bfloat16)
    own_shape = jax.ShapeDtypeStruct(span_wide, jnp.float32)
    send_shape = jax.ShapeDtypeStruct(span_wide, jnp.bfloat16)
    row_tile = min(ROW_TILE, rows_span)

    def cost(blocks_seen):
        pairs = rows_span * blocks_seen * KEY_BLOCK
        return pl.CostEstimate(
            flops=10 * pairs * head_size, bytes_accessed=4 * 2**20, transcendentals=pairs
        )

    dq, lower_total, own_upper, *send_upper = pl.pallas_call(
        functools.partial(upper_kernel, count, heads, span_rows, head_size),
        grid=(1,),
        out_shape=(
            dq_shape,
            jax.ShapeDtypeStruct((total // 2, 2 * head_size), jnp.float32),
            own_shape,
            *[send_shape] * (count - 1),
        ),
        in_specs=[SCALARS, row_spec(1), fixed((rows_span, head_size)), row_spec(1), lse_spec(1)]
        + sorted_specs,
        out_specs=(
            row_spec(1), fixed((total // 2, 2 * head_size)), *[fixed(span_wide)] * count
        ),
        scratch_shapes=[
            pltpu.VMEM((total, 2 * head_size), jnp.float32),
            pltpu.VMEM((head_size, row_tile), jnp.float32),
        ],
        compiler_params=params(),
        cost_estimate=cost(3 * total // (4 * KEY_BLOCK)),
    )(
        span_start, q_flat, upper_grad.reshape(rows_span, head_size), o_flat, lse_flat, *sorted_keys
    )
    got_upper = [from_behind(send_upper[step - 1], "ctx", step) for step in range(1, count)]

    dq, own_lower, *send_lower = pl.pallas_call(
        functools.partial(lower_kernel, count, heads, span_rows, head_size),
        grid=(1,),
        out_shape=(dq_shape, own_shape, *[send_shape] * (count - 1)),
        in_specs=[SCALARS, row_spec(0), fixed((rows_span, head_size)), row_spec(0), lse_spec(0)]
        + sorted_specs
        + [fixed((total // 2, 2 * head_size)), pl.BlockSpec(memory_space=pl.ANY)],
        out_specs=(row_spec(0), *[fixed(span_wide)] * count),
        scratch_shapes=[
            pltpu.VMEM((total // 2, 2 * head_size), jnp.float32),
            pltpu.VMEM((head_size, row_tile), jnp.float32),
        ],
        input_output_aliases={9: 0},
        compiler_params=params(),
        cost_estimate=cost(total // (4 * KEY_BLOCK)),
    )(
        span_start, q_flat, lower_grad.reshape(rows_span, head_size), o_flat, lse_flat, *sorted_keys,
        lower_total, dq,
    )
    got_lower = [from_behind(send_lower[step - 1], "ctx", step) for step in range(1, count)]

    key_out, value_out = pl.pallas_call(
        functools.partial(add_kernel, count, span_rows, head_size),
        out_shape=(jax.ShapeDtypeStruct((row_count, head_size), jnp.bfloat16),) * 2,
        in_specs=[WHOLE] * (2 * count),
        out_specs=(WHOLE,) * 2,
        compiler_params=params(),
    )(own_lower, *got_lower, own_upper, *got_upper)
    return (dq.reshape(queries.shape), key_out[None], value_out[None])


def solution(mesh):
    placed = (
        P("section", "ctx", None, None),
        P("section", "ctx", None),
        P("section", "ctx", None),
        P("section", "ctx", None, None),
        P("section", "ctx", None, None),
        P("section", None, "ctx"),
        P(),
    )
    return jax.shard_map(
        body,
        mesh=mesh,
        in_specs=placed,
        out_specs=(
            P("section", "ctx", None, None),
            P("section", "ctx", None),
            P("section", "ctx", None),
        ),
        check_vma=False,
    )
```

```python
import functools
import math

import jax
import jax.numpy as jnp
from jax import lax
from jax.experimental import pallas as pl
from jax.experimental.pallas import tpu as pltpu
from jax.sharding import PartitionSpec as P

KEY_BLOCK = 256
CHUNK_TOKENS = 64
VMEM_LIMIT = 40 * 1024 * 1024

WHOLE = pl.BlockSpec(memory_space=pltpu.VMEM)
SCALARS = pl.BlockSpec(memory_space=pltpu.SMEM)
ANYWHERE = pl.BlockSpec(memory_space=pl.ANY)
NT = (((1,), (1,)), ((), ()))


def from_behind(shard, axis, by):
    length = lax.axis_size(axis)
    return lax.ppermute(shard, axis, [(i, (i + by) % length) for i in range(length)])


def with_partner(shard, axis, step):
    length = lax.axis_size(axis)
    return lax.ppermute(shard, axis, [(i, i ^ step) for i in range(length)])


def params():
    return pltpu.CompilerParams(vmem_limit_bytes=VMEM_LIMIT)


def cut_kernel(cuts, source_ref, *refs):
    out_refs, sems = refs[: len(cuts)], refs[len(cuts)]
    copies = [
        pltpu.make_async_copy(source_ref.at[pl.ds(first, size)], out_ref, sems.at[i])
        for i, ((first, size), out_ref) in enumerate(zip(cuts, out_refs))
    ]
    for copy in copies:
        copy.start()
    for copy in copies:
        copy.wait()


def cut(source, cuts):
    return pl.pallas_call(
        functools.partial(cut_kernel, cuts),
        out_shape=[
            jax.ShapeDtypeStruct((size, *source.shape[1:]), source.dtype) for _, size in cuts
        ],
        in_specs=[pl.BlockSpec(memory_space=pltpu.HBM)],
        out_specs=[ANYWHERE] * len(cuts),
        scratch_shapes=[pltpu.SemaphoreType.DMA((len(cuts),))],
        compiler_params=params(),
        cost_estimate=pl.CostEstimate(
            flops=0, bytes_accessed=2 * source.size * source.dtype.itemsize, transcendentals=0
        ),
    )(source)


def sort_keys_kernel(count, span_rows, head_size, starts_ref, *refs):
    blocks = refs[:count]
    keys_ref, values_ref, keys_t_ref = refs[count:]
    me = lax.axis_index("ctx")
    values_ref[:, head_size:] = jnp.full(
        (values_ref.shape[0], values_ref.shape[1] - head_size), -1.0, values_ref.dtype
    )
    for step in range(count):
        owner = lax.bitwise_xor(me, step)
        for half in range(2):
            start = pl.multiple_of(starts_ref[2 * owner + half], span_rows)
            rows = pl.ds(start, span_rows)
            part = blocks[step][half * span_rows : (half + 1) * span_rows, :]
            keys_ref[rows, :] = part[:, :head_size]
            values_ref[rows, :head_size] = part[:, head_size:]
            keys_t_ref[:, rows] = part[:, :head_size].astype(jnp.float32).T.astype(jnp.bfloat16)


def sort_keys(span_start, blocks, span_rows, head_size):
    count = len(blocks)
    total = count * 2 * span_rows
    return pl.pallas_call(
        functools.partial(sort_keys_kernel, count, span_rows, head_size),
        out_shape=(
            jax.ShapeDtypeStruct((total, head_size), jnp.bfloat16),
            jax.ShapeDtypeStruct((total, 2 * head_size), jnp.bfloat16),
            jax.ShapeDtypeStruct((head_size, total), jnp.bfloat16),
        ),
        in_specs=[SCALARS] + [WHOLE] * count,
        out_specs=(WHOLE,) * 3,
        compiler_params=params(),
    )(span_start, *blocks)


def chunk_grads(
    chunk, heads, span_rows, starts_ref, q_ref, g_ref, o_ref, lse_ref, keys_ref, values_ref,
    keys_t_ref, total_ref, dq_acc,
):
    half, first, tokens = chunk
    head_size = q_ref.shape[1]
    scale = head_size**-0.5
    to_log2 = math.log2(math.e)
    me = lax.axis_index("ctx")
    start = starts_ref[2 * me + half]
    row_count = tokens * heads
    row_first = (half * span_rows + first) * heads
    rows = slice(row_first, row_first + row_count)
    full_blocks = start // KEY_BLOCK

    q = q_ref[rows, :]
    g = g_ref[...]
    products = (g.astype(jnp.float32) * o_ref[rows, :].astype(jnp.float32)).astype(jnp.bfloat16)
    g_wide = jnp.concatenate([g, products], axis=1)
    lse2 = lse_ref[0:1, rows] * to_log2
    dq_acc[...] = jnp.zeros_like(dq_acc)

    def block(index, masked):
        base = pl.multiple_of(index * KEY_BLOCK, KEY_BLOCK)
        at = pl.ds(base, KEY_BLOCK)
        scores = lax.dot_general(keys_ref[at, :], q, NT, preferred_element_type=jnp.float32)
        probs = jnp.exp2(scores * (scale * to_log2) - lse2)
        if masked:
            query_row = lax.broadcasted_iota(jnp.int32, (1, row_count), 1)
            query_pos = start + first + query_row // heads
            key_pos = base + lax.broadcasted_iota(jnp.int32, (KEY_BLOCK, 1), 0)
            probs = jnp.where(key_pos <= query_pos, probs, 0.0)
        centred = lax.dot_general(values_ref[at, :], g_wide, NT, preferred_element_type=jnp.float32)
        grad_scores = (probs * centred).astype(jnp.bfloat16)
        probs_low = probs.astype(jnp.bfloat16)
        total_ref[at, :head_size] += jnp.dot(grad_scores, q, preferred_element_type=jnp.float32)
        total_ref[at, head_size:] += jnp.dot(probs_low, g, preferred_element_type=jnp.float32)
        dq_acc[...] += jnp.dot(keys_t_ref[:, at], grad_scores, preferred_element_type=jnp.float32)

    def dense(index, carry):
        block(index, False)
        return carry

    lax.fori_loop(0, full_blocks, dense, 0)
    block(full_blocks, True)
    return (dq_acc[...] * scale).T.astype(jnp.bfloat16)


def hand_out(half, count, span_rows, starts_ref, total_ref, own_ref, send_refs):
    head_size = total_ref.shape[1] // 2
    scale = head_size**-0.5
    me = lax.axis_index("ctx")
    for step in range(count):
        owner = lax.bitwise_xor(me, step)
        start = pl.multiple_of(starts_ref[2 * owner + half], span_rows)
        rows = pl.ds(start, span_rows)
        target = own_ref if step == 0 else send_refs[step - 1]
        target[:, :head_size] = (total_ref[rows, :head_size] * scale).astype(target.dtype)
        target[:, head_size:] = total_ref[rows, head_size:].astype(target.dtype)


def add_terms(term_refs):
    total = term_refs[0][...]
    for term_ref in term_refs[1:]:
        total = total + term_ref[...].astype(jnp.float32)
    return total


def chunk_kernel(
    chunk, heads, span_rows, count, is_first, hands_out, is_last, starts_ref, q_ref, g_ref, o_ref,
    lse_ref, keys_ref, values_ref, keys_t_ref, *refs,
):
    refs = list(refs)
    take = lambda number: [refs.pop(0) for _ in range(number)]
    total_in = None if is_first else take(1)[0]
    upper_terms = take(count) if is_last else []
    (dq_ref,) = take(1)
    total_out = None if is_last else take(1)[0]
    handed = take(count) if hands_out else []
    upper_out = take(1) if is_last else []
    total_ref, dq_acc = take(2)

    total_ref[...] = jnp.zeros_like(total_ref) if is_first else total_in[...]
    dq_ref[...] = chunk_grads(
        chunk, heads, span_rows, starts_ref, q_ref, g_ref, o_ref, lse_ref, keys_ref, values_ref,
        keys_t_ref, total_ref, dq_acc,
    )
    if hands_out:
        hand_out(chunk[0], count, span_rows, starts_ref, total_ref, handed[0], handed[1:])
    if not is_last:
        total_out[...] = total_ref[: total_out.shape[0], :]
    else:
        upper_out[0][...] = add_terms(upper_terms).astype(jnp.bfloat16)


def add_kernel(count, span_rows, head_size, *refs):
    term_refs, upper_ref, (key_ref, value_ref) = refs[:count], refs[count], refs[count + 1 :]
    lower = add_terms(term_refs).astype(jnp.bfloat16)
    for out_ref, columns in ((key_ref, slice(0, head_size)), (value_ref, slice(head_size, None))):
        out_ref[:span_rows, :] = lower[:, columns]
        out_ref[span_rows:, :] = upper_ref[:, columns]


def join_kernel(places, *refs):
    part_refs, out_ref, sems = refs[: len(places)], refs[len(places)], refs[len(places) + 1]
    copies = [
        pltpu.make_async_copy(part_ref, out_ref.at[pl.ds(first, part_ref.shape[0])], sems.at[i])
        for i, (first, part_ref) in enumerate(zip(places, part_refs))
    ]
    for copy in copies:
        copy.start()
    for copy in copies:
        copy.wait()


def join(parts, places, shape):
    return pl.pallas_call(
        functools.partial(join_kernel, places),
        out_shape=jax.ShapeDtypeStruct(shape, parts[0].dtype),
        in_specs=[ANYWHERE] * len(parts),
        out_specs=ANYWHERE,
        scratch_shapes=[pltpu.SemaphoreType.DMA((len(parts),))],
        compiler_params=params(),
    )(*parts)


def body(queries, keys, values, outputs, grad_held, lse, span_start):
    count = lax.axis_size("ctx")
    row_count, heads, head_size = queries.shape[1:]
    span_rows = row_count // 2
    total = count * row_count
    chunks = [
        (half, first, CHUNK_TOKENS) for half in (1, 0) for first in range(0, span_rows, CHUNK_TOKENS)
    ]
    per_half = len(chunks) // 2

    pieces = cut(grad_held[0], [(half * span_rows + first, size) for half, first, size in chunks])
    grads = [from_behind(piece, "section", -1) for piece in pieces]

    pair = jnp.concatenate([keys[0], values[0]], axis=1)
    blocks = [pair] + [with_partner(pair, "ctx", step) for step in range(1, count)]
    sorted_keys = sort_keys(span_start, blocks, span_rows, head_size)

    q_flat = queries.reshape(row_count * heads, head_size)
    o_flat = outputs.reshape(row_count * heads, head_size)
    lse_flat = lse[0].T.reshape(1, row_count * heads)

    span_wide = (span_rows, 2 * head_size)
    running, received, dq_parts = [], [], []
    for number, chunk in enumerate(chunks):
        half, _, tokens = chunk
        rows = tokens * heads
        is_first, is_last = number == 0, number == len(chunks) - 1
        hands_out = number % per_half == per_half - 1
        held = total if half == 1 else total // 2
        kept = total if half == 1 and not hands_out else total // 2
        out_shape = [jax.ShapeDtypeStruct((rows, head_size), jnp.bfloat16)]
        if not is_last:
            out_shape.append(jax.ShapeDtypeStruct((kept, 2 * head_size), jnp.float32))
        if hands_out:
            out_shape.append(jax.ShapeDtypeStruct(span_wide, jnp.float32))
            out_shape += [jax.ShapeDtypeStruct(span_wide, jnp.bfloat16)] * (count - 1)
        if is_last:
            out_shape.append(jax.ShapeDtypeStruct(span_wide, jnp.bfloat16))
        operands = [
            q_flat, grads[number].reshape(rows, head_size), o_flat, lse_flat, *sorted_keys, *running
        ]
        if is_last:
            operands += received
        pairs = rows * (3 * total // 4 if half == 1 else total // 4)
        results = pl.pallas_call(
            functools.partial(
                chunk_kernel, chunk, heads, span_rows, count, is_first, hands_out, is_last
            ),
            out_shape=out_shape,
            in_specs=[SCALARS] + [WHOLE] * len(operands),
            out_specs=[WHOLE] * len(out_shape),
            scratch_shapes=[
                pltpu.VMEM((held, 2 * head_size), jnp.float32),
                pltpu.VMEM((head_size, rows), jnp.float32),
            ],
            compiler_params=params(),
            cost_estimate=pl.CostEstimate(
                flops=20 * pairs * head_size, bytes_accessed=2 * 2**20, transcendentals=pairs
            ),
        )(span_start, *operands)
        results = list(results)
        dq_parts.append(results.pop(0))
        running = [] if is_last else [results.pop(0)]
        if hands_out:
            own, *sends = results[:count]
            received = [own] + [
                with_partner(send, "ctx", step) for step, send in enumerate(sends, start=1)
            ]
        if is_last:
            upper_sum = results[-1]

    key_out, value_out = pl.pallas_call(
        functools.partial(add_kernel, count, span_rows, head_size),
        out_shape=(jax.ShapeDtypeStruct((row_count, head_size), jnp.bfloat16),) * 2,
        in_specs=[WHOLE] * (count + 1),
        out_specs=(WHOLE,) * 2,
        compiler_params=params(),
    )(*received, upper_sum)
    places = [(half * span_rows + first) * heads for half, first, _ in chunks]
    dq = join(dq_parts, places, q_flat.shape)
    return (dq.reshape(queries.shape), key_out[None], value_out[None])


def solution(mesh):
    placed = (
        P("section", "ctx", None, None),
        P("section", "ctx", None),
        P("section", "ctx", None),
        P("section", "ctx", None, None),
        P("section", "ctx", None, None),
        P("section", None, "ctx"),
        P(),
    )
    return jax.shard_map(
        body,
        mesh=mesh,
        in_specs=placed,
        out_specs=(
            P("section", "ctx", None, None),
            P("section", "ctx", None),
            P("section", "ctx", None),
        ),
        check_vma=False,
    )
```

```python
import functools
import math

import jax
import jax.numpy as jnp
from jax import lax
from jax.experimental import pallas as pl
from jax.experimental.pallas import tpu as pltpu
from jax.sharding import PartitionSpec as P

KEY_BLOCK = 256
CHUNK_TOKENS = 64
VMEM_LIMIT = 40 * 1024 * 1024
CUT_LIMIT = 60 * 1024 * 1024

WHOLE = pl.BlockSpec(memory_space=pltpu.VMEM)
SCALARS = pl.BlockSpec(memory_space=pltpu.SMEM)
ANYWHERE = pl.BlockSpec(memory_space=pl.ANY)
NT = (((1,), (1,)), ((), ()))


def from_behind(shard, axis, by):
    length = lax.axis_size(axis)
    return lax.ppermute(shard, axis, [(i, (i + by) % length) for i in range(length)])


def with_partner(shard, axis, step):
    length = lax.axis_size(axis)
    return lax.ppermute(shard, axis, [(i, i ^ step) for i in range(length)])


def params(limit=VMEM_LIMIT):
    return pltpu.CompilerParams(vmem_limit_bytes=limit)


def cut_kernel(cuts, starts_in_ref, source_ref, keys_ref, values_ref, *refs):
    starts_ref, pair_ref, *out_refs, sems = refs
    head_size = keys_ref.shape[1]
    moves = [(keys_ref, pair_ref.at[:, pl.ds(0, head_size)])]
    moves.append((values_ref, pair_ref.at[:, pl.ds(head_size, head_size)]))
    for (first, size), out_ref in zip(cuts, out_refs):
        moves.append((source_ref.at[pl.ds(first, size)], out_ref))
    copies = [pltpu.make_async_copy(*move, sems.at[i]) for i, move in enumerate(moves)]
    for copy in copies:
        copy.start()
    for span in range(starts_ref.shape[0]):
        starts_ref[span] = starts_in_ref[span]
    for copy in copies:
        copy.wait()


def cut(span_start, source, keys, values, cuts):
    row_count, head_size = keys.shape
    return pl.pallas_call(
        functools.partial(cut_kernel, cuts),
        out_shape=[
            jax.ShapeDtypeStruct(span_start.shape, span_start.dtype),
            jax.ShapeDtypeStruct((row_count, 2 * head_size), keys.dtype),
        ]
        + [jax.ShapeDtypeStruct((size, *source.shape[1:]), source.dtype) for _, size in cuts],
        in_specs=[SCALARS] + [ANYWHERE] * 3,
        out_specs=[SCALARS] + [ANYWHERE] * (len(cuts) + 1),
        scratch_shapes=[pltpu.SemaphoreType.DMA((len(cuts) + 2,))],
        compiler_params=params(CUT_LIMIT),
        cost_estimate=pl.CostEstimate(
            flops=0, bytes_accessed=2 * source.size * source.dtype.itemsize, transcendentals=0
        ),
    )(span_start, source, keys, values)


def sort_keys_kernel(codes, span_rows, head_size, starts_ref, *refs):
    count = len(codes)
    blocks = refs[:count]
    keys_ref, values_ref, keys_t_ref = refs[count:]
    me = lax.axis_index("ctx")
    values_ref[:, head_size:] = jnp.full(
        (values_ref.shape[0], values_ref.shape[1] - head_size), -1.0, values_ref.dtype
    )
    for block, code in zip(blocks, codes):
        owner = lax.bitwise_xor(me, code)
        for half in range(2):
            start = pl.multiple_of(starts_ref[2 * owner + half], span_rows)
            rows = pl.ds(start, span_rows)
            part = block[half * span_rows : (half + 1) * span_rows, :]
            keys_ref[rows, :] = part[:, :head_size]
            values_ref[rows, :head_size] = part[:, head_size:]
            keys_t_ref[:, rows] = part[:, :head_size].astype(jnp.float32).T.astype(jnp.bfloat16)


def sort_keys(span_start, blocks, codes, span_rows, head_size):
    count = len(blocks)
    total = count * 2 * span_rows
    return pl.pallas_call(
        functools.partial(sort_keys_kernel, codes, span_rows, head_size),
        out_shape=(
            jax.ShapeDtypeStruct((total, head_size), jnp.bfloat16),
            jax.ShapeDtypeStruct((total, 2 * head_size), jnp.bfloat16),
            jax.ShapeDtypeStruct((head_size, total), jnp.bfloat16),
        ),
        in_specs=[SCALARS] + [WHOLE] * count,
        out_specs=(WHOLE,) * 3,
        compiler_params=params(),
    )(span_start, *blocks)


def chunk_grads(
    chunk, heads, span_rows, starts_ref, q_ref, g_ref, o_ref, lse_ref, keys_ref, values_ref,
    keys_t_ref, total_ref, dq_ref,
):
    half, first, tokens = chunk
    head_size = q_ref.shape[1]
    scale = head_size**-0.5
    to_log2 = math.log2(math.e)
    me = lax.axis_index("ctx")
    start = starts_ref[2 * me + half]
    row_count = tokens * heads
    row_first = (half * span_rows + first) * heads
    rows = slice(row_first, row_first + row_count)
    full_blocks = start // KEY_BLOCK

    q = q_ref[rows, :]
    g = g_ref[...]
    products = (g.astype(jnp.float32) * o_ref[rows, :].astype(jnp.float32)).astype(jnp.bfloat16)
    g_wide = jnp.concatenate([g, products], axis=1)
    lse2 = lse_ref[0:1, rows] * to_log2
    dq_ref[...] = jnp.zeros_like(dq_ref)

    def block(index, masked):
        base = pl.multiple_of(index * KEY_BLOCK, KEY_BLOCK)
        at = pl.ds(base, KEY_BLOCK)
        scores = lax.dot_general(keys_ref[at, :], q, NT, preferred_element_type=jnp.float32)
        probs = jnp.exp2(scores * (scale * to_log2) - lse2)
        if masked:
            query_row = lax.broadcasted_iota(jnp.int32, (1, row_count), 1)
            query_pos = start + first + query_row // heads
            key_pos = base + lax.broadcasted_iota(jnp.int32, (KEY_BLOCK, 1), 0)
            probs = jnp.where(key_pos <= query_pos, probs, 0.0)
        centred = lax.dot_general(values_ref[at, :], g_wide, NT, preferred_element_type=jnp.float32)
        grad_scores = (probs * centred).astype(jnp.bfloat16)
        probs_low = probs.astype(jnp.bfloat16)
        total_ref[at, :head_size] += jnp.dot(grad_scores, q, preferred_element_type=jnp.float32)
        total_ref[at, head_size:] += jnp.dot(probs_low, g, preferred_element_type=jnp.float32)
        dq_ref[...] += jnp.dot(keys_t_ref[:, at], grad_scores, preferred_element_type=jnp.float32)

    def dense(index, carry):
        block(index, False)
        return carry

    lax.fori_loop(0, full_blocks, dense, 0)
    block(full_blocks, True)


def hand_out(half, count, span_rows, starts_ref, total_ref, own_ref, send_refs):
    head_size = total_ref.shape[1] // 2
    scale = head_size**-0.5
    me = lax.axis_index("ctx")
    for step in range(count):
        owner = lax.bitwise_xor(me, step)
        start = pl.multiple_of(starts_ref[2 * owner + half], span_rows)
        rows = pl.ds(start, span_rows)
        target = own_ref if step == 0 else send_refs[step - 1]
        target[:, :head_size] = (total_ref[rows, :head_size] * scale).astype(target.dtype)
        target[:, head_size:] = total_ref[rows, head_size:].astype(target.dtype)


def add_terms(term_refs):
    total = term_refs[0][...]
    for term_ref in term_refs[1:]:
        total = total + term_ref[...].astype(jnp.float32)
    return total


def chunk_kernel(
    chunk, heads, span_rows, count, is_first, hands_out, n_after, starts_ref, q_ref, g_ref, o_ref,
    lse_ref, keys_ref, values_ref, keys_t_ref, *refs,
):
    refs = list(refs[n_after:])
    total_in = None if is_first else refs.pop(0)
    dq_ref, total_ref, *handed = refs
    if is_first:
        total_ref[...] = jnp.zeros_like(total_ref)
    else:
        total_ref[...] = total_in[: total_ref.shape[0], :]
    chunk_grads(
        chunk, heads, span_rows, starts_ref, q_ref, g_ref, o_ref, lse_ref, keys_ref, values_ref,
        keys_t_ref, total_ref, dq_ref,
    )
    if hands_out:
        hand_out(chunk[0], count, span_rows, starts_ref, total_ref, handed[0], handed[1:])


def add_kernel(count, span_rows, head_size, *refs):
    term_refs, upper_ref, (key_ref, value_ref) = refs[:count], refs[count], refs[count + 1 :]
    lower = add_terms(term_refs).astype(jnp.bfloat16)
    for out_ref, columns in ((key_ref, slice(0, head_size)), (value_ref, slice(head_size, None))):
        out_ref[:span_rows, :] = lower[:, columns]
        out_ref[span_rows:, :] = upper_ref[:, columns]


def finish_kernel(count, places, *refs):
    term_refs, refs = refs[:count], refs[count:]
    part_refs, (upper_ref, out_ref, held, sems) = refs[: len(places)], refs[len(places) :]
    scale = out_ref.shape[1] ** -0.5
    copies = []
    for i, (first, part_ref) in enumerate(zip(places, part_refs)):
        rows = pl.ds(first, part_ref.shape[1])
        held[rows, :] = (part_ref[...] * scale).T.astype(jnp.bfloat16)
        copies.append(pltpu.make_async_copy(held.at[rows], out_ref.at[rows], sems.at[i]))
        copies[-1].start()
    upper_ref[...] = add_terms(term_refs).astype(jnp.bfloat16)
    for copy in copies:
        copy.wait()


def finish(terms, parts, places, shape):
    return pl.pallas_call(
        functools.partial(finish_kernel, len(terms), places),
        out_shape=(
            jax.ShapeDtypeStruct(terms[0].shape, jnp.bfloat16),
            jax.ShapeDtypeStruct(shape, jnp.bfloat16),
        ),
        in_specs=[WHOLE] * (len(terms) + len(parts)),
        out_specs=(WHOLE, ANYWHERE),
        scratch_shapes=[
            pltpu.VMEM(shape, jnp.bfloat16),
            pltpu.SemaphoreType.DMA((len(parts),)),
        ],
        compiler_params=params(),
    )(*terms, *parts)


def body(queries, keys, values, outputs, grad_held, lse, span_start):
    count = lax.axis_size("ctx")
    row_count, heads, head_size = queries.shape[1:]
    span_rows = row_count // 2
    total = count * row_count
    chunks = [
        (half, first, CHUNK_TOKENS) for half in (1, 0) for first in range(0, span_rows, CHUNK_TOKENS)
    ]
    per_half = len(chunks) // 2

    starts, pair, *pieces = cut(
        span_start, grad_held[0], keys[0], values[0],
        [(half * span_rows + first, size) for half, first, size in chunks],
    )
    grads = [from_behind(piece, "section", -1) for piece in pieces]

    blocks, codes = [pair], [0]
    step = count // 2
    while step:
        blocks = blocks + [with_partner(block, "ctx", step) for block in blocks]
        codes = codes + [code ^ step for code in codes]
        step //= 2
    sorted_keys = sort_keys(starts, blocks, codes, span_rows, head_size)

    q_flat = queries.reshape(row_count * heads, head_size)
    o_flat = outputs.reshape(row_count * heads, head_size)
    lse_flat = lse[0].T.reshape(1, row_count * heads)

    span_wide = (span_rows, 2 * head_size)
    running, received, dq_parts = [], [], []
    for number, chunk in enumerate(chunks):
        half, _, tokens = chunk
        rows = tokens * heads
        is_first = number == 0
        hands_out = number % per_half == per_half - 1
        after = received if number == len(chunks) - 1 else []
        if after:
            upper_terms = received
        operands = [
            q_flat, grads[number].reshape(rows, head_size), o_flat, lse_flat, *sorted_keys, *after,
            *running,
        ]
        out_shape = [
            jax.ShapeDtypeStruct((head_size, rows), jnp.float32),
            jax.ShapeDtypeStruct((total if half else total // 2, 2 * head_size), jnp.float32),
        ]
        if hands_out:
            out_shape.append(jax.ShapeDtypeStruct(span_wide, jnp.float32))
            out_shape += [jax.ShapeDtypeStruct(span_wide, jnp.bfloat16)] * (count - 1)
        pairs = rows * (3 * total // 4 if half == 1 else total // 4)
        dq, running_total, *handed = pl.pallas_call(
            functools.partial(
                chunk_kernel, chunk, heads, span_rows, count, is_first, hands_out, len(after)
            ),
            out_shape=out_shape,
            in_specs=[SCALARS] + [WHOLE] * len(operands),
            out_specs=[WHOLE] * len(out_shape),
            compiler_params=params(),
            cost_estimate=pl.CostEstimate(
                flops=20 * pairs * head_size, bytes_accessed=2 * 2**20, transcendentals=pairs
            ),
        )(starts, *operands)
        dq_parts.append(dq)
        running = [running_total]
        if hands_out:
            received = [handed[0]] + [
                with_partner(send, "ctx", step) for step, send in enumerate(handed[1:], start=1)
            ]

    places = [(half * span_rows + first) * heads for half, first, _ in chunks]
    upper_sum, dq = finish(upper_terms, dq_parts, places, q_flat.shape)
    key_out, value_out = pl.pallas_call(
        functools.partial(add_kernel, count, span_rows, head_size),
        out_shape=(jax.ShapeDtypeStruct((row_count, head_size), jnp.bfloat16),) * 2,
        in_specs=[WHOLE] * (count + 1),
        out_specs=(WHOLE,) * 2,
        compiler_params=params(),
    )(*received, upper_sum)
    return (dq.reshape(queries.shape), key_out[None], value_out[None])


def solution(mesh):
    placed = (
        P("section", "ctx", None, None),
        P("section", "ctx", None),
        P("section", "ctx", None),
        P("section", "ctx", None, None),
        P("section", "ctx", None, None),
        P("section", None, "ctx"),
        P(),
    )
    return jax.shard_map(
        body,
        mesh=mesh,
        in_specs=placed,
        out_specs=(
            P("section", "ctx", None, None),
            P("section", "ctx", None),
            P("section", "ctx", None),
        ),
        check_vma=False,
    )
```

```python
import functools
import math

import jax
import jax.numpy as jnp
from jax import lax
from jax.experimental import pallas as pl
from jax.experimental.pallas import tpu as pltpu
from jax.sharding import PartitionSpec as P

KEY_BLOCK = 256
CHUNK_TOKENS = 64
VMEM_LIMIT = 40 * 1024 * 1024

WHOLE = pl.BlockSpec(memory_space=pltpu.VMEM)
SCALARS = pl.BlockSpec(memory_space=pltpu.SMEM)
ANYWHERE = pl.BlockSpec(memory_space=pl.ANY)
NT = (((1,), (1,)), ((), ()))


def from_behind(shard, axis, by):
    length = lax.axis_size(axis)
    return lax.ppermute(shard, axis, [(i, (i + by) % length) for i in range(length)])


def with_partner(shard, axis, step):
    length = lax.axis_size(axis)
    return lax.ppermute(shard, axis, [(i, i ^ step) for i in range(length)])


def params(limit=VMEM_LIMIT):
    return pltpu.CompilerParams(vmem_limit_bytes=limit)


def sort_keys_kernel(codes, span_rows, head_size, starts_ref, *refs):
    count = len(codes)
    blocks = refs[:count]
    keys_ref, values_ref, keys_t_ref = refs[count:]
    me = lax.axis_index("ctx")
    values_ref[:, head_size:] = jnp.full(
        (values_ref.shape[0], values_ref.shape[1] - head_size), -1.0, values_ref.dtype
    )
    for block, code in zip(blocks, codes):
        owner = lax.bitwise_xor(me, code)
        for half in range(2):
            start = pl.multiple_of(starts_ref[2 * owner + half], span_rows)
            rows = pl.ds(start, span_rows)
            part = slice(half * span_rows, (half + 1) * span_rows)
            keys = block[0, part, :]
            keys_ref[rows, :] = keys
            values_ref[rows, :head_size] = block[1, part, :]
            keys_t_ref[:, rows] = keys.astype(jnp.float32).T.astype(jnp.bfloat16)


def sort_keys(span_start, blocks, codes, span_rows, head_size):
    count = len(blocks)
    total = count * 2 * span_rows
    return pl.pallas_call(
        functools.partial(sort_keys_kernel, codes, span_rows, head_size),
        out_shape=(
            jax.ShapeDtypeStruct((total, head_size), jnp.bfloat16),
            jax.ShapeDtypeStruct((total, 2 * head_size), jnp.bfloat16),
            jax.ShapeDtypeStruct((head_size, total), jnp.bfloat16),
        ),
        in_specs=[SCALARS] + [WHOLE] * count,
        out_specs=(WHOLE,) * 3,
        compiler_params=params(),
    )(span_start, *blocks)


def chunk_grads(
    chunk, heads, span_rows, starts_ref, q_ref, g_ref, o_ref, lse_ref, keys_ref, values_ref,
    keys_t_ref, total_ref, dq_ref,
):
    half, first, tokens = chunk
    head_size = q_ref.shape[1]
    scale = head_size**-0.5
    to_log2 = math.log2(math.e)
    me = lax.axis_index("ctx")
    start = starts_ref[2 * me + half]
    row_count = tokens * heads
    row_first = (half * span_rows + first) * heads
    rows = slice(row_first, row_first + row_count)
    full_blocks = start // KEY_BLOCK

    q = q_ref[rows, :]
    g = g_ref[...]
    products = (g.astype(jnp.float32) * o_ref[rows, :].astype(jnp.float32)).astype(jnp.bfloat16)
    g_wide = jnp.concatenate([g, products], axis=1)
    lse2 = lse_ref[0:1, rows] * to_log2
    dq_ref[...] = jnp.zeros_like(dq_ref)

    def block(index, masked):
        base = pl.multiple_of(index * KEY_BLOCK, KEY_BLOCK)
        at = pl.ds(base, KEY_BLOCK)
        scores = lax.dot_general(keys_ref[at, :], q, NT, preferred_element_type=jnp.float32)
        probs = jnp.exp2(scores * (scale * to_log2) - lse2)
        if masked:
            query_row = lax.broadcasted_iota(jnp.int32, (1, row_count), 1)
            query_pos = start + first + query_row // heads
            key_pos = base + lax.broadcasted_iota(jnp.int32, (KEY_BLOCK, 1), 0)
            probs = jnp.where(key_pos <= query_pos, probs, 0.0)
        centred = lax.dot_general(values_ref[at, :], g_wide, NT, preferred_element_type=jnp.float32)
        grad_scores = (probs * centred).astype(jnp.bfloat16)
        probs_low = probs.astype(jnp.bfloat16)
        total_ref[at, :head_size] += jnp.dot(grad_scores, q, preferred_element_type=jnp.float32)
        total_ref[at, head_size:] += jnp.dot(probs_low, g, preferred_element_type=jnp.float32)
        dq_ref[...] += jnp.dot(keys_t_ref[:, at], grad_scores, preferred_element_type=jnp.float32)

    def dense(index, carry):
        block(index, False)
        return carry

    lax.fori_loop(0, full_blocks, dense, 0)
    block(full_blocks, True)


def hand_out(half, count, span_rows, starts_ref, total_ref, own_ref, send_refs):
    head_size = total_ref.shape[1] // 2
    scale = head_size**-0.5
    me = lax.axis_index("ctx")
    for step in range(count):
        owner = lax.bitwise_xor(me, step)
        start = pl.multiple_of(starts_ref[2 * owner + half], span_rows)
        rows = pl.ds(start, span_rows)
        target = own_ref if step == 0 else send_refs[step - 1]
        target[:, :head_size] = (total_ref[rows, :head_size] * scale).astype(target.dtype)
        target[:, head_size:] = total_ref[rows, head_size:].astype(target.dtype)


def add_terms(term_refs):
    total = term_refs[0][...]
    for term_ref in term_refs[1:]:
        total = total + term_ref[...].astype(jnp.float32)
    return total


def chunk_kernel(
    chunk, heads, span_rows, count, is_first, is_last, hands_out, n_after, starts_ref, q_ref, g_ref, o_ref,
    lse_ref, keys_ref, values_ref, keys_t_ref, *refs,
):
    refs = list(refs[n_after:])
    total_in = None if is_first else refs.pop(0)
    total_ref = refs.pop() if is_last else refs.pop(1)
    dq_ref, *handed = refs
    if is_first:
        total_ref[...] = jnp.zeros_like(total_ref)
    else:
        total_ref[...] = total_in[: total_ref.shape[0], :]
    chunk_grads(
        chunk, heads, span_rows, starts_ref, q_ref, g_ref, o_ref, lse_ref, keys_ref, values_ref,
        keys_t_ref, total_ref, dq_ref,
    )
    if hands_out:
        hand_out(chunk[0], count, span_rows, starts_ref, total_ref, handed[0], handed[1:])


def add_kernel(count, span_rows, head_size, *refs):
    term_refs, upper_ref, (key_ref, value_ref) = refs[:count], refs[count], refs[count + 1 :]
    lower = add_terms(term_refs).astype(jnp.bfloat16)
    for out_ref, columns in ((key_ref, slice(0, head_size)), (value_ref, slice(head_size, None))):
        out_ref[:span_rows, :] = lower[:, columns]
        out_ref[span_rows:, :] = upper_ref[:, columns]


def finish_kernel(count, places, *refs):
    term_refs, refs = refs[:count], refs[count:]
    part_refs, (upper_ref, out_ref, held, sems) = refs[: len(places)], refs[len(places) :]
    scale = out_ref.shape[1] ** -0.5
    copies = []
    for i, (first, part_ref) in enumerate(zip(places, part_refs)):
        rows = pl.ds(first, part_ref.shape[1])
        held[rows, :] = (part_ref[...] * scale).T.astype(jnp.bfloat16)
        copies.append(pltpu.make_async_copy(held.at[rows], out_ref.at[rows], sems.at[i]))
        copies[-1].start()
    upper_ref[...] = add_terms(term_refs).astype(jnp.bfloat16)
    for copy in copies:
        copy.wait()


def finish(terms, parts, places, shape):
    return pl.pallas_call(
        functools.partial(finish_kernel, len(terms), places),
        out_shape=(
            jax.ShapeDtypeStruct(terms[0].shape, jnp.bfloat16),
            jax.ShapeDtypeStruct(shape, jnp.bfloat16),
        ),
        in_specs=[WHOLE] * (len(terms) + len(parts)),
        out_specs=(WHOLE, ANYWHERE),
        scratch_shapes=[
            pltpu.VMEM(shape, jnp.bfloat16),
            pltpu.SemaphoreType.DMA((len(parts),)),
        ],
        compiler_params=params(),
    )(*terms, *parts)


def body(queries, keys, values, outputs, grad_held, lse, span_start):
    count = lax.axis_size("ctx")
    row_count, heads, head_size = queries.shape[1:]
    span_rows = row_count // 2
    total = count * row_count
    chunks = [
        (half, first, CHUNK_TOKENS) for half in (1, 0) for first in range(0, span_rows, CHUNK_TOKENS)
    ]
    per_half = len(chunks) // 2

    cuts = [half * span_rows + first for half, first, _ in chunks]
    pieces = [grad_held[0, cuts[0] : cuts[0] + CHUNK_TOKENS]]
    pieces[0], rest = lax.optimization_barrier((pieces[0], grad_held[0]))
    pieces += [rest[at : at + CHUNK_TOKENS] for at in cuts[1:]]
    grads = [from_behind(piece, "section", -1) for piece in pieces]

    pair = jnp.concatenate([keys, values], axis=0)
    blocks, codes = [pair], [0]
    step = count // 2
    while step:
        blocks = blocks + [with_partner(block, "ctx", step) for block in blocks]
        codes = codes + [code ^ step for code in codes]
        step //= 2
    sorted_keys = sort_keys(span_start, blocks, codes, span_rows, head_size)

    q_flat = queries.reshape(row_count * heads, head_size)
    o_flat = outputs.reshape(row_count * heads, head_size)
    lse_flat = lse[0].T.reshape(1, row_count * heads)

    span_wide = (span_rows, 2 * head_size)
    running, received, dq_parts = [], [], []
    for number, chunk in enumerate(chunks):
        half, _, tokens = chunk
        rows = tokens * heads
        is_first, is_last = number == 0, number == len(chunks) - 1
        hands_out = number % per_half == per_half - 1
        after = received if is_last else []
        if after:
            upper_terms = received
        operands = [
            q_flat, grads[number].reshape(rows, head_size), o_flat, lse_flat, *sorted_keys, *after,
            *running,
        ]
        total_shape = (total if half else total // 2, 2 * head_size)
        out_shape = [jax.ShapeDtypeStruct((head_size, rows), jnp.float32)]
        if not is_last:
            out_shape.append(jax.ShapeDtypeStruct(total_shape, jnp.float32))
        if hands_out:
            out_shape.append(jax.ShapeDtypeStruct(span_wide, jnp.float32))
            out_shape += [jax.ShapeDtypeStruct(span_wide, jnp.bfloat16)] * (count - 1)
        pairs = rows * (3 * total // 4 if half == 1 else total // 4)
        dq, *handed = pl.pallas_call(
            functools.partial(
                chunk_kernel, chunk, heads, span_rows, count, is_first, is_last, hands_out,
                len(after),
            ),
            out_shape=out_shape,
            in_specs=[SCALARS] + [WHOLE] * len(operands),
            out_specs=[WHOLE] * len(out_shape),
            scratch_shapes=[pltpu.VMEM(total_shape, jnp.float32)] if is_last else [],
            compiler_params=params(),
            cost_estimate=pl.CostEstimate(
                flops=20 * pairs * head_size, bytes_accessed=2 * 2**20, transcendentals=pairs
            ),
        )(span_start, *operands)
        dq_parts.append(dq)
        running = [] if is_last else [handed.pop(0)]
        if hands_out:
            received = [handed[0]] + [
                with_partner(send, "ctx", step) for step, send in enumerate(handed[1:], start=1)
            ]

    places = [(half * span_rows + first) * heads for half, first, _ in chunks]
    upper_sum, dq = finish(upper_terms, dq_parts, places, q_flat.shape)
    key_out, value_out = pl.pallas_call(
        functools.partial(add_kernel, count, span_rows, head_size),
        out_shape=(jax.ShapeDtypeStruct((row_count, head_size), jnp.bfloat16),) * 2,
        in_specs=[WHOLE] * (count + 1),
        out_specs=(WHOLE,) * 2,
        compiler_params=params(),
    )(*received, upper_sum)
    return (dq.reshape(queries.shape), key_out[None], value_out[None])


def solution(mesh):
    placed = (
        P("section", "ctx", None, None),
        P("section", "ctx", None),
        P("section", "ctx", None),
        P("section", "ctx", None, None),
        P("section", "ctx", None, None),
        P("section", None, "ctx"),
        P(),
    )
    return jax.shard_map(
        body,
        mesh=mesh,
        in_specs=placed,
        out_specs=(
            P("section", "ctx", None, None),
            P("section", "ctx", None),
            P("section", "ctx", None),
        ),
        check_vma=False,
    )
```

```python
import functools
import math

import jax
import jax.numpy as jnp
from jax import lax
from jax.experimental import pallas as pl
from jax.experimental.pallas import tpu as pltpu
from jax.sharding import PartitionSpec as P

KEY_BLOCK = 256
CHUNK_TOKENS = 64
VMEM_LIMIT = 40 * 1024 * 1024
CUT_LIMIT = 63 * 1024 * 1024

WHOLE = pl.BlockSpec(memory_space=pltpu.VMEM)
SCALARS = pl.BlockSpec(memory_space=pltpu.SMEM)
ANYWHERE = pl.BlockSpec(memory_space=pl.ANY)
NT = (((1,), (1,)), ((), ()))


def from_behind(shard, axis, by):
    length = lax.axis_size(axis)
    return lax.ppermute(shard, axis, [(i, (i + by) % length) for i in range(length)])


def with_partner(shard, axis, step):
    length = lax.axis_size(axis)
    return lax.ppermute(shard, axis, [(i, i ^ step) for i in range(length)])


def params(limit=VMEM_LIMIT):
    return pltpu.CompilerParams(vmem_limit_bytes=limit)


def cut_kernel(cuts, source_ref, *refs):
    *out_refs, held, in_sems, out_sems = refs
    copies = []
    for i, ((first, size), out_ref) in enumerate(zip(cuts, out_refs)):
        rows = pl.ds(first, size)
        copies.append((
            pltpu.make_async_copy(source_ref.at[rows], held.at[rows], in_sems.at[i]),
            pltpu.make_async_copy(held.at[rows], out_ref, out_sems.at[i]),
        ))
    for fetch, _ in copies:
        fetch.start()
    for fetch, store in copies:
        fetch.wait()
        store.start()
    for _, store in copies:
        store.wait()


def cut(source, cuts):
    return pl.pallas_call(
        functools.partial(cut_kernel, cuts),
        out_shape=[
            jax.ShapeDtypeStruct((size, *source.shape[1:]), source.dtype) for _, size in cuts
        ],
        in_specs=[ANYWHERE],
        out_specs=[ANYWHERE] * len(cuts),
        scratch_shapes=[
            pltpu.VMEM(source.shape, source.dtype),
            pltpu.SemaphoreType.DMA((len(cuts),)),
            pltpu.SemaphoreType.DMA((len(cuts),)),
        ],
        compiler_params=params(CUT_LIMIT),
        cost_estimate=pl.CostEstimate(
            flops=0, bytes_accessed=2 * source.size * source.dtype.itemsize, transcendentals=0
        ),
    )(source)


def sort_keys_kernel(codes, span_rows, head_size, starts_ref, *refs):
    count = len(codes)
    blocks = refs[:count]
    keys_ref, values_ref, keys_t_ref = refs[count:]
    me = lax.axis_index("ctx")
    values_ref[:, head_size:] = jnp.full(
        (values_ref.shape[0], values_ref.shape[1] - head_size), -1.0, values_ref.dtype
    )
    for block, code in zip(blocks, codes):
        owner = lax.bitwise_xor(me, code)
        for half in range(2):
            start = pl.multiple_of(starts_ref[2 * owner + half], span_rows)
            rows = pl.ds(start, span_rows)
            part = slice(half * span_rows, (half + 1) * span_rows)
            keys = block[0, part, :]
            keys_ref[rows, :] = keys
            values_ref[rows, :head_size] = block[1, part, :]
            keys_t_ref[:, rows] = keys.astype(jnp.float32).T.astype(jnp.bfloat16)


def sort_keys(span_start, blocks, codes, span_rows, head_size):
    count = len(blocks)
    total = count * 2 * span_rows
    return pl.pallas_call(
        functools.partial(sort_keys_kernel, codes, span_rows, head_size),
        out_shape=(
            jax.ShapeDtypeStruct((total, head_size), jnp.bfloat16),
            jax.ShapeDtypeStruct((total, 2 * head_size), jnp.bfloat16),
            jax.ShapeDtypeStruct((head_size, total), jnp.bfloat16),
        ),
        in_specs=[SCALARS] + [WHOLE] * count,
        out_specs=(WHOLE,) * 3,
        compiler_params=params(),
    )(span_start, *blocks)


def chunk_grads(
    chunk, heads, span_rows, starts_ref, q_ref, g_ref, o_ref, lse_ref, keys_ref, values_ref,
    keys_t_ref, total_ref, dq_ref,
):
    half, first, tokens = chunk
    head_size = q_ref.shape[1]
    scale = head_size**-0.5
    to_log2 = math.log2(math.e)
    me = lax.axis_index("ctx")
    start = starts_ref[2 * me + half]
    row_count = tokens * heads
    row_first = (half * span_rows + first) * heads
    rows = slice(row_first, row_first + row_count)
    full_blocks = start // KEY_BLOCK

    q = q_ref[rows, :]
    g = g_ref[...]
    products = (g.astype(jnp.float32) * o_ref[rows, :].astype(jnp.float32)).astype(jnp.bfloat16)
    g_wide = jnp.concatenate([g, products], axis=1)
    lse2 = lse_ref[0:1, rows] * to_log2
    dq_ref[...] = jnp.zeros_like(dq_ref)

    def block(index, masked):
        base = pl.multiple_of(index * KEY_BLOCK, KEY_BLOCK)
        at = pl.ds(base, KEY_BLOCK)
        scores = lax.dot_general(keys_ref[at, :], q, NT, preferred_element_type=jnp.float32)
        probs = jnp.exp2(scores * (scale * to_log2) - lse2)
        if masked:
            query_row = lax.broadcasted_iota(jnp.int32, (1, row_count), 1)
            query_pos = start + first + query_row // heads
            key_pos = base + lax.broadcasted_iota(jnp.int32, (KEY_BLOCK, 1), 0)
            probs = jnp.where(key_pos <= query_pos, probs, 0.0)
        centred = lax.dot_general(values_ref[at, :], g_wide, NT, preferred_element_type=jnp.float32)
        grad_scores = (probs * centred).astype(jnp.bfloat16)
        probs_low = probs.astype(jnp.bfloat16)
        total_ref[at, :head_size] += jnp.dot(grad_scores, q, preferred_element_type=jnp.float32)
        total_ref[at, head_size:] += jnp.dot(probs_low, g, preferred_element_type=jnp.float32)
        dq_ref[...] += jnp.dot(keys_t_ref[:, at], grad_scores, preferred_element_type=jnp.float32)

    def dense(index, carry):
        block(index, False)
        return carry

    lax.fori_loop(0, full_blocks, dense, 0)
    block(full_blocks, True)


def hand_out(half, count, span_rows, starts_ref, total_ref, own_ref, send_refs):
    head_size = total_ref.shape[1] // 2
    scale = head_size**-0.5
    me = lax.axis_index("ctx")
    for step in range(count):
        owner = lax.bitwise_xor(me, step)
        start = pl.multiple_of(starts_ref[2 * owner + half], span_rows)
        rows = pl.ds(start, span_rows)
        target = own_ref if step == 0 else send_refs[step - 1]
        target[:, :head_size] = (total_ref[rows, :head_size] * scale).astype(target.dtype)
        target[:, head_size:] = total_ref[rows, head_size:].astype(target.dtype)


def add_terms(term_refs):
    total = term_refs[0][...]
    for term_ref in term_refs[1:]:
        total = total + term_ref[...].astype(jnp.float32)
    return total


def chunk_kernel(
    chunk, heads, span_rows, count, is_first, is_last, hands_out, n_after, starts_ref, q_ref, g_ref, o_ref,
    lse_ref, keys_ref, values_ref, keys_t_ref, *refs,
):
    refs = list(refs[n_after:])
    total_in = None if is_first else refs.pop(0)
    total_ref = refs.pop() if is_last else refs.pop(1)
    dq_ref, *handed = refs
    if is_first:
        total_ref[...] = jnp.zeros_like(total_ref)
    else:
        total_ref[...] = total_in[: total_ref.shape[0], :]
    chunk_grads(
        chunk, heads, span_rows, starts_ref, q_ref, g_ref, o_ref, lse_ref, keys_ref, values_ref,
        keys_t_ref, total_ref, dq_ref,
    )
    if hands_out:
        hand_out(chunk[0], count, span_rows, starts_ref, total_ref, handed[0], handed[1:])


def add_kernel(count, span_rows, head_size, *refs):
    term_refs, upper_ref, (key_ref, value_ref) = refs[:count], refs[count], refs[count + 1 :]
    lower = add_terms(term_refs).astype(jnp.bfloat16)
    for out_ref, columns in ((key_ref, slice(0, head_size)), (value_ref, slice(head_size, None))):
        out_ref[:span_rows, :] = lower[:, columns]
        out_ref[span_rows:, :] = upper_ref[:, columns]


def finish_kernel(count, places, *refs):
    term_refs, refs = refs[:count], refs[count:]
    part_refs, (upper_ref, out_ref, held, sems) = refs[: len(places)], refs[len(places) :]
    scale = out_ref.shape[1] ** -0.5
    copies = []
    for i, (first, part_ref) in enumerate(zip(places, part_refs)):
        rows = pl.ds(first, part_ref.shape[1])
        held[rows, :] = (part_ref[...] * scale).T.astype(jnp.bfloat16)
        copies.append(pltpu.make_async_copy(held.at[rows], out_ref.at[rows], sems.at[i]))
        copies[-1].start()
    upper_ref[...] = add_terms(term_refs).astype(jnp.bfloat16)
    for copy in copies:
        copy.wait()


def finish(terms, parts, places, shape):
    return pl.pallas_call(
        functools.partial(finish_kernel, len(terms), places),
        out_shape=(
            jax.ShapeDtypeStruct(terms[0].shape, jnp.bfloat16),
            jax.ShapeDtypeStruct(shape, jnp.bfloat16),
        ),
        in_specs=[WHOLE] * (len(terms) + len(parts)),
        out_specs=(WHOLE, ANYWHERE),
        scratch_shapes=[
            pltpu.VMEM(shape, jnp.bfloat16),
            pltpu.SemaphoreType.DMA((len(parts),)),
        ],
        compiler_params=params(),
    )(*terms, *parts)


def body(queries, keys, values, outputs, grad_held, lse, span_start):
    count = lax.axis_size("ctx")
    row_count, heads, head_size = queries.shape[1:]
    span_rows = row_count // 2
    total = count * row_count
    chunks = [
        (half, first, CHUNK_TOKENS) for half in (1, 0) for first in range(0, span_rows, CHUNK_TOKENS)
    ]
    per_half = len(chunks) // 2

    pieces = cut(
        grad_held[0], [(half * span_rows + first, size) for half, first, size in chunks]
    )
    pieces = list(pieces)
    grads = [from_behind(pieces[0], "section", -1)]
    keys, values, pieces[0] = lax.optimization_barrier((keys, values, pieces[0]))
    pair = jnp.concatenate([keys, values], axis=0)
    blocks, codes = [pair], [0]
    step = count // 2
    while step:
        blocks = blocks + [with_partner(block, "ctx", step) for block in blocks]
        codes = codes + [code ^ step for code in codes]
        step //= 2
    gates = [pair, blocks[1]] + grads
    for number, piece in enumerate(pieces[1:]):
        piece, _ = lax.optimization_barrier((piece, gates[min(number, 2)]))
        grads.append(from_behind(piece, "section", -1))
    sorted_keys = sort_keys(span_start, blocks, codes, span_rows, head_size)

    q_flat = queries.reshape(row_count * heads, head_size)
    o_flat = outputs.reshape(row_count * heads, head_size)
    lse_flat = lse[0].T.reshape(1, row_count * heads)

    span_wide = (span_rows, 2 * head_size)
    running, received, dq_parts = [], [], []
    for number, chunk in enumerate(chunks):
        half, _, tokens = chunk
        rows = tokens * heads
        is_first, is_last = number == 0, number == len(chunks) - 1
        hands_out = number % per_half == per_half - 1
        after = received if is_last else []
        if after:
            upper_terms = received
        operands = [
            q_flat, grads[number].reshape(rows, head_size), o_flat, lse_flat, *sorted_keys, *after,
            *running,
        ]
        total_shape = (total if half else total // 2, 2 * head_size)
        out_shape = [jax.ShapeDtypeStruct((head_size, rows), jnp.float32)]
        if not is_last:
            out_shape.append(jax.ShapeDtypeStruct(total_shape, jnp.float32))
        if hands_out:
            out_shape.append(jax.ShapeDtypeStruct(span_wide, jnp.float32))
            out_shape += [jax.ShapeDtypeStruct(span_wide, jnp.bfloat16)] * (count - 1)
        pairs = rows * (3 * total // 4 if half == 1 else total // 4)
        dq, *handed = pl.pallas_call(
            functools.partial(
                chunk_kernel, chunk, heads, span_rows, count, is_first, is_last, hands_out,
                len(after),
            ),
            out_shape=out_shape,
            in_specs=[SCALARS] + [WHOLE] * len(operands),
            out_specs=[WHOLE] * len(out_shape),
            scratch_shapes=[pltpu.VMEM(total_shape, jnp.float32)] if is_last else [],
            compiler_params=params(),
            cost_estimate=pl.CostEstimate(
                flops=20 * pairs * head_size, bytes_accessed=2 * 2**20, transcendentals=pairs
            ),
        )(span_start, *operands)
        dq_parts.append(dq)
        running = [] if is_last else [handed.pop(0)]
        if hands_out:
            received = [handed[0]] + [
                with_partner(send, "ctx", step) for step, send in enumerate(handed[1:], start=1)
            ]

    places = [(half * span_rows + first) * heads for half, first, _ in chunks]
    upper_sum, dq = finish(upper_terms, dq_parts, places, q_flat.shape)
    key_out, value_out = pl.pallas_call(
        functools.partial(add_kernel, count, span_rows, head_size),
        out_shape=(jax.ShapeDtypeStruct((row_count, head_size), jnp.bfloat16),) * 2,
        in_specs=[WHOLE] * (count + 1),
        out_specs=(WHOLE,) * 2,
        compiler_params=params(),
    )(*received, upper_sum)
    return (dq.reshape(queries.shape), key_out[None], value_out[None])


def solution(mesh):
    placed = (
        P("section", "ctx", None, None),
        P("section", "ctx", None),
        P("section", "ctx", None),
        P("section", "ctx", None, None),
        P("section", "ctx", None, None),
        P("section", None, "ctx"),
        P(),
    )
    return jax.shard_map(
        body,
        mesh=mesh,
        in_specs=placed,
        out_specs=(
            P("section", "ctx", None, None),
            P("section", "ctx", None),
            P("section", "ctx", None),
        ),
        check_vma=False,
    )
```

```python
import functools
import math

import jax
import jax.numpy as jnp
from jax import lax
from jax.experimental import pallas as pl
from jax.experimental.pallas import tpu as pltpu
from jax.sharding import PartitionSpec as P

KEY_BLOCK = 256
CHUNK_TOKENS = 64
VMEM_LIMIT = 40 * 1024 * 1024
CUT_LIMIT = 62 * 1024 * 1024
SORT_FLOPS = 10**9
WIDEN_FLOPS = 4 * 10**9

WHOLE = pl.BlockSpec(memory_space=pltpu.VMEM)
SCALARS = pl.BlockSpec(memory_space=pltpu.SMEM)
ANYWHERE = pl.BlockSpec(memory_space=pl.ANY)
NT = (((1,), (1,)), ((), ()))


def from_behind(shard, axis, by):
    length = lax.axis_size(axis)
    return lax.ppermute(shard, axis, [(i, (i + by) % length) for i in range(length)])


def with_partner(shard, axis, step):
    length = lax.axis_size(axis)
    return lax.ppermute(shard, axis, [(i, i ^ step) for i in range(length)])


def params(limit=VMEM_LIMIT):
    return pltpu.CompilerParams(vmem_limit_bytes=limit)


def cut_kernel(cuts, source_ref, keys_ref, values_ref, *refs):
    pair_ref, *out_refs, held, held_pair, in_sems, out_sems = refs
    moves = []
    for (first, size), out_ref in zip(cuts, out_refs):
        rows = pl.ds(first, size)
        moves.append((source_ref.at[rows], held.at[rows], out_ref))
    for i, part_ref in enumerate((keys_ref, values_ref)):
        moves.append((part_ref.at[0], held_pair.at[i], pair_ref.at[i]))
    copies = [
        (
            pltpu.make_async_copy(source, stage, in_sems.at[i]),
            pltpu.make_async_copy(stage, target, out_sems.at[i]),
        )
        for i, (source, stage, target) in enumerate(moves)
    ]
    for fetch, _ in copies:
        fetch.start()
    for fetch, store in copies:
        fetch.wait()
        store.start()
    for _, store in copies:
        store.wait()


def cut(source, keys, values, cuts):
    pair = (2, *keys.shape[1:])
    return pl.pallas_call(
        functools.partial(cut_kernel, cuts),
        out_shape=[jax.ShapeDtypeStruct(pair, keys.dtype)]
        + [jax.ShapeDtypeStruct((size, *source.shape[1:]), source.dtype) for _, size in cuts],
        in_specs=[ANYWHERE] * 3,
        out_specs=[ANYWHERE] * (len(cuts) + 1),
        scratch_shapes=[
            pltpu.VMEM(source.shape, source.dtype),
            pltpu.VMEM(pair, keys.dtype),
            pltpu.SemaphoreType.DMA((len(cuts) + 2,)),
            pltpu.SemaphoreType.DMA((len(cuts) + 2,)),
        ],
        compiler_params=params(CUT_LIMIT),
        cost_estimate=pl.CostEstimate(
            flops=0, bytes_accessed=2 * source.size * source.dtype.itemsize, transcendentals=0
        ),
    )(source, keys, values)


def widen_kernel(rows, g_ref, o_ref, wide_ref):
    head_size = g_ref.shape[1]
    g = g_ref[...]
    wide_ref[:, :head_size] = g
    wide_ref[:, head_size:] = times(g, o_ref[rows, :])


def widen(grad, outputs, first):
    row_count, head_size = grad.shape
    return pl.pallas_call(
        functools.partial(widen_kernel, slice(first, first + row_count)),
        out_shape=jax.ShapeDtypeStruct((row_count, 2 * head_size), grad.dtype),
        in_specs=[WHOLE] * 2,
        out_specs=WHOLE,
        compiler_params=params(),
        cost_estimate=pl.CostEstimate(
            flops=WIDEN_FLOPS, bytes_accessed=grad.size * 8, transcendentals=0
        ),
    )(grad, outputs)


def times(g, o):
    return (g.astype(jnp.float32) * o.astype(jnp.float32)).astype(jnp.bfloat16)


def sort_keys_kernel(codes, span_rows, head_size, starts_ref, *refs):
    count = len(codes)
    blocks = refs[:count]
    keys_ref, values_ref, keys_t_ref = refs[count:]
    me = lax.axis_index("ctx")
    values_ref[:, head_size:] = jnp.full(
        (values_ref.shape[0], values_ref.shape[1] - head_size), -1.0, values_ref.dtype
    )
    for block, code in zip(blocks, codes):
        owner = lax.bitwise_xor(me, code)
        for half in range(2):
            start = pl.multiple_of(starts_ref[2 * owner + half], span_rows)
            rows = pl.ds(start, span_rows)
            part = slice(half * span_rows, (half + 1) * span_rows)
            keys = block[0, part, :]
            keys_ref[rows, :] = keys
            values_ref[rows, :head_size] = block[1, part, :]
            keys_t_ref[:, rows] = keys.astype(jnp.float32).T.astype(jnp.bfloat16)


def sort_keys(span_start, blocks, codes, span_rows, head_size):
    count = len(blocks)
    total = count * 2 * span_rows
    return pl.pallas_call(
        functools.partial(sort_keys_kernel, codes, span_rows, head_size),
        out_shape=(
            jax.ShapeDtypeStruct((total, head_size), jnp.bfloat16),
            jax.ShapeDtypeStruct((total, 2 * head_size), jnp.bfloat16),
            jax.ShapeDtypeStruct((head_size, total), jnp.bfloat16),
        ),
        in_specs=[SCALARS] + [WHOLE] * count,
        out_specs=(WHOLE,) * 3,
        compiler_params=params(),
        cost_estimate=pl.CostEstimate(
            flops=SORT_FLOPS, bytes_accessed=8 * total * head_size, transcendentals=0
        ),
    )(span_start, *blocks)


def chunk_grads(
    chunk, heads, span_rows, starts_ref, q_ref, g_ref, o_ref, lse_ref, keys_ref, values_ref,
    keys_t_ref, total_ref, dq_ref,
):
    half, first, tokens = chunk
    head_size = q_ref.shape[1]
    scale = head_size**-0.5
    to_log2 = math.log2(math.e)
    me = lax.axis_index("ctx")
    start = starts_ref[2 * me + half]
    row_count = tokens * heads
    row_first = (half * span_rows + first) * heads
    rows = slice(row_first, row_first + row_count)
    full_blocks = start // KEY_BLOCK

    q = q_ref[rows, :]
    g = g_ref[...]
    if g.shape[1] == head_size:
        g_wide = jnp.concatenate([g, times(g, o_ref[rows, :])], axis=1)
    else:
        g, g_wide = g[:, :head_size], g
    lse2 = lse_ref[0:1, rows] * to_log2
    dq_ref[...] = jnp.zeros_like(dq_ref)

    def block(index, masked):
        base = pl.multiple_of(index * KEY_BLOCK, KEY_BLOCK)
        at = pl.ds(base, KEY_BLOCK)
        scores = lax.dot_general(keys_ref[at, :], q, NT, preferred_element_type=jnp.float32)
        probs = jnp.exp2(scores * (scale * to_log2) - lse2)
        if masked:
            query_row = lax.broadcasted_iota(jnp.int32, (1, row_count), 1)
            query_pos = start + first + query_row // heads
            key_pos = base + lax.broadcasted_iota(jnp.int32, (KEY_BLOCK, 1), 0)
            probs = jnp.where(key_pos <= query_pos, probs, 0.0)
        centred = lax.dot_general(values_ref[at, :], g_wide, NT, preferred_element_type=jnp.float32)
        grad_scores = (probs * centred).astype(jnp.bfloat16)
        probs_low = probs.astype(jnp.bfloat16)
        total_ref[at, :head_size] += jnp.dot(grad_scores, q, preferred_element_type=jnp.float32)
        total_ref[at, head_size:] += jnp.dot(probs_low, g, preferred_element_type=jnp.float32)
        dq_ref[...] += jnp.dot(keys_t_ref[:, at], grad_scores, preferred_element_type=jnp.float32)

    def dense(index, carry):
        block(index, False)
        return carry

    lax.fori_loop(0, full_blocks, dense, 0)
    block(full_blocks, True)


def hand_out(half, count, span_rows, starts_ref, total_ref, own_ref, send_ref):
    head_size = total_ref.shape[1] // 2
    scale = head_size**-0.5
    me = lax.axis_index("ctx")
    for owner in range(count):
        start = pl.multiple_of(starts_ref[2 * owner + half], span_rows)
        rows = pl.ds(start, span_rows)
        send_ref[owner, :, :head_size] = (total_ref[rows, :head_size] * scale).astype(jnp.bfloat16)
        send_ref[owner, :, head_size:] = total_ref[rows, head_size:].astype(jnp.bfloat16)
    rows = pl.ds(pl.multiple_of(starts_ref[2 * me + half], span_rows), span_rows)
    own_ref[:, :head_size] = total_ref[rows, :head_size] * scale
    own_ref[:, head_size:] = total_ref[rows, head_size:]


def add_terms(own_ref, terms_ref):
    me = lax.axis_index("ctx")
    total = own_ref[...]
    for owner in range(terms_ref.shape[0]):
        term = terms_ref[owner].astype(jnp.float32)
        total = total + jnp.where(me == owner, 0.0, term)
    return total.astype(jnp.bfloat16)


def chunk_kernel(
    chunk, heads, span_rows, count, is_first, is_last, hands_out, n_after, starts_ref, q_ref, g_ref, o_ref,
    lse_ref, keys_ref, values_ref, keys_t_ref, *refs,
):
    refs = list(refs[n_after:])
    total_in = None if is_first else refs.pop(0)
    total_ref = refs.pop() if is_last else refs.pop(1)
    dq_ref, *handed = refs
    if is_first:
        total_ref[...] = jnp.zeros_like(total_ref)
    else:
        total_ref[...] = total_in[: total_ref.shape[0], :]
    chunk_grads(
        chunk, heads, span_rows, starts_ref, q_ref, g_ref, o_ref, lse_ref, keys_ref, values_ref,
        keys_t_ref, total_ref, dq_ref,
    )
    if hands_out:
        hand_out(chunk[0], count, span_rows, starts_ref, total_ref, *handed)


def add_kernel(span_rows, head_size, own_ref, terms_ref, upper_ref, key_ref, value_ref):
    lower = add_terms(own_ref, terms_ref)
    for out_ref, columns in ((key_ref, slice(0, head_size)), (value_ref, slice(head_size, None))):
        out_ref[:span_rows, :] = lower[:, columns]
        out_ref[span_rows:, :] = upper_ref[:, columns]


def finish_kernel(places, own_ref, terms_ref, *refs):
    part_refs, (upper_ref, out_ref, held, sems) = refs[: len(places)], refs[len(places) :]
    scale = out_ref.shape[1] ** -0.5
    copies = []
    for i, (first, part_ref) in enumerate(zip(places, part_refs)):
        rows = pl.ds(first, part_ref.shape[1])
        held[rows, :] = (part_ref[...] * scale).T.astype(jnp.bfloat16)
        copies.append(pltpu.make_async_copy(held.at[rows], out_ref.at[rows], sems.at[i]))
        copies[-1].start()
    upper_ref[...] = add_terms(own_ref, terms_ref)
    for copy in copies:
        copy.wait()


def finish(terms, parts, places, shape):
    return pl.pallas_call(
        functools.partial(finish_kernel, places),
        out_shape=(
            jax.ShapeDtypeStruct(terms[0].shape, jnp.bfloat16),
            jax.ShapeDtypeStruct(shape, jnp.bfloat16),
        ),
        in_specs=[WHOLE] * (len(terms) + len(parts)),
        out_specs=(WHOLE, ANYWHERE),
        scratch_shapes=[
            pltpu.VMEM(shape, jnp.bfloat16),
            pltpu.SemaphoreType.DMA((len(parts),)),
        ],
        compiler_params=params(),
    )(*terms, *parts)


def body(queries, keys, values, outputs, grad_held, lse, span_start):
    count = lax.axis_size("ctx")
    row_count, heads, head_size = queries.shape[1:]
    span_rows = row_count // 2
    total = count * row_count
    chunks = [
        (half, first, CHUNK_TOKENS) for half in (1, 0) for first in range(0, span_rows, CHUNK_TOKENS)
    ]
    per_half = len(chunks) // 2

    pair, *pieces = cut(
        grad_held[0], keys, values,
        [(half * span_rows + first, size) for half, first, size in chunks],
    )
    grads = [from_behind(pieces[0], "section", -1)]
    blocks, codes = [pair], [0]
    step = count // 2
    while step:
        blocks = blocks + [with_partner(block, "ctx", step) for block in blocks]
        codes = codes + [code ^ step for code in codes]
        step //= 2
    for piece, gate in zip(pieces[1:], [None, None] + [blocks[1]] * len(pieces)):
        if gate is not None:
            piece, _ = lax.optimization_barrier((piece, gate))
        grads.append(from_behind(piece, "section", -1))
    sorted_keys = sort_keys(span_start, blocks, codes, span_rows, head_size)

    q_flat = queries.reshape(row_count * heads, head_size)
    o_flat = outputs.reshape(row_count * heads, head_size)
    lse_flat = lse[0].T.reshape(1, row_count * heads)

    span_wide = (span_rows, 2 * head_size)
    running, received, dq_parts = [], [], []
    for number, chunk in enumerate(chunks):
        half, _, tokens = chunk
        rows = tokens * heads
        is_first, is_last = number == 0, number == len(chunks) - 1
        hands_out = number % per_half == per_half - 1
        after = received if is_last else []
        if after:
            upper_terms = received
        grad = grads[number].reshape(rows, head_size)
        if is_first:
            grad = widen(grad, o_flat, (half * span_rows + chunk[1]) * heads)
        operands = [
            q_flat, grad, o_flat, lse_flat, *sorted_keys, *after,
            *running,
        ]
        total_shape = (total if half else total // 2, 2 * head_size)
        out_shape = [jax.ShapeDtypeStruct((head_size, rows), jnp.float32)]
        if not is_last:
            out_shape.append(jax.ShapeDtypeStruct(total_shape, jnp.float32))
        if hands_out:
            out_shape.append(jax.ShapeDtypeStruct(span_wide, jnp.float32))
            out_shape.append(jax.ShapeDtypeStruct((count, *span_wide), jnp.bfloat16))
        pairs = rows * (3 * total // 4 if half == 1 else total // 4)
        dq, *handed = pl.pallas_call(
            functools.partial(
                chunk_kernel, chunk, heads, span_rows, count, is_first, is_last, hands_out,
                len(after),
            ),
            out_shape=out_shape,
            in_specs=[SCALARS] + [WHOLE] * len(operands),
            out_specs=[WHOLE] * len(out_shape),
            scratch_shapes=[pltpu.VMEM(total_shape, jnp.float32)] if is_last else [],
            compiler_params=params(),
            cost_estimate=pl.CostEstimate(
                flops=20 * pairs * head_size, bytes_accessed=2 * 2**20, transcendentals=pairs
            ),
        )(span_start, *operands)
        dq_parts.append(dq)
        running = [] if is_last else [handed.pop(0)]
        if hands_out:
            received = [handed[0], lax.all_to_all(handed[1], "ctx", 0, 0)]

    places = [(half * span_rows + first) * heads for half, first, _ in chunks]
    upper_sum, dq = finish(upper_terms, dq_parts, places, q_flat.shape)
    key_out, value_out = pl.pallas_call(
        functools.partial(add_kernel, span_rows, head_size),
        out_shape=(jax.ShapeDtypeStruct((row_count, head_size), jnp.bfloat16),) * 2,
        in_specs=[WHOLE] * 3,
        out_specs=(WHOLE,) * 2,
        compiler_params=params(),
    )(*received, upper_sum)
    return (dq.reshape(queries.shape), key_out[None], value_out[None])


def solution(mesh):
    placed = (
        P("section", "ctx", None, None),
        P("section", "ctx", None),
        P("section", "ctx", None),
        P("section", "ctx", None, None),
        P("section", "ctx", None, None),
        P("section", None, "ctx"),
        P(),
    )
    return jax.shard_map(
        body,
        mesh=mesh,
        in_specs=placed,
        out_specs=(
            P("section", "ctx", None, None),
            P("section", "ctx", None),
            P("section", "ctx", None),
        ),
        check_vma=False,
    )
```

```python
import functools
import math

import jax
import jax.numpy as jnp
from jax import lax
from jax.experimental import pallas as pl
from jax.experimental.pallas import tpu as pltpu
from jax.sharding import PartitionSpec as P

KEY_BLOCK = 256
CHUNK_TOKENS = 64
VMEM_LIMIT = 40 * 1024 * 1024
SORT_FLOPS = 10**9
WIDEN_FLOPS = 4 * 10**9

WHOLE = pl.BlockSpec(memory_space=pltpu.VMEM)
SCALARS = pl.BlockSpec(memory_space=pltpu.SMEM)
ANYWHERE = pl.BlockSpec(memory_space=pl.ANY)
NT = (((1,), (1,)), ((), ()))


def from_behind(shard, axis, by):
    length = lax.axis_size(axis)
    return lax.ppermute(shard, axis, [(i, (i + by) % length) for i in range(length)])


def with_partner(shard, axis, step):
    length = lax.axis_size(axis)
    return lax.ppermute(shard, axis, [(i, i ^ step) for i in range(length)])


def params(limit=VMEM_LIMIT):
    return pltpu.CompilerParams(vmem_limit_bytes=limit)


def cut_kernel(cuts, source_ref, starts_ref, *refs):
    *out_refs, sems = refs
    copies = [
        pltpu.make_async_copy(source_ref.at[pl.ds(first, size)], out_ref, sems.at[i])
        for i, ((first, size), out_ref) in enumerate(zip(cuts, out_refs))
    ]
    for copy in copies:
        copy.start()
    for copy in copies:
        copy.wait()


def cut(source, span_start, cuts):
    return pl.pallas_call(
        functools.partial(cut_kernel, cuts),
        out_shape=[
            jax.ShapeDtypeStruct((size, *source.shape[1:]), source.dtype) for _, size in cuts
        ],
        in_specs=[ANYWHERE, WHOLE],
        out_specs=[ANYWHERE] * len(cuts),
        scratch_shapes=[pltpu.SemaphoreType.DMA((len(cuts),))],
        compiler_params=params(),
        cost_estimate=pl.CostEstimate(
            flops=0, bytes_accessed=2 * source.size * source.dtype.itemsize, transcendentals=0
        ),
    )(source, span_start)


def widen_kernel(rows, g_ref, o_ref, *refs):
    wide_ref = refs[-1]
    head_size = g_ref.shape[1]
    g = g_ref[...]
    wide_ref[:, :head_size] = g
    wide_ref[:, head_size:] = times(g, o_ref[rows, :])


def widen(grad, outputs, first, *others):
    row_count, head_size = grad.shape
    return pl.pallas_call(
        functools.partial(widen_kernel, slice(first, first + row_count)),
        out_shape=jax.ShapeDtypeStruct((row_count, 2 * head_size), grad.dtype),
        in_specs=[WHOLE] * (2 + len(others)),
        out_specs=WHOLE,
        compiler_params=params(),
        cost_estimate=pl.CostEstimate(
            flops=WIDEN_FLOPS, bytes_accessed=grad.size * 8, transcendentals=0
        ),
    )(grad, outputs, *others)


def times(g, o):
    return (g.astype(jnp.float32) * o.astype(jnp.float32)).astype(jnp.bfloat16)


def sort_keys_kernel(codes, span_rows, head_size, starts_ref, *refs):
    count = len(codes)
    blocks = refs[:count]
    keys_ref, values_ref, keys_t_ref = refs[count:]
    me = lax.axis_index("ctx")
    values_ref[:, head_size:] = jnp.full(
        (values_ref.shape[0], values_ref.shape[1] - head_size), -1.0, values_ref.dtype
    )
    for block, code in zip(blocks, codes):
        owner = lax.bitwise_xor(me, code)
        for half in range(2):
            start = pl.multiple_of(starts_ref[2 * owner + half], span_rows)
            rows = pl.ds(start, span_rows)
            part = slice(half * span_rows, (half + 1) * span_rows)
            keys = block[0, part, :]
            keys_ref[rows, :] = keys
            values_ref[rows, :head_size] = block[1, part, :]
            keys_t_ref[:, rows] = keys.astype(jnp.float32).T.astype(jnp.bfloat16)


def sort_keys(span_start, blocks, codes, span_rows, head_size):
    count = len(blocks)
    total = count * 2 * span_rows
    return pl.pallas_call(
        functools.partial(sort_keys_kernel, codes, span_rows, head_size),
        out_shape=(
            jax.ShapeDtypeStruct((total, head_size), jnp.bfloat16),
            jax.ShapeDtypeStruct((total, 2 * head_size), jnp.bfloat16),
            jax.ShapeDtypeStruct((head_size, total), jnp.bfloat16),
        ),
        in_specs=[SCALARS] + [WHOLE] * count,
        out_specs=(WHOLE,) * 3,
        compiler_params=params(),
        cost_estimate=pl.CostEstimate(
            flops=SORT_FLOPS, bytes_accessed=8 * total * head_size, transcendentals=0
        ),
    )(span_start, *blocks)


def chunk_grads(
    chunk, heads, span_rows, starts_ref, q_ref, g_ref, o_ref, lse_ref, keys_ref, values_ref,
    keys_t_ref, total_ref, dq_ref,
):
    half, first, tokens = chunk
    head_size = q_ref.shape[1]
    scale = head_size**-0.5
    to_log2 = math.log2(math.e)
    me = lax.axis_index("ctx")
    start = starts_ref[2 * me + half]
    row_count = tokens * heads
    row_first = (half * span_rows + first) * heads
    rows = slice(row_first, row_first + row_count)
    full_blocks = start // KEY_BLOCK

    q = q_ref[rows, :]
    g = g_ref[...]
    if g.shape[1] == head_size:
        g_wide = jnp.concatenate([g, times(g, o_ref[rows, :])], axis=1)
    else:
        g, g_wide = g[:, :head_size], g
    lse2 = lse_ref[0:1, rows] * to_log2
    dq_ref[...] = jnp.zeros_like(dq_ref)

    def block(index, masked):
        base = pl.multiple_of(index * KEY_BLOCK, KEY_BLOCK)
        at = pl.ds(base, KEY_BLOCK)
        scores = lax.dot_general(keys_ref[at, :], q, NT, preferred_element_type=jnp.float32)
        probs = jnp.exp2(scores * (scale * to_log2) - lse2)
        if masked:
            query_row = lax.broadcasted_iota(jnp.int32, (1, row_count), 1)
            query_pos = start + first + query_row // heads
            key_pos = base + lax.broadcasted_iota(jnp.int32, (KEY_BLOCK, 1), 0)
            probs = jnp.where(key_pos <= query_pos, probs, 0.0)
        centred = lax.dot_general(values_ref[at, :], g_wide, NT, preferred_element_type=jnp.float32)
        grad_scores = (probs * centred).astype(jnp.bfloat16)
        probs_low = probs.astype(jnp.bfloat16)
        total_ref[at, :head_size] += jnp.dot(grad_scores, q, preferred_element_type=jnp.float32)
        total_ref[at, head_size:] += jnp.dot(probs_low, g, preferred_element_type=jnp.float32)
        dq_ref[...] += jnp.dot(keys_t_ref[:, at], grad_scores, preferred_element_type=jnp.float32)

    def dense(index, carry):
        block(index, False)
        return carry

    lax.fori_loop(0, full_blocks, dense, 0)
    block(full_blocks, True)


def hand_out(half, count, span_rows, starts_ref, total_ref, own_ref, send_refs):
    head_size = total_ref.shape[1] // 2
    scale = head_size**-0.5
    me = lax.axis_index("ctx")
    for step in range(count):
        owner = lax.bitwise_xor(me, step)
        start = pl.multiple_of(starts_ref[2 * owner + half], span_rows)
        rows = pl.ds(start, span_rows)
        target = own_ref if step == 0 else send_refs[step - 1]
        target[:, :head_size] = (total_ref[rows, :head_size] * scale).astype(target.dtype)
        target[:, head_size:] = total_ref[rows, head_size:].astype(target.dtype)


def add_terms(term_refs):
    total = term_refs[0][...]
    for term_ref in term_refs[1:]:
        total = total + term_ref[...].astype(jnp.float32)
    return total


def chunk_kernel(
    chunk, heads, span_rows, count, is_first, is_last, hands_out, n_after, starts_ref, q_ref, g_ref, o_ref,
    lse_ref, keys_ref, values_ref, keys_t_ref, *refs,
):
    refs = list(refs[n_after:])
    total_in = None if is_first else refs.pop(0)
    total_ref = refs.pop() if is_last else refs.pop(1)
    dq_ref, *handed = refs
    if is_first:
        total_ref[...] = jnp.zeros_like(total_ref)
    else:
        total_ref[...] = total_in[: total_ref.shape[0], :]
    chunk_grads(
        chunk, heads, span_rows, starts_ref, q_ref, g_ref, o_ref, lse_ref, keys_ref, values_ref,
        keys_t_ref, total_ref, dq_ref,
    )
    if hands_out:
        hand_out(chunk[0], count, span_rows, starts_ref, total_ref, handed[0], handed[1:])


def add_kernel(count, span_rows, head_size, *refs):
    term_refs, upper_ref, (key_ref, value_ref) = refs[:count], refs[count], refs[count + 1 :]
    lower = add_terms(term_refs).astype(jnp.bfloat16)
    for out_ref, columns in ((key_ref, slice(0, head_size)), (value_ref, slice(head_size, None))):
        out_ref[:span_rows, :] = lower[:, columns]
        out_ref[span_rows:, :] = upper_ref[:, columns]


def finish_kernel(count, places, *refs):
    term_refs, refs = refs[:count], refs[count:]
    part_refs, (upper_ref, out_ref, held, sems) = refs[: len(places)], refs[len(places) :]
    scale = out_ref.shape[1] ** -0.5
    copies = []
    for i, (first, part_ref) in enumerate(zip(places, part_refs)):
        rows = pl.ds(first, part_ref.shape[1])
        held[rows, :] = (part_ref[...] * scale).T.astype(jnp.bfloat16)
        copies.append(pltpu.make_async_copy(held.at[rows], out_ref.at[rows], sems.at[i]))
        copies[-1].start()
    upper_ref[...] = add_terms(term_refs).astype(jnp.bfloat16)
    for copy in copies:
        copy.wait()


def finish(terms, parts, places, shape):
    return pl.pallas_call(
        functools.partial(finish_kernel, len(terms), places),
        out_shape=(
            jax.ShapeDtypeStruct(terms[0].shape, jnp.bfloat16),
            jax.ShapeDtypeStruct(shape, jnp.bfloat16),
        ),
        in_specs=[WHOLE] * (len(terms) + len(parts)),
        out_specs=(WHOLE, ANYWHERE),
        scratch_shapes=[
            pltpu.VMEM(shape, jnp.bfloat16),
            pltpu.SemaphoreType.DMA((len(parts),)),
        ],
        compiler_params=params(),
    )(*terms, *parts)


def body(queries, keys, values, outputs, grad_held, lse, span_start):
    count = lax.axis_size("ctx")
    row_count, heads, head_size = queries.shape[1:]
    span_rows = row_count // 2
    total = count * row_count
    chunks = [
        (half, first, CHUNK_TOKENS) for half in (1, 0) for first in range(0, span_rows, CHUNK_TOKENS)
    ]
    per_half = len(chunks) // 2

    pieces = cut(
        grad_held[0], span_start, [(half * span_rows + first, size) for half, first, size in chunks]
    )
    grads = [from_behind(pieces[0], "section", -1)]
    pair = jnp.concatenate(lax.optimization_barrier((keys, values, pieces[0]))[:2], axis=0)
    blocks, codes = [pair], [0]
    step = count // 2
    while step:
        blocks = blocks + [with_partner(block, "ctx", step) for block in blocks]
        codes = codes + [code ^ step for code in codes]
        step //= 2
    for piece, gate in zip(pieces[1:], [None, None] + [blocks[1]] * len(pieces)):
        if gate is not None:
            piece, _ = lax.optimization_barrier((piece, gate))
        grads.append(from_behind(piece, "section", -1))
    sorted_keys = sort_keys(span_start, blocks, codes, span_rows, head_size)

    q_flat = queries.reshape(row_count * heads, head_size)
    o_flat = outputs.reshape(row_count * heads, head_size)
    lse_flat = lse[0].T.reshape(1, row_count * heads)

    span_wide = (span_rows, 2 * head_size)
    running, received, dq_parts = [], [], []
    for number, chunk in enumerate(chunks):
        half, _, tokens = chunk
        rows = tokens * heads
        is_first, is_last = number == 0, number == len(chunks) - 1
        hands_out = number % per_half == per_half - 1
        after = received if is_last else []
        if after:
            upper_terms = received
        grad = grads[number].reshape(rows, head_size)
        if is_first:
            grad = widen(grad, o_flat, (half * span_rows + chunk[1]) * heads)
        operands = [
            q_flat, grad, o_flat, lse_flat, *sorted_keys, *after,
            *running,
        ]
        total_shape = (total if half else total // 2, 2 * head_size)
        out_shape = [jax.ShapeDtypeStruct((head_size, rows), jnp.float32)]
        if not is_last:
            out_shape.append(jax.ShapeDtypeStruct(total_shape, jnp.float32))
        if hands_out:
            out_shape.append(jax.ShapeDtypeStruct(span_wide, jnp.float32))
            out_shape += [jax.ShapeDtypeStruct(span_wide, jnp.bfloat16)] * (count - 1)
        pairs = rows * (3 * total // 4 if half == 1 else total // 4)
        dq, *handed = pl.pallas_call(
            functools.partial(
                chunk_kernel, chunk, heads, span_rows, count, is_first, is_last, hands_out,
                len(after),
            ),
            out_shape=out_shape,
            in_specs=[SCALARS] + [WHOLE] * len(operands),
            out_specs=[WHOLE] * len(out_shape),
            scratch_shapes=[pltpu.VMEM(total_shape, jnp.float32)] if is_last else [],
            compiler_params=params(),
            cost_estimate=pl.CostEstimate(
                flops=20 * pairs * head_size, bytes_accessed=2 * 2**20, transcendentals=pairs
            ),
        )(span_start, *operands)
        dq_parts.append(dq)
        running = [] if is_last else [handed.pop(0)]
        if hands_out:
            received = [handed[0]] + [
                with_partner(send, "ctx", step) for step, send in enumerate(handed[1:], start=1)
            ]

    places = [(half * span_rows + first) * heads for half, first, _ in chunks]
    upper_sum, dq = finish(upper_terms, dq_parts, places, q_flat.shape)
    key_out, value_out = pl.pallas_call(
        functools.partial(add_kernel, count, span_rows, head_size),
        out_shape=(jax.ShapeDtypeStruct((row_count, head_size), jnp.bfloat16),) * 2,
        in_specs=[WHOLE] * (count + 1),
        out_specs=(WHOLE,) * 2,
        compiler_params=params(),
    )(*received, upper_sum)
    return (dq.reshape(queries.shape), key_out[None], value_out[None])


def solution(mesh):
    placed = (
        P("section", "ctx", None, None),
        P("section", "ctx", None),
        P("section", "ctx", None),
        P("section", "ctx", None, None),
        P("section", "ctx", None, None),
        P("section", None, "ctx"),
        P(),
    )
    return jax.shard_map(
        body,
        mesh=mesh,
        in_specs=placed,
        out_specs=(
            P("section", "ctx", None, None),
            P("section", "ctx", None),
            P("section", "ctx", None),
        ),
        check_vma=False,
    )
```

```python
import functools
import math

import jax
import jax.numpy as jnp
from jax import lax
from jax.experimental import pallas as pl
from jax.experimental.pallas import tpu as pltpu
from jax.sharding import PartitionSpec as P

KEY_BLOCK = 256
CHUNK_TOKENS = 64
VMEM_LIMIT = 40 * 1024 * 1024
SORT_FLOPS = 10**9
WIDEN_FLOPS = 4*10**9

WHOLE = pl.BlockSpec(memory_space=pltpu.VMEM)
SCALARS = pl.BlockSpec(memory_space=pltpu.SMEM)
ANYWHERE = pl.BlockSpec(memory_space=pl.ANY)
NT = (((1,), (1,)), ((), ()))


def from_behind(shard, axis, by):
    length = lax.axis_size(axis)
    return lax.ppermute(shard, axis, [(i, (i + by) % length) for i in range(length)])


def with_partner(shard, axis, step):
    length = lax.axis_size(axis)
    return lax.ppermute(shard, axis, [(i, i ^ step) for i in range(length)])


def params(limit=VMEM_LIMIT):
    return pltpu.CompilerParams(vmem_limit_bytes=limit)


def cut_kernel(cuts, source_ref, *refs):
    *out_refs, sems = refs
    copies = [
        pltpu.make_async_copy(source_ref.at[pl.ds(first, size)], out_ref, sems.at[i])
        for i, ((first, size), out_ref) in enumerate(zip(cuts, out_refs))
    ]
    for copy in copies:
        copy.start()
    for copy in copies:
        copy.wait()


def cut(source, cuts):
    return pl.pallas_call(
        functools.partial(cut_kernel, cuts),
        out_shape=[
            jax.ShapeDtypeStruct((size, *source.shape[1:]), source.dtype) for _, size in cuts
        ],
        in_specs=[ANYWHERE],
        out_specs=[ANYWHERE] * len(cuts),
        scratch_shapes=[pltpu.SemaphoreType.DMA((len(cuts),))],
        compiler_params=params(),
        cost_estimate=pl.CostEstimate(
            flops=0, bytes_accessed=2 * source.size * source.dtype.itemsize, transcendentals=0
        ),
    )(source)


def widen_kernel(rows, g_ref, o_ref, *refs):
    wide_ref = refs[-1]
    head_size = g_ref.shape[1]
    g = g_ref[...]
    wide_ref[:, :head_size] = g
    wide_ref[:, head_size:] = times(g, o_ref[rows, :])


def widen(grad, outputs, first, *others):
    row_count, head_size = grad.shape
    return pl.pallas_call(
        functools.partial(widen_kernel, slice(first, first + row_count)),
        out_shape=jax.ShapeDtypeStruct((row_count, 2 * head_size), grad.dtype),
        in_specs=[WHOLE] * (2 + len(others)),
        out_specs=WHOLE,
        compiler_params=params(),
        cost_estimate=pl.CostEstimate(
            flops=WIDEN_FLOPS, bytes_accessed=grad.size * 8, transcendentals=0
        ),
    )(grad, outputs, *others)


def times(g, o):
    return (g.astype(jnp.float32) * o.astype(jnp.float32)).astype(jnp.bfloat16)


def sort_keys_kernel(codes, span_rows, head_size, starts_ref, *refs):
    held_ref, got_ref, keys_ref, values_ref, keys_t_ref = refs
    half_count = len(codes) // 2
    blocks = [(ref, 2 * i) for ref in (held_ref, got_ref) for i in range(half_count)]
    me = lax.axis_index("ctx")
    values_ref[:, head_size:] = jnp.full(
        (values_ref.shape[0], values_ref.shape[1] - head_size), -1.0, values_ref.dtype
    )
    for (block, at), code in zip(blocks, codes):
        owner = lax.bitwise_xor(me, code)
        for half in range(2):
            start = pl.multiple_of(starts_ref[2 * owner + half], span_rows)
            rows = pl.ds(start, span_rows)
            part = slice(half * span_rows, (half + 1) * span_rows)
            keys = block[at, part, :]
            keys_ref[rows, :] = keys
            values_ref[rows, :head_size] = block[at + 1, part, :]
            keys_t_ref[:, rows] = keys.astype(jnp.float32).T.astype(jnp.bfloat16)


def sort_keys(span_start, blocks, codes, span_rows, head_size):
    total = len(codes) * 2 * span_rows
    return pl.pallas_call(
        functools.partial(sort_keys_kernel, codes, span_rows, head_size),
        out_shape=(
            jax.ShapeDtypeStruct((total, head_size), jnp.bfloat16),
            jax.ShapeDtypeStruct((total, 2 * head_size), jnp.bfloat16),
            jax.ShapeDtypeStruct((head_size, total), jnp.bfloat16),
        ),
        in_specs=[SCALARS] + [WHOLE] * len(blocks),
        out_specs=(WHOLE,) * 3,
        compiler_params=params(),
        cost_estimate=pl.CostEstimate(
            flops=SORT_FLOPS, bytes_accessed=8 * total * head_size, transcendentals=0
        ),
    )(span_start, *blocks)


def chunk_grads(
    chunk, heads, span_rows, starts_ref, q_ref, g_ref, o_ref, lse_ref, keys_ref, values_ref,
    keys_t_ref, total_ref, dq_ref,
):
    half, first, tokens = chunk
    head_size = q_ref.shape[1]
    scale = head_size**-0.5
    to_log2 = math.log2(math.e)
    me = lax.axis_index("ctx")
    start = starts_ref[2 * me + half]
    row_count = tokens * heads
    row_first = (half * span_rows + first) * heads
    rows = slice(row_first, row_first + row_count)
    full_blocks = start // KEY_BLOCK

    q = q_ref[rows, :]
    g = g_ref[...]
    if g.shape[1] == head_size:
        g_wide = jnp.concatenate([g, times(g, o_ref[rows, :])], axis=1)
    else:
        g, g_wide = g[:, :head_size], g
    lse2 = lse_ref[0:1, rows] * to_log2
    dq_ref[...] = jnp.zeros_like(dq_ref)

    def block(index, masked):
        base = pl.multiple_of(index * KEY_BLOCK, KEY_BLOCK)
        at = pl.ds(base, KEY_BLOCK)
        scores = lax.dot_general(keys_ref[at, :], q, NT, preferred_element_type=jnp.float32)
        probs = jnp.exp2(scores * (scale * to_log2) - lse2)
        if masked:
            query_row = lax.broadcasted_iota(jnp.int32, (1, row_count), 1)
            query_pos = start + first + query_row // heads
            key_pos = base + lax.broadcasted_iota(jnp.int32, (KEY_BLOCK, 1), 0)
            probs = jnp.where(key_pos <= query_pos, probs, 0.0)
        centred = lax.dot_general(values_ref[at, :], g_wide, NT, preferred_element_type=jnp.float32)
        grad_scores = (probs * centred).astype(jnp.bfloat16)
        probs_low = probs.astype(jnp.bfloat16)
        total_ref[at, :head_size] += jnp.dot(grad_scores, q, preferred_element_type=jnp.float32)
        total_ref[at, head_size:] += jnp.dot(probs_low, g, preferred_element_type=jnp.float32)
        dq_ref[...] += jnp.dot(keys_t_ref[:, at], grad_scores, preferred_element_type=jnp.float32)

    def dense(index, carry):
        block(index, False)
        return carry

    lax.fori_loop(0, full_blocks, dense, 0)
    block(full_blocks, True)


def hand_out(half, count, span_rows, starts_ref, total_ref, own_ref, send_refs):
    head_size = total_ref.shape[1] // 2
    scale = head_size**-0.5
    me = lax.axis_index("ctx")
    for step in range(count):
        owner = lax.bitwise_xor(me, step)
        start = pl.multiple_of(starts_ref[2 * owner + half], span_rows)
        rows = pl.ds(start, span_rows)
        target = own_ref if step == 0 else send_refs[step - 1]
        target[:, :head_size] = (total_ref[rows, :head_size] * scale).astype(target.dtype)
        target[:, head_size:] = total_ref[rows, head_size:].astype(target.dtype)


def add_terms(term_refs):
    total = term_refs[0][...]
    for term_ref in term_refs[1:]:
        total = total + term_ref[...].astype(jnp.float32)
    return total


def chunk_kernel(
    chunk, heads, span_rows, count, is_first, is_last, hands_out, n_after, starts_ref, q_ref, g_ref, o_ref,
    lse_ref, keys_ref, values_ref, keys_t_ref, *refs,
):
    refs = list(refs[n_after:])
    total_in = None if is_first else refs.pop(0)
    total_ref = refs.pop() if is_last else refs.pop(1)
    dq_ref, *handed = refs
    if is_first:
        total_ref[...] = jnp.zeros_like(total_ref)
    else:
        total_ref[...] = total_in[: total_ref.shape[0], :]
    chunk_grads(
        chunk, heads, span_rows, starts_ref, q_ref, g_ref, o_ref, lse_ref, keys_ref, values_ref,
        keys_t_ref, total_ref, dq_ref,
    )
    if hands_out:
        hand_out(chunk[0], count, span_rows, starts_ref, total_ref, handed[0], handed[1:])


def add_kernel(count, span_rows, head_size, *refs):
    term_refs, upper_ref, (key_ref, value_ref) = refs[:count], refs[count], refs[count + 1 :]
    lower = add_terms(term_refs).astype(jnp.bfloat16)
    for out_ref, columns in ((key_ref, slice(0, head_size)), (value_ref, slice(head_size, None))):
        out_ref[:span_rows, :] = lower[:, columns]
        out_ref[span_rows:, :] = upper_ref[:, columns]


def finish_kernel(count, places, *refs):
    term_refs, refs = refs[:count], refs[count:]
    part_refs, (upper_ref, out_ref, held, sems) = refs[: len(places)], refs[len(places) :]
    scale = out_ref.shape[1] ** -0.5
    copies = []
    for i, (first, part_ref) in enumerate(zip(places, part_refs)):
        rows = pl.ds(first, part_ref.shape[1])
        held[rows, :] = (part_ref[...] * scale).T.astype(jnp.bfloat16)
        copies.append(pltpu.make_async_copy(held.at[rows], out_ref.at[rows], sems.at[i]))
        copies[-1].start()
    upper_ref[...] = add_terms(term_refs).astype(jnp.bfloat16)
    for copy in copies:
        copy.wait()


def finish(terms, parts, places, shape):
    return pl.pallas_call(
        functools.partial(finish_kernel, len(terms), places),
        out_shape=(
            jax.ShapeDtypeStruct(terms[0].shape, jnp.bfloat16),
            jax.ShapeDtypeStruct(shape, jnp.bfloat16),
        ),
        in_specs=[WHOLE] * (len(terms) + len(parts)),
        out_specs=(WHOLE, ANYWHERE),
        scratch_shapes=[
            pltpu.VMEM(shape, jnp.bfloat16),
            pltpu.SemaphoreType.DMA((len(parts),)),
        ],
        compiler_params=params(),
    )(*terms, *parts)


def body(queries, keys, values, outputs, grad_held, lse, span_start):
    count = lax.axis_size("ctx")
    row_count, heads, head_size = queries.shape[1:]
    span_rows = row_count // 2
    total = count * row_count
    chunks = [
        (half, first, CHUNK_TOKENS) for half in (1, 0) for first in range(0, span_rows, CHUNK_TOKENS)
    ]
    per_half = len(chunks) // 2

    pieces = cut(grad_held[0], [(half * span_rows + first, size) for half, first, size in chunks])
    grads = [from_behind(pieces[0], "section", -1)]
    pair = jnp.concatenate(lax.optimization_barrier((keys, values, pieces[0]))[:2], axis=0)
    gathered, codes, step = pair, [0], count // 2
    while step:
        held, gathered = gathered, with_partner(gathered, "ctx", step)
        codes = codes + [code ^ step for code in codes]
        if step > 1:
            gathered = jnp.concatenate([held, gathered], axis=0)
        step //= 2
    for piece, gate in zip(pieces[1:], [None] * (len(pieces) - 2) + [pair]):
        if gate is not None:
            piece, _ = lax.optimization_barrier((piece, gate))
        grads.append(from_behind(piece, "section", -1))
    sorted_keys = sort_keys(span_start, [held, gathered], codes, span_rows, head_size)

    q_flat = queries.reshape(row_count * heads, head_size)
    o_flat = outputs.reshape(row_count * heads, head_size)
    lse_flat = lse[0].T.reshape(1, row_count * heads)

    span_wide = (span_rows, 2 * head_size)
    running, received, dq_parts = [], [], []
    for number, chunk in enumerate(chunks):
        half, _, tokens = chunk
        rows = tokens * heads
        is_first, is_last = number == 0, number == len(chunks) - 1
        hands_out = number % per_half == per_half - 1
        after = received[:2] if is_last else []
        if is_last:
            upper_terms = received
        grad = grads[number].reshape(rows, head_size)
        if is_first:
            grad = widen(grad, o_flat, (half * span_rows + chunk[1]) * heads)
        operands = [
            q_flat, grad, o_flat, lse_flat, *sorted_keys, *after,
            *running,
        ]
        total_shape = (total if half else total // 2, 2 * head_size)
        out_shape = [jax.ShapeDtypeStruct((head_size, rows), jnp.float32)]
        if not is_last:
            out_shape.append(jax.ShapeDtypeStruct(total_shape, jnp.float32))
        if hands_out:
            out_shape.append(jax.ShapeDtypeStruct(span_wide, jnp.float32))
            out_shape += [jax.ShapeDtypeStruct(span_wide, jnp.bfloat16)] * (count - 1)
        pairs = rows * (3 * total // 4 if half == 1 else total // 4)
        dq, *handed = pl.pallas_call(
            functools.partial(
                chunk_kernel, chunk, heads, span_rows, count, is_first, is_last, hands_out,
                len(after),
            ),
            out_shape=out_shape,
            in_specs=[SCALARS] + [WHOLE] * len(operands),
            out_specs=[WHOLE] * len(out_shape),
            scratch_shapes=[pltpu.VMEM(total_shape, jnp.float32)] if is_last else [],
            compiler_params=params(),
            cost_estimate=pl.CostEstimate(
                flops=20 * pairs * head_size, bytes_accessed=2 * 2**20, transcendentals=pairs
            ),
        )(span_start, *operands)
        dq_parts.append(dq)
        running = [] if is_last else [handed.pop(0)]
        if hands_out:
            received = [handed[0]] + [
                with_partner(send, "ctx", step) for step, send in enumerate(handed[1:], start=1)
            ]

    places = [(half * span_rows + first) * heads for half, first, _ in chunks]
    upper_sum, dq = finish(upper_terms, dq_parts, places, q_flat.shape)
    key_out, value_out = pl.pallas_call(
        functools.partial(add_kernel, count, span_rows, head_size),
        out_shape=(jax.ShapeDtypeStruct((row_count, head_size), jnp.bfloat16),) * 2,
        in_specs=[WHOLE] * (count + 1),
        out_specs=(WHOLE,) * 2,
        compiler_params=params(),
    )(*received, upper_sum)
    return (dq.reshape(queries.shape), key_out[None], value_out[None])


def solution(mesh):
    placed = (
        P("section", "ctx", None, None),
        P("section", "ctx", None),
        P("section", "ctx", None),
        P("section", "ctx", None, None),
        P("section", "ctx", None, None),
        P("section", None, "ctx"),
        P(),
    )
    return jax.shard_map(
        body,
        mesh=mesh,
        in_specs=placed,
        out_specs=(
            P("section", "ctx", None, None),
            P("section", "ctx", None),
            P("section", "ctx", None),
        ),
        check_vma=False,
    )
```

```python
import functools
import math

import jax
import jax.numpy as jnp
from jax import lax
from jax.experimental import pallas as pl
from jax.experimental.pallas import tpu as pltpu
from jax.sharding import PartitionSpec as P

KEY_BLOCK = 256
UPPER_CHUNKS = (64, 64)
LOWER_CHUNKS = (96, 32)
VMEM_LIMIT = 40 * 1024 * 1024
SORT_FLOPS = 10**9
WIDEN_FLOPS = 4 * 10**9

WHOLE = pl.BlockSpec(memory_space=pltpu.VMEM)
SCALARS = pl.BlockSpec(memory_space=pltpu.SMEM)
ANYWHERE = pl.BlockSpec(memory_space=pl.ANY)
NT = (((1,), (1,)), ((), ()))


def from_behind(shard, axis, by):
    length = lax.axis_size(axis)
    return lax.ppermute(shard, axis, [(i, (i + by) % length) for i in range(length)])


def with_partner(shard, axis, step):
    length = lax.axis_size(axis)
    return lax.ppermute(shard, axis, [(i, i ^ step) for i in range(length)])


def params(limit=VMEM_LIMIT):
    return pltpu.CompilerParams(vmem_limit_bytes=limit)


def cut_kernel(cuts, source_ref, *refs):
    *out_refs, sems = refs
    copies = [
        pltpu.make_async_copy(source_ref.at[pl.ds(first, size)], out_ref, sems.at[i])
        for i, ((first, size), out_ref) in enumerate(zip(cuts, out_refs))
    ]
    for copy in copies:
        copy.start()
    for copy in copies:
        copy.wait()


def cut(source, cuts):
    return pl.pallas_call(
        functools.partial(cut_kernel, cuts),
        out_shape=[
            jax.ShapeDtypeStruct((size, *source.shape[1:]), source.dtype) for _, size in cuts
        ],
        in_specs=[ANYWHERE],
        out_specs=[ANYWHERE] * len(cuts),
        scratch_shapes=[pltpu.SemaphoreType.DMA((len(cuts),))],
        compiler_params=params(),
        cost_estimate=pl.CostEstimate(
            flops=0, bytes_accessed=2 * source.size * source.dtype.itemsize, transcendentals=0
        ),
    )(source)


def widen_kernel(rows, g_ref, o_ref, *refs):
    wide_ref = refs[-1]
    head_size = g_ref.shape[1]
    g = g_ref[...]
    wide_ref[:, :head_size] = g
    wide_ref[:, head_size:] = times(g, o_ref[rows, :])


def widen(grad, outputs, first, *others):
    row_count, head_size = grad.shape
    return pl.pallas_call(
        functools.partial(widen_kernel, slice(first, first + row_count)),
        out_shape=jax.ShapeDtypeStruct((row_count, 2 * head_size), grad.dtype),
        in_specs=[WHOLE] * (2 + len(others)),
        out_specs=WHOLE,
        compiler_params=params(),
        cost_estimate=pl.CostEstimate(
            flops=WIDEN_FLOPS, bytes_accessed=grad.size * 8, transcendentals=0
        ),
    )(grad, outputs, *others)


def times(g, o):
    return (g.astype(jnp.float32) * o.astype(jnp.float32)).astype(jnp.bfloat16)


def stack_kernel(*refs):
    *part_refs, out_ref = refs
    first = 0
    for part_ref in part_refs:
        out_ref[first : first + part_ref.shape[0]] = part_ref[...]
        first += part_ref.shape[0]


def stack(parts):
    shape = (sum(part.shape[0] for part in parts), *parts[0].shape[1:])
    return pl.pallas_call(
        stack_kernel,
        out_shape=jax.ShapeDtypeStruct(shape, parts[0].dtype),
        in_specs=[WHOLE] * len(parts),
        out_specs=WHOLE,
        compiler_params=params(),
        cost_estimate=pl.CostEstimate(flops=0, bytes_accessed=2**18, transcendentals=0),
    )(*parts)


def sort_keys_kernel(codes, span_rows, head_size, starts_ref, *refs):
    held_ref, got_ref, keys_ref, values_ref, keys_t_ref = refs
    half_count = len(codes) // 2
    blocks = [(ref, 2 * i) for ref in (held_ref, got_ref) for i in range(half_count)]
    me = lax.axis_index("ctx")
    values_ref[:, head_size:] = jnp.full(
        (values_ref.shape[0], values_ref.shape[1] - head_size), -1.0, values_ref.dtype
    )
    for (block, at), code in zip(blocks, codes):
        owner = lax.bitwise_xor(me, code)
        for half in range(2):
            start = pl.multiple_of(starts_ref[2 * owner + half], span_rows)
            rows = pl.ds(start, span_rows)
            part = slice(half * span_rows, (half + 1) * span_rows)
            keys = block[at, part, :]
            keys_ref[rows, :] = keys
            values_ref[rows, :head_size] = block[at + 1, part, :]
            keys_t_ref[:, rows] = keys.astype(jnp.float32).T.astype(jnp.bfloat16)


def sort_keys(span_start, blocks, codes, span_rows, head_size):
    total = len(codes) * 2 * span_rows
    return pl.pallas_call(
        functools.partial(sort_keys_kernel, codes, span_rows, head_size),
        out_shape=(
            jax.ShapeDtypeStruct((total, head_size), jnp.bfloat16),
            jax.ShapeDtypeStruct((total, 2 * head_size), jnp.bfloat16),
            jax.ShapeDtypeStruct((head_size, total), jnp.bfloat16),
        ),
        in_specs=[SCALARS] + [WHOLE] * len(blocks),
        out_specs=(WHOLE,) * 3,
        compiler_params=params(),
        cost_estimate=pl.CostEstimate(
            flops=SORT_FLOPS, bytes_accessed=8 * total * head_size, transcendentals=0
        ),
    )(span_start, *blocks)


def chunk_grads(
    chunk, heads, span_rows, starts_ref, q_ref, g_ref, o_ref, lse_ref, keys_ref, values_ref,
    keys_t_ref, total_ref, dq_ref,
):
    half, first, tokens = chunk
    head_size = q_ref.shape[1]
    scale = head_size**-0.5
    to_log2 = math.log2(math.e)
    me = lax.axis_index("ctx")
    start = starts_ref[2 * me + half]
    row_count = tokens * heads
    row_first = (half * span_rows + first) * heads
    rows = slice(row_first, row_first + row_count)
    full_blocks = start // KEY_BLOCK

    q = q_ref[rows, :]
    g = g_ref[...]
    if g.shape[1] == head_size:
        g_wide = jnp.concatenate([g, times(g, o_ref[rows, :])], axis=1)
    else:
        g, g_wide = g[:, :head_size], g
    lse2 = lse_ref[0:1, rows] * to_log2
    dq_ref[...] = jnp.zeros_like(dq_ref)

    def block(index, masked):
        base = pl.multiple_of(index * KEY_BLOCK, KEY_BLOCK)
        at = pl.ds(base, KEY_BLOCK)
        scores = lax.dot_general(keys_ref[at, :], q, NT, preferred_element_type=jnp.float32)
        probs = jnp.exp2(scores * (scale * to_log2) - lse2)
        if masked:
            query_row = lax.broadcasted_iota(jnp.int32, (1, row_count), 1)
            query_pos = start + first + query_row // heads
            key_pos = base + lax.broadcasted_iota(jnp.int32, (KEY_BLOCK, 1), 0)
            probs = jnp.where(key_pos <= query_pos, probs, 0.0)
        centred = lax.dot_general(values_ref[at, :], g_wide, NT, preferred_element_type=jnp.float32)
        grad_scores = (probs * centred).astype(jnp.bfloat16)
        probs_low = probs.astype(jnp.bfloat16)
        total_ref[at, :head_size] += jnp.dot(grad_scores, q, preferred_element_type=jnp.float32)
        total_ref[at, head_size:] += jnp.dot(probs_low, g, preferred_element_type=jnp.float32)
        dq_ref[...] += jnp.dot(keys_t_ref[:, at], grad_scores, preferred_element_type=jnp.float32)

    def dense(index, carry):
        block(index, False)
        return carry

    lax.fori_loop(0, full_blocks, dense, 0)
    block(full_blocks, True)


def hand_out(half, count, span_rows, starts_ref, total_ref, own_ref, send_refs):
    head_size = total_ref.shape[1] // 2
    scale = head_size**-0.5
    me = lax.axis_index("ctx")
    for step in range(count):
        owner = lax.bitwise_xor(me, step)
        start = pl.multiple_of(starts_ref[2 * owner + half], span_rows)
        rows = pl.ds(start, span_rows)
        target = own_ref if step == 0 else send_refs[step - 1]
        target[:, :head_size] = (total_ref[rows, :head_size] * scale).astype(target.dtype)
        target[:, head_size:] = total_ref[rows, head_size:].astype(target.dtype)


def add_terms(term_refs):
    total = term_refs[0][...]
    for term_ref in term_refs[1:]:
        total = total + term_ref[...].astype(jnp.float32)
    return total


def chunk_kernel(
    chunk, heads, span_rows, count, is_first, is_last, hands_out, n_after, starts_ref, q_ref, g_ref, o_ref,
    lse_ref, keys_ref, values_ref, keys_t_ref, *refs,
):
    refs = list(refs[n_after:])
    total_in = None if is_first else refs.pop(0)
    total_ref = refs.pop() if is_last else refs.pop(1)
    dq_ref, *handed = refs
    if is_first:
        total_ref[...] = jnp.zeros_like(total_ref)
    else:
        total_ref[...] = total_in[: total_ref.shape[0], :]
    chunk_grads(
        chunk, heads, span_rows, starts_ref, q_ref, g_ref, o_ref, lse_ref, keys_ref, values_ref,
        keys_t_ref, total_ref, dq_ref,
    )
    if hands_out:
        hand_out(chunk[0], count, span_rows, starts_ref, total_ref, handed[0], handed[1:])


def add_kernel(count, span_rows, head_size, *refs):
    term_refs, upper_ref, (key_ref, value_ref) = refs[:count], refs[count], refs[count + 1 :]
    lower = add_terms(term_refs).astype(jnp.bfloat16)
    for out_ref, columns in ((key_ref, slice(0, head_size)), (value_ref, slice(head_size, None))):
        out_ref[:span_rows, :] = lower[:, columns]
        out_ref[span_rows:, :] = upper_ref[:, columns]


def finish_kernel(count, places, *refs):
    term_refs, refs = refs[:count], refs[count:]
    part_refs, (upper_ref, out_ref, held, sems) = refs[: len(places)], refs[len(places) :]
    scale = out_ref.shape[1] ** -0.5
    copies = []
    for i, (first, part_ref) in enumerate(zip(places, part_refs)):
        rows = pl.ds(first, part_ref.shape[1])
        held[rows, :] = (part_ref[...] * scale).T.astype(jnp.bfloat16)
        copies.append(pltpu.make_async_copy(held.at[rows], out_ref.at[rows], sems.at[i]))
        copies[-1].start()
    upper_ref[...] = add_terms(term_refs).astype(jnp.bfloat16)
    for copy in copies:
        copy.wait()


def finish(terms, parts, places, shape):
    return pl.pallas_call(
        functools.partial(finish_kernel, len(terms), places),
        out_shape=(
            jax.ShapeDtypeStruct(terms[0].shape, jnp.bfloat16),
            jax.ShapeDtypeStruct(shape, jnp.bfloat16),
        ),
        in_specs=[WHOLE] * (len(terms) + len(parts)),
        out_specs=(WHOLE, ANYWHERE),
        scratch_shapes=[
            pltpu.VMEM(shape, jnp.bfloat16),
            pltpu.SemaphoreType.DMA((len(parts),)),
        ],
        compiler_params=params(),
    )(*terms, *parts)


def body(queries, keys, values, outputs, grad_held, lse, span_start):
    count = lax.axis_size("ctx")
    row_count, heads, head_size = queries.shape[1:]
    span_rows = row_count // 2
    total = count * row_count
    chunks = []
    for half, sizes in ((1, UPPER_CHUNKS), (0, LOWER_CHUNKS)):
        chunks += [(half, sum(sizes[:i]), size) for i, size in enumerate(sizes)]

    pieces = cut(grad_held[0], [(half * span_rows + first, size) for half, first, size in chunks])
    grads = [from_behind(pieces[0], "section", -1)]
    pair = jnp.concatenate(lax.optimization_barrier((keys, values, pieces[0]))[:2], axis=0)
    gathered, codes, step = pair, [0], count // 2
    while step:
        held, gathered = gathered, with_partner(gathered, "ctx", step)
        codes = codes + [code ^ step for code in codes]
        if step > 1:
            gathered = stack([held, gathered])
        step //= 2
    for piece, gate in zip(pieces[1:], [None] * (len(pieces) - 2) + [held]):
        if gate is not None:
            piece, _ = lax.optimization_barrier((piece, gate))
        grads.append(from_behind(piece, "section", -1))
    sorted_keys = sort_keys(span_start, [held, gathered], codes, span_rows, head_size)

    q_flat = queries.reshape(row_count * heads, head_size)
    o_flat = outputs.reshape(row_count * heads, head_size)
    lse_flat = lse[0].T.reshape(1, row_count * heads)

    span_wide = (span_rows, 2 * head_size)
    running, received, dq_parts = [], [], []
    for number, chunk in enumerate(chunks):
        half, _, tokens = chunk
        rows = tokens * heads
        is_first, is_last = number == 0, number == len(chunks) - 1
        hands_out = chunk[1] + tokens == span_rows
        after = received[:2] if is_last else []
        if is_last:
            upper_terms = received
        grad = grads[number].reshape(rows, head_size)
        if is_first:
            grad = widen(grad, o_flat, (half * span_rows + chunk[1]) * heads)
        operands = [
            q_flat, grad, o_flat, lse_flat, *sorted_keys, *after,
            *running,
        ]
        total_shape = (total if half else total // 2, 2 * head_size)
        out_shape = [jax.ShapeDtypeStruct((head_size, rows), jnp.float32)]
        if not is_last:
            out_shape.append(jax.ShapeDtypeStruct(total_shape, jnp.float32))
        if hands_out:
            out_shape.append(jax.ShapeDtypeStruct(span_wide, jnp.float32))
            out_shape += [jax.ShapeDtypeStruct(span_wide, jnp.bfloat16)] * (count - 1)
        pairs = rows * (3 * total // 4 if half == 1 else total // 4)
        dq, *handed = pl.pallas_call(
            functools.partial(
                chunk_kernel, chunk, heads, span_rows, count, is_first, is_last, hands_out,
                len(after),
            ),
            out_shape=out_shape,
            in_specs=[SCALARS] + [WHOLE] * len(operands),
            out_specs=[WHOLE] * len(out_shape),
            scratch_shapes=[pltpu.VMEM(total_shape, jnp.float32)] if is_last else [],
            compiler_params=params(),
            cost_estimate=pl.CostEstimate(
                flops=20 * pairs * head_size, bytes_accessed=2 * 2**20, transcendentals=pairs
            ),
        )(span_start, *operands)
        dq_parts.append(dq)
        running = [] if is_last else [handed.pop(0)]
        if hands_out:
            sends = list(enumerate(handed[1:], start=1))
            received = [with_partner(send, "ctx", step) for step, send in reversed(sends)]
            received = [handed[0]] + received[::-1]

    places = [(half * span_rows + first) * heads for half, first, _ in chunks]
    upper_sum, dq = finish(upper_terms, dq_parts, places, q_flat.shape)
    key_out, value_out = pl.pallas_call(
        functools.partial(add_kernel, count, span_rows, head_size),
        out_shape=(jax.ShapeDtypeStruct((row_count, head_size), jnp.bfloat16),) * 2,
        in_specs=[WHOLE] * (count + 1),
        out_specs=(WHOLE,) * 2,
        compiler_params=params(),
    )(*received, upper_sum)
    return (dq.reshape(queries.shape), key_out[None], value_out[None])


def solution(mesh):
    placed = (
        P("section", "ctx", None, None),
        P("section", "ctx", None),
        P("section", "ctx", None),
        P("section", "ctx", None, None),
        P("section", "ctx", None, None),
        P("section", None, "ctx"),
        P(),
    )
    return jax.shard_map(
        body,
        mesh=mesh,
        in_specs=placed,
        out_specs=(
            P("section", "ctx", None, None),
            P("section", "ctx", None),
            P("section", "ctx", None),
        ),
        check_vma=False,
    )
```

```python
import functools
import math

import jax
import jax.numpy as jnp
from jax import lax
from jax.experimental import pallas as pl
from jax.experimental.pallas import tpu as pltpu
from jax.sharding import PartitionSpec as P

KEY_BLOCK = 256
VMEM_BASE = 16 * 1024 * 1024
VMEM_PER_KEY = 8 * 1024
PROBS_TILE = 1024
UPPER_CHUNKS = (64, 64)
LOWER_CHUNKS = (96, 32)
SORT_FLOPS = 10**9
WIDEN_FLOPS = 4 * 10**9

WHOLE = pl.BlockSpec(memory_space=pltpu.VMEM)
SCALARS = pl.BlockSpec(memory_space=pltpu.SMEM)
ANYWHERE = pl.BlockSpec(memory_space=pl.ANY)
NT = (((1,), (1,)), ((), ()))


def from_behind(shard, axis, by):
    length = lax.axis_size(axis)
    return lax.ppermute(shard, axis, [(i, (i + by) % length) for i in range(length)])


def with_partner(shard, axis, step):
    length = lax.axis_size(axis)
    return lax.ppermute(shard, axis, [(i, i ^ step) for i in range(length)])


def params(key_count=1024):
    return pltpu.CompilerParams(vmem_limit_bytes=VMEM_BASE + VMEM_PER_KEY * key_count)


def cut_kernel(cuts, source_ref, *refs):
    *out_refs, sems = refs
    copies = [
        pltpu.make_async_copy(source_ref.at[pl.ds(first, size)], out_ref, sems.at[i])
        for i, ((first, size), out_ref) in enumerate(zip(cuts, out_refs))
    ]
    for copy in copies:
        copy.start()
    for copy in copies:
        copy.wait()


def cut(source, cuts):
    return pl.pallas_call(
        functools.partial(cut_kernel, cuts),
        out_shape=[
            jax.ShapeDtypeStruct((size, *source.shape[1:]), source.dtype) for _, size in cuts
        ],
        in_specs=[ANYWHERE],
        out_specs=[ANYWHERE] * len(cuts),
        scratch_shapes=[pltpu.SemaphoreType.DMA((len(cuts),))],
        compiler_params=params(),
        cost_estimate=pl.CostEstimate(
            flops=0, bytes_accessed=2 * source.size * source.dtype.itemsize, transcendentals=0
        ),
    )(source)


def widen_kernel(rows, g_ref, o_ref, *refs):
    wide_ref = refs[-1]
    head_size = g_ref.shape[1]
    g = g_ref[...]
    wide_ref[:, :head_size] = g
    wide_ref[:, head_size:] = times(g, o_ref[rows, :])


def widen(grad, outputs, first, *others):
    row_count, head_size = grad.shape
    return pl.pallas_call(
        functools.partial(widen_kernel, slice(first, first + row_count)),
        out_shape=jax.ShapeDtypeStruct((row_count, 2 * head_size), grad.dtype),
        in_specs=[WHOLE] * (2 + len(others)),
        out_specs=WHOLE,
        compiler_params=params(),
        cost_estimate=pl.CostEstimate(
            flops=WIDEN_FLOPS, bytes_accessed=grad.size * 8, transcendentals=0
        ),
    )(grad, outputs, *others)


def times(g, o):
    return (g.astype(jnp.float32) * o.astype(jnp.float32)).astype(jnp.bfloat16)


def stack_kernel(*refs):
    *part_refs, out_ref = refs
    first = 0
    for part_ref in part_refs:
        out_ref[first : first + part_ref.shape[0]] = part_ref[...]
        first += part_ref.shape[0]


def stack(parts):
    shape = (sum(part.shape[0] for part in parts), *parts[0].shape[1:])
    return pl.pallas_call(
        stack_kernel,
        out_shape=jax.ShapeDtypeStruct(shape, parts[0].dtype),
        in_specs=[WHOLE] * len(parts),
        out_specs=WHOLE,
        compiler_params=params(),
        cost_estimate=pl.CostEstimate(flops=0, bytes_accessed=2**18, transcendentals=0),
    )(*parts)


def sort_keys_kernel(codes, span_rows, head_size, starts_ref, *refs):
    held_ref, got_ref, keys_ref, values_ref, keys_t_ref = refs
    half_count = len(codes) // 2
    blocks = [(ref, 2 * i) for ref in (held_ref, got_ref) for i in range(half_count)]
    me = lax.axis_index("ctx")
    values_ref[:, head_size:] = jnp.full(
        (values_ref.shape[0], values_ref.shape[1] - head_size), -1.0, values_ref.dtype
    )
    for (block, at), code in zip(blocks, codes):
        owner = lax.bitwise_xor(me, code)
        for half in range(2):
            start = pl.multiple_of(starts_ref[2 * owner + half], span_rows)
            rows = pl.ds(start, span_rows)
            part = slice(half * span_rows, (half + 1) * span_rows)
            keys = block[at, part, :]
            keys_ref[rows, :] = keys
            values_ref[rows, :head_size] = block[at + 1, part, :]
            keys_t_ref[:, rows] = keys.astype(jnp.float32).T.astype(jnp.bfloat16)


def sort_keys(span_start, blocks, codes, span_rows, head_size):
    total = len(codes) * 2 * span_rows
    return pl.pallas_call(
        functools.partial(sort_keys_kernel, codes, span_rows, head_size),
        out_shape=(
            jax.ShapeDtypeStruct((total, head_size), jnp.bfloat16),
            jax.ShapeDtypeStruct((total, 2 * head_size), jnp.bfloat16),
            jax.ShapeDtypeStruct((head_size, total), jnp.bfloat16),
        ),
        in_specs=[SCALARS] + [WHOLE] * len(blocks),
        out_specs=(WHOLE,) * 3,
        compiler_params=params(),
        cost_estimate=pl.CostEstimate(
            flops=SORT_FLOPS, bytes_accessed=8 * total * head_size, transcendentals=0
        ),
    )(span_start, *blocks)


def scaled_probs(q, keys, lse2, positions=None):
    head_size = q.shape[1]
    to_log2 = math.log2(math.e)
    scores = lax.dot_general(keys, q, NT, preferred_element_type=jnp.float32)
    probs = jnp.exp2(scores * (head_size**-0.5 * to_log2) - lse2)
    if positions is not None:
        query_first, key_first, heads = positions
        query_row = lax.broadcasted_iota(jnp.int32, (1, q.shape[0]), 1)
        key_row = lax.broadcasted_iota(jnp.int32, (keys.shape[0], 1), 0)
        probs = jnp.where(key_first + key_row <= query_first + query_row // heads, probs, 0.0)
    return probs


def over_key_blocks(start, block):
    full_blocks = start // KEY_BLOCK

    def dense(index, carry):
        block(pl.multiple_of(index * KEY_BLOCK, KEY_BLOCK), False)
        return carry

    lax.fori_loop(0, full_blocks, dense, 0)
    block(pl.multiple_of(full_blocks * KEY_BLOCK, KEY_BLOCK), True)


def probs_kernel(half, heads, span_rows, tile, starts_ref, q_ref, lse_ref, keys_ref, *refs):
    probs_ref = refs[-1]
    start = starts_ref[2 * lax.axis_index("ctx") + half]
    row_first = half * span_rows * heads

    def block(base, masked):
        at = pl.ds(base, KEY_BLOCK)
        for first in range(0, span_rows * heads, tile):
            rows = slice(row_first + first, row_first + first + tile)
            probs_ref[at, first : first + tile] = scaled_probs(
                q_ref[rows, :],
                keys_ref[at, :],
                lse_ref[0:1, rows] * math.log2(math.e),
                (start + first // heads, base, heads) if masked else None,
            )

    over_key_blocks(start, block)


def span_probs(span_start, q_flat, lse_flat, sorted_keys, after, heads, key_count):
    rows_span = q_flat.shape[0] // 2
    return pl.pallas_call(
        functools.partial(probs_kernel, 0, heads, rows_span // heads, min(PROBS_TILE, rows_span)),
        out_shape=jax.ShapeDtypeStruct((key_count, rows_span), jnp.float32),
        in_specs=[SCALARS] + [WHOLE] * 3 + [ANYWHERE],
        out_specs=WHOLE,
        compiler_params=params(2 * key_count),
        cost_estimate=pl.CostEstimate(
            flops=4 * rows_span * key_count * q_flat.shape[1],
            bytes_accessed=4 * rows_span * key_count,
            transcendentals=rows_span * key_count,
        ),
    )(span_start, q_flat, lse_flat, sorted_keys, after)


def chunk_grads(
    chunk, heads, span_rows, starts_ref, q_ref, g_ref, o_ref, lse_ref, keys_ref, values_ref,
    keys_t_ref, probs_ref, total_ref, dq_ref,
):
    half, first, tokens = chunk
    head_size = q_ref.shape[1]
    start = starts_ref[2 * lax.axis_index("ctx") + half]
    row_count = tokens * heads
    row_first = (half * span_rows + first) * heads
    rows = slice(row_first, row_first + row_count)

    q = q_ref[rows, :]
    g = g_ref[...]
    if g.shape[1] == head_size:
        g_wide = jnp.concatenate([g, times(g, o_ref[rows, :])], axis=1)
    else:
        g, g_wide = g[:, :head_size], g
    lse2 = lse_ref[0:1, rows] * math.log2(math.e)
    dq_ref[...] = jnp.zeros_like(dq_ref)

    def block(base, masked):
        at = pl.ds(base, KEY_BLOCK)
        if probs_ref is None:
            positions = (start + first, base, heads) if masked else None
            probs = scaled_probs(q, keys_ref[at, :], lse2, positions)
        else:
            probs = probs_ref[at, first * heads : first * heads + row_count]
        centred = lax.dot_general(values_ref[at, :], g_wide, NT, preferred_element_type=jnp.float32)
        grad_scores = (probs * centred).astype(jnp.bfloat16)
        probs_low = probs.astype(jnp.bfloat16)
        total_ref[at, :head_size] += jnp.dot(grad_scores, q, preferred_element_type=jnp.float32)
        total_ref[at, head_size:] += jnp.dot(probs_low, g, preferred_element_type=jnp.float32)
        dq_ref[...] += jnp.dot(keys_t_ref[:, at], grad_scores, preferred_element_type=jnp.float32)

    over_key_blocks(start, block)


def hand_out(half, count, span_rows, starts_ref, total_ref, own_ref, send_refs):
    head_size = total_ref.shape[1] // 2
    scale = head_size**-0.5
    me = lax.axis_index("ctx")
    for step in range(count):
        owner = lax.bitwise_xor(me, step)
        start = pl.multiple_of(starts_ref[2 * owner + half], span_rows)
        rows = pl.ds(start, span_rows)
        target = own_ref if step == 0 else send_refs[step - 1]
        target[:, :head_size] = (total_ref[rows, :head_size] * scale).astype(target.dtype)
        target[:, head_size:] = total_ref[rows, head_size:].astype(target.dtype)


def add_terms(term_refs):
    total = term_refs[0][...]
    for term_ref in term_refs[1:]:
        total = total + term_ref[...].astype(jnp.float32)
    return total


def chunk_kernel(
    chunk, heads, span_rows, count, is_first, is_last, hands_out, n_after, starts_ref, q_ref, g_ref, o_ref,
    lse_ref, keys_ref, values_ref, keys_t_ref, *refs,
):
    refs = list(refs[n_after:])
    probs_ref = None if chunk[0] else refs.pop(0)
    total_in = None if is_first else refs.pop(0)
    total_ref = refs.pop() if is_last else refs.pop(1)
    dq_ref, *handed = refs
    if is_first:
        total_ref[...] = jnp.zeros_like(total_ref)
    else:
        total_ref[...] = total_in[: total_ref.shape[0], :]
    chunk_grads(
        chunk, heads, span_rows, starts_ref, q_ref, g_ref, o_ref, lse_ref, keys_ref, values_ref,
        keys_t_ref, probs_ref, total_ref, dq_ref,
    )
    if hands_out:
        hand_out(chunk[0], count, span_rows, starts_ref, total_ref, handed[0], handed[1:])


def add_kernel(count, span_rows, head_size, *refs):
    term_refs, upper_ref, (key_ref, value_ref) = refs[:count], refs[count], refs[count + 1 :]
    lower = add_terms(term_refs).astype(jnp.bfloat16)
    for out_ref, columns in ((key_ref, slice(0, head_size)), (value_ref, slice(head_size, None))):
        out_ref[:span_rows, :] = lower[:, columns]
        out_ref[span_rows:, :] = upper_ref[:, columns]


def finish_kernel(count, places, *refs):
    term_refs, refs = refs[:count], refs[count:]
    part_refs, (upper_ref, out_ref, held, sems) = refs[: len(places)], refs[len(places) :]
    scale = out_ref.shape[1] ** -0.5
    copies = []
    for i, (first, part_ref) in enumerate(zip(places, part_refs)):
        rows = pl.ds(first, part_ref.shape[1])
        held[rows, :] = (part_ref[...] * scale).T.astype(jnp.bfloat16)
        copies.append(pltpu.make_async_copy(held.at[rows], out_ref.at[rows], sems.at[i]))
        copies[-1].start()
    upper_ref[...] = add_terms(term_refs).astype(jnp.bfloat16)
    for copy in copies:
        copy.wait()


def finish(terms, parts, places, shape):
    return pl.pallas_call(
        functools.partial(finish_kernel, len(terms), places),
        out_shape=(
            jax.ShapeDtypeStruct(terms[0].shape, jnp.bfloat16),
            jax.ShapeDtypeStruct(shape, jnp.bfloat16),
        ),
        in_specs=[WHOLE] * (len(terms) + len(parts)),
        out_specs=(WHOLE, ANYWHERE),
        scratch_shapes=[
            pltpu.VMEM(shape, jnp.bfloat16),
            pltpu.SemaphoreType.DMA((len(parts),)),
        ],
        compiler_params=params(),
    )(*terms, *parts)


def body(queries, keys, values, outputs, grad_held, lse, span_start):
    count = lax.axis_size("ctx")
    row_count, heads, head_size = queries.shape[1:]
    span_rows = row_count // 2
    total = count * row_count
    chunks = []
    for half, sizes in ((1, UPPER_CHUNKS), (0, LOWER_CHUNKS)):
        chunks += [(half, sum(sizes[:i]), size) for i, size in enumerate(sizes)]

    pieces = cut(grad_held[0], [(half * span_rows + first, size) for half, first, size in chunks])
    grads = [from_behind(pieces[0], "section", -1)]
    pair = jnp.concatenate(lax.optimization_barrier((keys, values, pieces[0]))[:2], axis=0)
    gathered, codes, step = pair, [0], count // 2
    while step:
        held, gathered = gathered, with_partner(gathered, "ctx", step)
        codes = codes + [code ^ step for code in codes]
        if step > 1:
            gathered = stack([held, gathered])
        step //= 2
    for piece, gate in zip(pieces[1:], [None] * (len(pieces) - 2) + [held]):
        if gate is not None:
            piece, _ = lax.optimization_barrier((piece, gate))
        grads.append(from_behind(piece, "section", -1))
    sorted_keys = sort_keys(span_start, [held, gathered], codes, span_rows, head_size)

    q_flat = queries.reshape(row_count * heads, head_size)
    o_flat = outputs.reshape(row_count * heads, head_size)
    lse_flat = lse[0].T.reshape(1, row_count * heads)

    span_wide = (span_rows, 2 * head_size)
    running, received, dq_parts, probs = [], [], [], []
    for number, chunk in enumerate(chunks):
        half, _, tokens = chunk
        rows = tokens * heads
        is_first, is_last = number == 0, number == len(chunks) - 1
        hands_out = chunk[1] + tokens == span_rows
        after = received[:2] if is_last else []
        if is_last:
            upper_terms = received
        grad = grads[number].reshape(rows, head_size)
        if is_first:
            grad = widen(grad, o_flat, (half * span_rows + chunk[1]) * heads)
        if half == 0 and not probs:
            probs = [span_probs(span_start, q_flat, lse_flat, sorted_keys[0], running[0], heads, total // 2)]
        operands = [
            q_flat, grad, o_flat, lse_flat, *sorted_keys, *after,
            *probs, *running,
        ]
        total_shape = (total if half else total // 2, 2 * head_size)
        out_shape = [jax.ShapeDtypeStruct((head_size, rows), jnp.float32)]
        if not is_last:
            out_shape.append(jax.ShapeDtypeStruct(total_shape, jnp.float32))
        if hands_out:
            out_shape.append(jax.ShapeDtypeStruct(span_wide, jnp.float32))
            out_shape += [jax.ShapeDtypeStruct(span_wide, jnp.bfloat16)] * (count - 1)
        pairs = rows * (3 * total // 4 if half == 1 else total // 4)
        dq, *handed = pl.pallas_call(
            functools.partial(
                chunk_kernel, chunk, heads, span_rows, count, is_first, is_last, hands_out,
                len(after),
            ),
            out_shape=out_shape,
            in_specs=[SCALARS] + [WHOLE] * len(operands),
            out_specs=[WHOLE] * len(out_shape),
            scratch_shapes=[pltpu.VMEM(total_shape, jnp.float32)] if is_last else [],
            compiler_params=params(total),
            cost_estimate=pl.CostEstimate(
                flops=20 * pairs * head_size, bytes_accessed=2 * 2**20, transcendentals=pairs
            ),
        )(span_start, *operands)
        dq_parts.append(dq)
        running = [] if is_last else [handed.pop(0)]
        if hands_out:
            sends = list(enumerate(handed[1:], start=1))
            received = [with_partner(send, "ctx", step) for step, send in reversed(sends)]
            received = [handed[0]] + received[::-1]

    places = [(half * span_rows + first) * heads for half, first, _ in chunks]
    upper_sum, dq = finish(upper_terms, dq_parts, places, q_flat.shape)
    key_out, value_out = pl.pallas_call(
        functools.partial(add_kernel, count, span_rows, head_size),
        out_shape=(jax.ShapeDtypeStruct((row_count, head_size), jnp.bfloat16),) * 2,
        in_specs=[WHOLE] * (count + 1),
        out_specs=(WHOLE,) * 2,
        compiler_params=params(),
    )(*received, upper_sum)
    return (dq.reshape(queries.shape), key_out[None], value_out[None])


def solution(mesh):
    placed = (
        P("section", "ctx", None, None),
        P("section", "ctx", None),
        P("section", "ctx", None),
        P("section", "ctx", None, None),
        P("section", "ctx", None, None),
        P("section", None, "ctx"),
        P(),
    )
    return jax.shard_map(
        body,
        mesh=mesh,
        in_specs=placed,
        out_specs=(
            P("section", "ctx", None, None),
            P("section", "ctx", None),
            P("section", "ctx", None),
        ),
        check_vma=False,
    )
```

```python
import functools
import math

import jax
import jax.numpy as jnp
from jax import lax
from jax.experimental import pallas as pl
from jax.experimental.pallas import tpu as pltpu
from jax.sharding import PartitionSpec as P

KEY_BLOCK = 512
LANES = 128
UPPER_CHUNKS = (64, 64)
LOWER_CHUNKS = (80, 48)
VMEM_LIMIT = 40 * 1024 * 1024
SORT_FLOPS = 10**9
WIDEN_FLOPS = 4 * 10**9

WHOLE = pl.BlockSpec(memory_space=pltpu.VMEM)
SCALARS = pl.BlockSpec(memory_space=pltpu.SMEM)
ANYWHERE = pl.BlockSpec(memory_space=pl.ANY)
NT = (((1,), (1,)), ((), ()))


def from_behind(shard, axis, by):
    length = lax.axis_size(axis)
    return lax.ppermute(shard, axis, [(i, (i + by) % length) for i in range(length)])


def with_partner(shard, axis, step):
    length = lax.axis_size(axis)
    return lax.ppermute(shard, axis, [(i, i ^ step) for i in range(length)])


def params(limit=VMEM_LIMIT):
    return pltpu.CompilerParams(vmem_limit_bytes=limit)


def cut_kernel(cuts, source_ref, *refs):
    *out_refs, sems = refs
    copies = [
        pltpu.make_async_copy(source_ref.at[pl.ds(first, size)], out_ref, sems.at[i])
        for i, ((first, size), out_ref) in enumerate(zip(cuts, out_refs))
    ]
    for copy in copies:
        copy.start()
    for copy in copies:
        copy.wait()


def cut(source, cuts):
    return pl.pallas_call(
        functools.partial(cut_kernel, cuts),
        out_shape=[
            jax.ShapeDtypeStruct((size, *source.shape[1:]), source.dtype) for _, size in cuts
        ],
        in_specs=[ANYWHERE],
        out_specs=[ANYWHERE] * len(cuts),
        scratch_shapes=[pltpu.SemaphoreType.DMA((len(cuts),))],
        compiler_params=params(),
        cost_estimate=pl.CostEstimate(
            flops=0, bytes_accessed=2 * source.size * source.dtype.itemsize, transcendentals=0
        ),
    )(source)


def widen_kernel(rows, g_ref, o_ref, *refs):
    wide_ref = refs[-1]
    head_size = g_ref.shape[1]
    g = g_ref[...]
    wide_ref[:, :head_size] = g
    wide_ref[:, head_size:] = times(g, o_ref[rows, :])


def widen(grad, outputs, first, *others):
    row_count, head_size = grad.shape
    return pl.pallas_call(
        functools.partial(widen_kernel, slice(first, first + row_count)),
        out_shape=jax.ShapeDtypeStruct((row_count, 2 * head_size), grad.dtype),
        in_specs=[WHOLE] * (2 + len(others)),
        out_specs=WHOLE,
        compiler_params=params(),
        cost_estimate=pl.CostEstimate(
            flops=WIDEN_FLOPS, bytes_accessed=grad.size * 8, transcendentals=0
        ),
    )(grad, outputs, *others)


def times(g, o):
    return (g.astype(jnp.float32) * o.astype(jnp.float32)).astype(jnp.bfloat16)


def stack_kernel(*refs):
    *part_refs, out_ref = refs
    first = 0
    for part_ref in part_refs:
        out_ref[first : first + part_ref.shape[0]] = part_ref[...]
        first += part_ref.shape[0]


def stack(parts):
    shape = (sum(part.shape[0] for part in parts), *parts[0].shape[1:])
    return pl.pallas_call(
        stack_kernel,
        out_shape=jax.ShapeDtypeStruct(shape, parts[0].dtype),
        in_specs=[WHOLE] * len(parts),
        out_specs=WHOLE,
        compiler_params=params(),
        cost_estimate=pl.CostEstimate(flops=0, bytes_accessed=2**18, transcendentals=0),
    )(*parts)


def place_of(places_ref, step, half):
    lane = lax.broadcasted_iota(jnp.int32, places_ref.shape, 1)
    place = jnp.max(jnp.where(lane == 2 * step + half, places_ref[...], 0.0))
    return pl.multiple_of(place.astype(jnp.int32), LANES)


def sort_keys_kernel(codes, span_rows, head_size, starts_ref, *refs):
    held_ref, got_ref, keys_ref, values_ref, keys_t_ref, places_ref = refs
    half_count = len(codes) // 2
    blocks = [(ref, 2 * i) for ref in (held_ref, got_ref) for i in range(half_count)]
    me = lax.axis_index("ctx")
    lane = lax.broadcasted_iota(jnp.int32, places_ref.shape, 1)
    places = jnp.zeros(places_ref.shape, jnp.float32)
    values_ref[:, head_size:] = jnp.full(
        (values_ref.shape[0], values_ref.shape[1] - head_size), -1.0, values_ref.dtype
    )
    for (block, at), code in zip(blocks, codes):
        owner = lax.bitwise_xor(me, code)
        for half in range(2):
            start = pl.multiple_of(starts_ref[2 * owner + half], span_rows)
            rows = pl.ds(start, span_rows)
            part = slice(half * span_rows, (half + 1) * span_rows)
            keys = block[at, part, :]
            keys_ref[rows, :] = keys
            values_ref[rows, :head_size] = block[at + 1, part, :]
            keys_t_ref[:, rows] = keys.astype(jnp.float32).T.astype(jnp.bfloat16)
            places = jnp.where(lane == 2 * code + half, start.astype(jnp.float32), places)
    places_ref[...] = places


def sort_keys(span_start, blocks, codes, span_rows, head_size):
    total = len(codes) * 2 * span_rows
    return pl.pallas_call(
        functools.partial(sort_keys_kernel, codes, span_rows, head_size),
        out_shape=(
            jax.ShapeDtypeStruct((total, head_size), jnp.bfloat16),
            jax.ShapeDtypeStruct((total, 2 * head_size), jnp.bfloat16),
            jax.ShapeDtypeStruct((head_size, total), jnp.bfloat16),
            jax.ShapeDtypeStruct((8, LANES), jnp.float32),
        ),
        in_specs=[SCALARS] + [WHOLE] * len(blocks),
        out_specs=(WHOLE,) * 4,
        compiler_params=params(),
        cost_estimate=pl.CostEstimate(
            flops=SORT_FLOPS, bytes_accessed=8 * total * head_size, transcendentals=0
        ),
    )(span_start, *blocks)


def chunk_grads(
    chunk, heads, span_rows, places_ref, q_ref, g_ref, o_ref, lse_ref, keys_ref, values_ref,
    keys_t_ref, total_ref, dq_ref,
):
    half, first, tokens = chunk
    head_size = q_ref.shape[1]
    scale = head_size**-0.5
    to_log2 = math.log2(math.e)
    start = place_of(places_ref, 0, half)
    row_count = tokens * heads
    row_first = (half * span_rows + first) * heads
    rows = slice(row_first, row_first + row_count)
    full_blocks = start // KEY_BLOCK

    q = q_ref[rows, :]
    g = g_ref[...]
    if g.shape[1] == head_size:
        g_wide = jnp.concatenate([g, times(g, o_ref[rows, :])], axis=1)
    else:
        g, g_wide = g[:, :head_size], g
    lse2 = lse_ref[0:1, rows] * to_log2
    dq_ref[...] = jnp.zeros_like(dq_ref)

    def block(base, size, masked):
        base = pl.multiple_of(base, KEY_BLOCK)
        at = pl.ds(base, size)
        scores = lax.dot_general(keys_ref[at, :], q, NT, preferred_element_type=jnp.float32)
        probs = jnp.exp2(scores * (scale * to_log2) - lse2)
        if masked:
            query_row = lax.broadcasted_iota(jnp.int32, (1, row_count), 1)
            query_pos = start + first + query_row // heads
            key_pos = base + lax.broadcasted_iota(jnp.int32, (size, 1), 0)
            probs = jnp.where(key_pos <= query_pos, probs, 0.0)
        centred = lax.dot_general(values_ref[at, :], g_wide, NT, preferred_element_type=jnp.float32)
        grad_scores = (probs * centred).astype(jnp.bfloat16)
        probs_low = probs.astype(jnp.bfloat16)
        total_ref[at, :head_size] += jnp.dot(grad_scores, q, preferred_element_type=jnp.float32)
        total_ref[at, head_size:] += jnp.dot(probs_low, g, preferred_element_type=jnp.float32)
        dq_ref[...] += jnp.dot(keys_t_ref[:, at], grad_scores, preferred_element_type=jnp.float32)

    def dense(index, carry):
        block(index * KEY_BLOCK, KEY_BLOCK, False)
        return carry

    lax.fori_loop(0, full_blocks, dense, 0)
    last = full_blocks * KEY_BLOCK
    short = start - last < KEY_BLOCK // 2

    @pl.when(short)
    def _():
        block(last, KEY_BLOCK // 2, True)

    @pl.when(jnp.logical_not(short))
    def _():
        block(last, KEY_BLOCK, True)


def hand_out(half, count, span_rows, places_ref, total_ref, own_ref, send_refs):
    head_size = total_ref.shape[1] // 2
    scale = head_size**-0.5
    for step, target in enumerate([own_ref, *send_refs]):
        rows = pl.ds(place_of(places_ref, step, half), span_rows)
        target[:, :head_size] = (total_ref[rows, :head_size] * scale).astype(target.dtype)
        target[:, head_size:] = total_ref[rows, head_size:].astype(target.dtype)


def add_terms(term_refs):
    total = term_refs[0][...]
    for term_ref in term_refs[1:]:
        total = total + term_ref[...].astype(jnp.float32)
    return total


def chunk_kernel(
    chunk, heads, span_rows, count, is_first, is_last, hands_out, n_after, q_ref, g_ref, o_ref,
    lse_ref, keys_ref, values_ref, keys_t_ref, places_ref, *refs,
):
    refs = list(refs[n_after:])
    total_in = None if is_first else refs.pop(0)
    total_ref = refs.pop() if is_last else refs.pop(1)
    dq_ref, *handed = refs
    if is_first:
        total_ref[...] = jnp.zeros_like(total_ref)
    else:
        total_ref[...] = total_in[: total_ref.shape[0], :]
    chunk_grads(
        chunk, heads, span_rows, places_ref, q_ref, g_ref, o_ref, lse_ref, keys_ref, values_ref,
        keys_t_ref, total_ref, dq_ref,
    )
    if hands_out:
        hand_out(chunk[0], count, span_rows, places_ref, total_ref, handed[0], handed[1:])


def add_kernel(count, span_rows, head_size, *refs):
    term_refs, upper_ref, (key_ref, value_ref) = refs[:count], refs[count], refs[count + 1 :]
    lower = add_terms(term_refs).astype(jnp.bfloat16)
    for out_ref, columns in ((key_ref, slice(0, head_size)), (value_ref, slice(head_size, None))):
        out_ref[:span_rows, :] = lower[:, columns]
        out_ref[span_rows:, :] = upper_ref[:, columns]


def finish_kernel(count, places, *refs):
    term_refs, refs = refs[:count], refs[count:]
    part_refs, (upper_ref, out_ref, held, sems) = refs[: len(places)], refs[len(places) :]
    scale = out_ref.shape[1] ** -0.5
    copies = []
    for i, (first, part_ref) in enumerate(zip(places, part_refs)):
        rows = pl.ds(first, part_ref.shape[1])
        held[rows, :] = (part_ref[...] * scale).T.astype(jnp.bfloat16)
        copies.append(pltpu.make_async_copy(held.at[rows], out_ref.at[rows], sems.at[i]))
        copies[-1].start()
    upper_ref[...] = add_terms(term_refs).astype(jnp.bfloat16)
    for copy in copies:
        copy.wait()


def finish(terms, parts, places, shape):
    return pl.pallas_call(
        functools.partial(finish_kernel, len(terms), places),
        out_shape=(
            jax.ShapeDtypeStruct(terms[0].shape, jnp.bfloat16),
            jax.ShapeDtypeStruct(shape, jnp.bfloat16),
        ),
        in_specs=[WHOLE] * (len(terms) + len(parts)),
        out_specs=(WHOLE, ANYWHERE),
        scratch_shapes=[
            pltpu.VMEM(shape, jnp.bfloat16),
            pltpu.SemaphoreType.DMA((len(parts),)),
        ],
        compiler_params=params(),
    )(*terms, *parts)


def body(queries, keys, values, outputs, grad_held, lse, span_start):
    count = lax.axis_size("ctx")
    row_count, heads, head_size = queries.shape[1:]
    span_rows = row_count // 2
    total = count * row_count
    chunks = []
    for half, sizes in ((1, UPPER_CHUNKS), (0, LOWER_CHUNKS)):
        chunks += [(half, sum(sizes[:i]), size) for i, size in enumerate(sizes)]

    pieces = cut(grad_held[0], [(half * span_rows + first, size) for half, first, size in chunks])
    grads = [from_behind(pieces[0], "section", -1)]
    pair = jnp.concatenate(lax.optimization_barrier((keys, values, pieces[0]))[:2], axis=0)
    gathered, codes, step = pair, [0], count // 2
    while step:
        held, gathered = gathered, with_partner(gathered, "ctx", step)
        codes = codes + [code ^ step for code in codes]
        if step > 1:
            gathered = stack([held, gathered])
        step //= 2
    for piece, gate in zip(pieces[1:], [None] * (len(pieces) - 2) + [held]):
        if gate is not None:
            piece, _ = lax.optimization_barrier((piece, gate))
        grads.append(from_behind(piece, "section", -1))
    sorted_keys = sort_keys(span_start, [held, gathered], codes, span_rows, head_size)

    q_flat = queries.reshape(row_count * heads, head_size)
    o_flat = outputs.reshape(row_count * heads, head_size)
    lse_flat = lse[0].T.reshape(1, row_count * heads)

    span_wide = (span_rows, 2 * head_size)
    running, received, dq_parts = [], [], []
    for number, chunk in enumerate(chunks):
        half, _, tokens = chunk
        rows = tokens * heads
        is_first, is_last = number == 0, number == len(chunks) - 1
        hands_out = chunk[1] + tokens == span_rows
        after = received[:2] if is_last else []
        if is_last:
            upper_terms = received
        grad = grads[number].reshape(rows, head_size)
        if is_first:
            grad = widen(grad, o_flat, (half * span_rows + chunk[1]) * heads)
        operands = [
            q_flat, grad, o_flat, lse_flat, *sorted_keys, *after,
            *running,
        ]
        total_shape = (total if half else total // 2, 2 * head_size)
        out_shape = [jax.ShapeDtypeStruct((head_size, rows), jnp.float32)]
        if not is_last:
            out_shape.append(jax.ShapeDtypeStruct(total_shape, jnp.float32))
        if hands_out:
            out_shape.append(jax.ShapeDtypeStruct(span_wide, jnp.float32))
            out_shape += [jax.ShapeDtypeStruct(span_wide, jnp.bfloat16)] * (count - 1)
        pairs = rows * (3 * total // 4 if half == 1 else total // 4)
        dq, *handed = pl.pallas_call(
            functools.partial(
                chunk_kernel, chunk, heads, span_rows, count, is_first, is_last, hands_out,
                len(after),
            ),
            out_shape=out_shape,
            in_specs=[WHOLE] * len(operands),
            out_specs=[WHOLE] * len(out_shape),
            scratch_shapes=[pltpu.VMEM(total_shape, jnp.float32)] if is_last else [],
            compiler_params=params(),
            cost_estimate=pl.CostEstimate(
                flops=20 * pairs * head_size, bytes_accessed=2 * 2**20, transcendentals=pairs
            ),
        )(*operands)
        dq_parts.append(dq)
        running = [] if is_last else [handed.pop(0)]
        if hands_out:
            sends = list(enumerate(handed[1:], start=1))
            received = [with_partner(send, "ctx", step) for step, send in reversed(sends)]
            received = [handed[0]] + received[::-1]

    places = [(half * span_rows + first) * heads for half, first, _ in chunks]
    upper_sum, dq = finish(upper_terms, dq_parts, places, q_flat.shape)
    key_out, value_out = pl.pallas_call(
        functools.partial(add_kernel, count, span_rows, head_size),
        out_shape=(jax.ShapeDtypeStruct((row_count, head_size), jnp.bfloat16),) * 2,
        in_specs=[WHOLE] * (count + 1),
        out_specs=(WHOLE,) * 2,
        compiler_params=params(),
    )(*received, upper_sum)
    return (dq.reshape(queries.shape), key_out[None], value_out[None])


def solution(mesh):
    placed = (
        P("section", "ctx", None, None),
        P("section", "ctx", None),
        P("section", "ctx", None),
        P("section", "ctx", None, None),
        P("section", "ctx", None, None),
        P("section", None, "ctx"),
        P(),
    )
    return jax.shard_map(
        body,
        mesh=mesh,
        in_specs=placed,
        out_specs=(
            P("section", "ctx", None, None),
            P("section", "ctx", None),
            P("section", "ctx", None),
        ),
        check_vma=False,
    )
```

```python
import functools
import math

import jax
import jax.numpy as jnp
from jax import lax
from jax.experimental import pallas as pl
from jax.experimental.pallas import tpu as pltpu
from jax.sharding import PartitionSpec as P

KEY_BLOCK = 512
LANES = 128
TILE_TOKENS = 64
UPPER_CHUNKS = (128,)
LOWER_CHUNKS = (80, 48)
VMEM_LIMIT = 40 * 1024 * 1024
SORT_FLOPS = 10**9
WIDEN_FLOPS = 4 * 10**9

WHOLE = pl.BlockSpec(memory_space=pltpu.VMEM)
SCALARS = pl.BlockSpec(memory_space=pltpu.SMEM)
ANYWHERE = pl.BlockSpec(memory_space=pl.ANY)
NT = (((1,), (1,)), ((), ()))


def from_behind(shard, axis, by):
    length = lax.axis_size(axis)
    return lax.ppermute(shard, axis, [(i, (i + by) % length) for i in range(length)])


def with_partner(shard, axis, step):
    length = lax.axis_size(axis)
    return lax.ppermute(shard, axis, [(i, i ^ step) for i in range(length)])


def params(limit=VMEM_LIMIT):
    return pltpu.CompilerParams(vmem_limit_bytes=limit)


def cut_kernel(cuts, source_ref, *refs):
    *out_refs, sems = refs
    copies = [
        pltpu.make_async_copy(source_ref.at[pl.ds(first, size)], out_ref, sems.at[i])
        for i, ((first, size), out_ref) in enumerate(zip(cuts, out_refs))
    ]
    for copy in copies:
        copy.start()
    for copy in copies:
        copy.wait()


def cut(source, cuts):
    return pl.pallas_call(
        functools.partial(cut_kernel, cuts),
        out_shape=[
            jax.ShapeDtypeStruct((size, *source.shape[1:]), source.dtype) for _, size in cuts
        ],
        in_specs=[ANYWHERE],
        out_specs=[ANYWHERE] * len(cuts),
        scratch_shapes=[pltpu.SemaphoreType.DMA((len(cuts),))],
        compiler_params=params(),
        cost_estimate=pl.CostEstimate(
            flops=0, bytes_accessed=2 * source.size * source.dtype.itemsize, transcendentals=0
        ),
    )(source)


def widen_kernel(rows, g_ref, o_ref, *refs):
    wide_ref = refs[-1]
    head_size = g_ref.shape[1]
    g = g_ref[...]
    wide_ref[:, :head_size] = g
    wide_ref[:, head_size:] = times(g, o_ref[rows, :])


def widen(grad, outputs, first, *others):
    row_count, head_size = grad.shape
    return pl.pallas_call(
        functools.partial(widen_kernel, slice(first, first + row_count)),
        out_shape=jax.ShapeDtypeStruct((row_count, 2 * head_size), grad.dtype),
        in_specs=[WHOLE] * (2 + len(others)),
        out_specs=WHOLE,
        compiler_params=params(),
        cost_estimate=pl.CostEstimate(
            flops=WIDEN_FLOPS, bytes_accessed=grad.size * 8, transcendentals=0
        ),
    )(grad, outputs, *others)


def times(g, o):
    return (g.astype(jnp.float32) * o.astype(jnp.float32)).astype(jnp.bfloat16)


def stack_kernel(*refs):
    *part_refs, out_ref = refs
    first = 0
    for part_ref in part_refs:
        out_ref[first : first + part_ref.shape[0]] = part_ref[...]
        first += part_ref.shape[0]


def stack(parts):
    shape = (sum(part.shape[0] for part in parts), *parts[0].shape[1:])
    return pl.pallas_call(
        stack_kernel,
        out_shape=jax.ShapeDtypeStruct(shape, parts[0].dtype),
        in_specs=[WHOLE] * len(parts),
        out_specs=WHOLE,
        compiler_params=params(),
        cost_estimate=pl.CostEstimate(flops=0, bytes_accessed=2**18, transcendentals=0),
    )(*parts)


def place_of(places_ref, step, half):
    lane = lax.broadcasted_iota(jnp.int32, places_ref.shape, 1)
    place = jnp.max(jnp.where(lane == 2 * step + half, places_ref[...], 0.0))
    return pl.multiple_of(place.astype(jnp.int32), LANES)


def sort_keys_kernel(codes, span_rows, head_size, starts_ref, *refs):
    held_ref, got_ref, _, keys_ref, values_ref, keys_t_ref, places_ref = refs
    half_count = len(codes) // 2
    blocks = [(ref, 2 * i) for ref in (held_ref, got_ref) for i in range(half_count)]
    me = lax.axis_index("ctx")
    lane = lax.broadcasted_iota(jnp.int32, places_ref.shape, 1)
    places = jnp.zeros(places_ref.shape, jnp.float32)
    values_ref[:, head_size:] = jnp.full(
        (values_ref.shape[0], values_ref.shape[1] - head_size), -1.0, values_ref.dtype
    )
    for (block, at), code in zip(blocks, codes):
        owner = lax.bitwise_xor(me, code)
        for half in range(2):
            start = pl.multiple_of(starts_ref[2 * owner + half], span_rows)
            rows = pl.ds(start, span_rows)
            part = slice(half * span_rows, (half + 1) * span_rows)
            keys = block[at, part, :]
            keys_ref[rows, :] = keys
            values_ref[rows, :head_size] = block[at + 1, part, :]
            keys_t_ref[:, rows] = keys.astype(jnp.float32).T.astype(jnp.bfloat16)
            places = jnp.where(lane == 2 * code + half, start.astype(jnp.float32), places)
    places_ref[...] = places


def sort_keys(span_start, blocks, fetched, codes, span_rows, head_size):
    total = len(codes) * 2 * span_rows
    return pl.pallas_call(
        functools.partial(sort_keys_kernel, codes, span_rows, head_size),
        out_shape=(
            jax.ShapeDtypeStruct((total, head_size), jnp.bfloat16),
            jax.ShapeDtypeStruct((total, 2 * head_size), jnp.bfloat16),
            jax.ShapeDtypeStruct((head_size, total), jnp.bfloat16),
            jax.ShapeDtypeStruct((8, LANES), jnp.float32),
        ),
        in_specs=[SCALARS] + [WHOLE] * (len(blocks) + 1),
        out_specs=(WHOLE,) * 4,
        compiler_params=params(),
        cost_estimate=pl.CostEstimate(
            flops=SORT_FLOPS, bytes_accessed=8 * total * head_size, transcendentals=0
        ),
    )(span_start, *blocks, fetched)


def tile_grads(
    part, heads, span_rows, places_ref, q_ref, g_ref, o_ref, lse_ref, keys_ref, values_ref,
    keys_t_ref, total_ref, dq_ref,
):
    half, first, tokens = part
    head_size = q_ref.shape[1]
    scale = head_size**-0.5
    to_log2 = math.log2(math.e)
    start = place_of(places_ref, 0, half)
    row_count = tokens * heads
    row_first = (half * span_rows + first) * heads
    rows = slice(row_first, row_first + row_count)
    full_blocks = start // KEY_BLOCK

    q = q_ref[rows, :]
    g = g_ref[...]
    if g.shape[1] == head_size:
        g_wide = jnp.concatenate([g, times(g, o_ref[rows, :])], axis=1)
    else:
        g, g_wide = g[:, :head_size], g
    lse2 = lse_ref[0:1, rows] * to_log2
    dq_ref[...] = jnp.zeros_like(dq_ref)

    def block(base, size, masked):
        base = pl.multiple_of(base, KEY_BLOCK)
        at = pl.ds(base, size)
        scores = lax.dot_general(keys_ref[at, :], q, NT, preferred_element_type=jnp.float32)
        probs = jnp.exp2(scores * (scale * to_log2) - lse2)
        if masked:
            query_row = lax.broadcasted_iota(jnp.int32, (1, row_count), 1)
            query_pos = start + first + query_row // heads
            key_pos = base + lax.broadcasted_iota(jnp.int32, (size, 1), 0)
            probs = jnp.where(key_pos <= query_pos, probs, 0.0)
        centred = lax.dot_general(values_ref[at, :], g_wide, NT, preferred_element_type=jnp.float32)
        grad_scores = (probs * centred).astype(jnp.bfloat16)
        probs_low = probs.astype(jnp.bfloat16)
        total_ref[at, :head_size] += jnp.dot(grad_scores, q, preferred_element_type=jnp.float32)
        total_ref[at, head_size:] += jnp.dot(probs_low, g, preferred_element_type=jnp.float32)
        dq_ref[...] += jnp.dot(keys_t_ref[:, at], grad_scores, preferred_element_type=jnp.float32)

    def dense(index, carry):
        block(index * KEY_BLOCK, KEY_BLOCK, False)
        return carry

    lax.fori_loop(0, full_blocks, dense, 0)
    last = full_blocks * KEY_BLOCK
    short = start - last < KEY_BLOCK // 2

    @pl.when(short)
    def _():
        block(last, KEY_BLOCK // 2, True)

    @pl.when(jnp.logical_not(short))
    def _():
        block(last, KEY_BLOCK, True)


def hand_out(half, count, span_rows, places_ref, total_ref, own_ref, send_refs):
    head_size = total_ref.shape[1] // 2
    scale = head_size**-0.5
    for step, target in enumerate([own_ref, *send_refs]):
        rows = pl.ds(place_of(places_ref, step, half), span_rows)
        target[:, :head_size] = (total_ref[rows, :head_size] * scale).astype(target.dtype)
        target[:, head_size:] = total_ref[rows, head_size:].astype(target.dtype)


def add_terms(term_refs):
    total = term_refs[0][...]
    for term_ref in term_refs[1:]:
        total = total + term_ref[...].astype(jnp.float32)
    return total


def chunk_kernel(
    chunk, heads, span_rows, count, is_first, is_last, hands_out, n_after, q_ref, g_ref, o_ref,
    lse_ref, keys_ref, values_ref, keys_t_ref, places_ref, *refs,
):
    refs = list(refs[n_after:])
    total_in = None if is_first else refs.pop(0)
    total_ref = refs.pop() if is_last else refs.pop(1)
    dq_ref, *handed = refs
    if is_first:
        total_ref[...] = jnp.zeros_like(total_ref)
    else:
        total_ref[...] = total_in[: total_ref.shape[0], :]
    half, first, tokens = chunk
    tile = TILE_TOKENS if tokens % TILE_TOKENS == 0 else tokens
    for at in range(0, tokens, tile):
        rows = pl.ds(at * heads, tile * heads)
        tile_grads(
            (half, first + at, tile), heads, span_rows, places_ref, q_ref, g_ref.at[rows], o_ref,
            lse_ref, keys_ref, values_ref, keys_t_ref, total_ref, dq_ref.at[:, rows],
        )
    if hands_out:
        hand_out(chunk[0], count, span_rows, places_ref, total_ref, handed[0], handed[1:])


def add_kernel(count, span_rows, head_size, *refs):
    term_refs, upper_ref, (key_ref, value_ref) = refs[:count], refs[count], refs[count + 1 :]
    lower = add_terms(term_refs).astype(jnp.bfloat16)
    for out_ref, columns in ((key_ref, slice(0, head_size)), (value_ref, slice(head_size, None))):
        out_ref[:span_rows, :] = lower[:, columns]
        out_ref[span_rows:, :] = upper_ref[:, columns]


def finish_kernel(count, places, *refs):
    term_refs, refs = refs[:count], refs[count:]
    part_refs, (upper_ref, out_ref, held, sems) = refs[: len(places)], refs[len(places) :]
    scale = out_ref.shape[1] ** -0.5
    copies = []
    for i, (first, part_ref) in enumerate(zip(places, part_refs)):
        rows = pl.ds(first, part_ref.shape[1])
        held[rows, :] = (part_ref[...] * scale).T.astype(jnp.bfloat16)
        copies.append(pltpu.make_async_copy(held.at[rows], out_ref.at[rows], sems.at[i]))
        copies[-1].start()
    upper_ref[...] = add_terms(term_refs).astype(jnp.bfloat16)
    for copy in copies:
        copy.wait()


def finish(terms, parts, places, shape):
    return pl.pallas_call(
        functools.partial(finish_kernel, len(terms), places),
        out_shape=(
            jax.ShapeDtypeStruct(terms[0].shape, jnp.bfloat16),
            jax.ShapeDtypeStruct(shape, jnp.bfloat16),
        ),
        in_specs=[WHOLE] * (len(terms) + len(parts)),
        out_specs=(WHOLE, ANYWHERE),
        scratch_shapes=[
            pltpu.VMEM(shape, jnp.bfloat16),
            pltpu.SemaphoreType.DMA((len(parts),)),
        ],
        compiler_params=params(),
    )(*terms, *parts)


def body(queries, keys, values, outputs, grad_held, lse, span_start):
    count = lax.axis_size("ctx")
    row_count, heads, head_size = queries.shape[1:]
    span_rows = row_count // 2
    total = count * row_count
    chunks = []
    for half, sizes in ((1, UPPER_CHUNKS), (0, LOWER_CHUNKS)):
        chunks += [(half, sum(sizes[:i]), size) for i, size in enumerate(sizes)]

    pieces = cut(grad_held[0], [(half * span_rows + first, size) for half, first, size in chunks])
    grads = [from_behind(pieces[0], "section", -1)]
    pair = jnp.concatenate(lax.optimization_barrier((keys, values, pieces[0]))[:2], axis=0)
    gathered, codes, step = pair, [0], count // 2
    while step:
        held, gathered = gathered, with_partner(gathered, "ctx", step)
        codes = codes + [code ^ step for code in codes]
        if step > 1:
            gathered = stack([held, gathered])
        step //= 2
    for piece, gate in zip(pieces[1:], [None] * (len(pieces) - 2) + [held]):
        if gate is not None:
            piece, _ = lax.optimization_barrier((piece, gate))
        grads.append(from_behind(piece, "section", -1))
    q_flat = queries.reshape(row_count * heads, head_size)
    sorted_keys = sort_keys(span_start, [held, gathered], q_flat, codes, span_rows, head_size)

    o_flat = outputs.reshape(row_count * heads, head_size)
    lse_flat = lse[0].T.reshape(1, row_count * heads)

    span_wide = (span_rows, 2 * head_size)
    running, received, dq_parts = [], [], []
    for number, chunk in enumerate(chunks):
        half, _, tokens = chunk
        rows = tokens * heads
        is_first, is_last = number == 0, number == len(chunks) - 1
        hands_out = chunk[1] + tokens == span_rows
        after = received[:2] if is_last else []
        if is_last:
            upper_terms = received
        grad = grads[number].reshape(rows, head_size)
        if is_first:
            grad = widen(grad, o_flat, (half * span_rows + chunk[1]) * heads)
        operands = [
            q_flat, grad, o_flat, lse_flat, *sorted_keys, *after,
            *running,
        ]
        total_shape = (total if half else total // 2, 2 * head_size)
        out_shape = [jax.ShapeDtypeStruct((head_size, rows), jnp.float32)]
        if not is_last:
            out_shape.append(jax.ShapeDtypeStruct(total_shape, jnp.float32))
        if hands_out:
            out_shape.append(jax.ShapeDtypeStruct(span_wide, jnp.float32))
            out_shape += [jax.ShapeDtypeStruct(span_wide, jnp.bfloat16)] * (count - 1)
        pairs = rows * (3 * total // 4 if half == 1 else total // 4)
        dq, *handed = pl.pallas_call(
            functools.partial(
                chunk_kernel, chunk, heads, span_rows, count, is_first, is_last, hands_out,
                len(after),
            ),
            out_shape=out_shape,
            in_specs=[WHOLE] * len(operands),
            out_specs=[WHOLE] * len(out_shape),
            scratch_shapes=[pltpu.VMEM(total_shape, jnp.float32)] if is_last else [],
            compiler_params=params(),
            cost_estimate=pl.CostEstimate(
                flops=20 * pairs * head_size, bytes_accessed=2 * 2**20, transcendentals=pairs
            ),
        )(*operands)
        dq_parts.append(dq)
        running = [] if is_last else [handed.pop(0)]
        if hands_out:
            sends = list(enumerate(handed[1:], start=1))
            received = [with_partner(send, "ctx", step) for step, send in reversed(sends)]
            received = [handed[0]] + received[::-1]

    places = [(half * span_rows + first) * heads for half, first, _ in chunks]
    upper_sum, dq = finish(upper_terms, dq_parts, places, q_flat.shape)
    key_out, value_out = pl.pallas_call(
        functools.partial(add_kernel, count, span_rows, head_size),
        out_shape=(jax.ShapeDtypeStruct((row_count, head_size), jnp.bfloat16),) * 2,
        in_specs=[WHOLE] * (count + 1),
        out_specs=(WHOLE,) * 2,
        compiler_params=params(),
    )(*received, upper_sum)
    return (dq.reshape(queries.shape), key_out[None], value_out[None])


def solution(mesh):
    placed = (
        P("section", "ctx", None, None),
        P("section", "ctx", None),
        P("section", "ctx", None),
        P("section", "ctx", None, None),
        P("section", "ctx", None, None),
        P("section", None, "ctx"),
        P(),
    )
    return jax.shard_map(
        body,
        mesh=mesh,
        in_specs=placed,
        out_specs=(
            P("section", "ctx", None, None),
            P("section", "ctx", None),
            P("section", "ctx", None),
        ),
        check_vma=False,
    )
```

```python
import functools
import math

import jax
import jax.numpy as jnp
from jax import lax
from jax.experimental import pallas as pl
from jax.experimental.pallas import tpu as pltpu
from jax.sharding import PartitionSpec as P

KEY_BLOCK = 512
LANES = 128
UPPER_CHUNKS = (80, 48)
LOWER_CHUNKS = (80, 48)
VMEM_LIMIT = 40 * 1024 * 1024
SORT_FLOPS = 10**9
WIDEN_FLOPS = 4 * 10**9

WHOLE = pl.BlockSpec(memory_space=pltpu.VMEM)
SCALARS = pl.BlockSpec(memory_space=pltpu.SMEM)
ANYWHERE = pl.BlockSpec(memory_space=pl.ANY)
NT = (((1,), (1,)), ((), ()))


def from_behind(shard, axis, by):
    length = lax.axis_size(axis)
    return lax.ppermute(shard, axis, [(i, (i + by) % length) for i in range(length)])


def with_partner(shard, axis, step):
    length = lax.axis_size(axis)
    return lax.ppermute(shard, axis, [(i, i ^ step) for i in range(length)])


def params(limit=VMEM_LIMIT):
    return pltpu.CompilerParams(vmem_limit_bytes=limit)


def cut_kernel(cuts, source_ref, *refs):
    *out_refs, sems = refs
    copies = [
        pltpu.make_async_copy(source_ref.at[pl.ds(first, size)], out_ref, sems.at[i])
        for i, ((first, size), out_ref) in enumerate(zip(cuts, out_refs))
    ]
    for copy in copies:
        copy.start()
    for copy in copies:
        copy.wait()


def cut(source, cuts):
    return pl.pallas_call(
        functools.partial(cut_kernel, cuts),
        out_shape=[
            jax.ShapeDtypeStruct((size, *source.shape[1:]), source.dtype) for _, size in cuts
        ],
        in_specs=[ANYWHERE],
        out_specs=[ANYWHERE] * len(cuts),
        scratch_shapes=[pltpu.SemaphoreType.DMA((len(cuts),))],
        compiler_params=params(),
        cost_estimate=pl.CostEstimate(
            flops=0, bytes_accessed=2 * source.size * source.dtype.itemsize, transcendentals=0
        ),
    )(source)


def widen_kernel(rows, g_ref, o_ref, *refs):
    wide_ref = refs[-1]
    head_size = g_ref.shape[1]
    g = g_ref[...]
    wide_ref[:, :head_size] = g
    wide_ref[:, head_size:] = times(g, o_ref[rows, :])


def widen(grad, outputs, first, *others):
    row_count, head_size = grad.shape
    return pl.pallas_call(
        functools.partial(widen_kernel, slice(first, first + row_count)),
        out_shape=jax.ShapeDtypeStruct((row_count, 2 * head_size), grad.dtype),
        in_specs=[WHOLE] * (2 + len(others)),
        out_specs=WHOLE,
        compiler_params=params(),
        cost_estimate=pl.CostEstimate(
            flops=WIDEN_FLOPS, bytes_accessed=grad.size * 8, transcendentals=0
        ),
    )(grad, outputs, *others)


def times(g, o):
    return (g.astype(jnp.float32) * o.astype(jnp.float32)).astype(jnp.bfloat16)


def stack_kernel(*refs):
    *part_refs, out_ref = refs
    first = 0
    for part_ref in part_refs:
        out_ref[first : first + part_ref.shape[0]] = part_ref[...]
        first += part_ref.shape[0]


def stack(parts):
    shape = (sum(part.shape[0] for part in parts), *parts[0].shape[1:])
    return pl.pallas_call(
        stack_kernel,
        out_shape=jax.ShapeDtypeStruct(shape, parts[0].dtype),
        in_specs=[WHOLE] * len(parts),
        out_specs=WHOLE,
        compiler_params=params(),
        cost_estimate=pl.CostEstimate(flops=0, bytes_accessed=2**18, transcendentals=0),
    )(*parts)


def place_of(places_ref, step, half):
    lane = lax.broadcasted_iota(jnp.int32, places_ref.shape, 1)
    place = jnp.max(jnp.where(lane == 2 * step + half, places_ref[...], 0.0))
    return pl.multiple_of(place.astype(jnp.int32), LANES)


def sort_keys_kernel(codes, span_rows, head_size, starts_ref, *refs):
    held_ref, got_ref, keys_ref, values_ref, keys_t_ref, places_ref = refs
    half_count = len(codes) // 2
    blocks = [(ref, 2 * i) for ref in (held_ref, got_ref) for i in range(half_count)]
    me = lax.axis_index("ctx")
    lane = lax.broadcasted_iota(jnp.int32, places_ref.shape, 1)
    places = jnp.zeros(places_ref.shape, jnp.float32)
    values_ref[:, head_size:] = jnp.full(
        (values_ref.shape[0], values_ref.shape[1] - head_size), -1.0, values_ref.dtype
    )
    for (block, at), code in zip(blocks, codes):
        owner = lax.bitwise_xor(me, code)
        for half in range(2):
            start = pl.multiple_of(starts_ref[2 * owner + half], span_rows)
            rows = pl.ds(start, span_rows)
            part = slice(half * span_rows, (half + 1) * span_rows)
            keys = block[at, part, :]
            keys_ref[rows, :] = keys
            values_ref[rows, :head_size] = block[at + 1, part, :]
            keys_t_ref[:, rows] = keys.astype(jnp.float32).T.astype(jnp.bfloat16)
            places = jnp.where(lane == 2 * code + half, start.astype(jnp.float32), places)
    places_ref[...] = places


def sort_keys(span_start, blocks, codes, span_rows, head_size):
    total = len(codes) * 2 * span_rows
    return pl.pallas_call(
        functools.partial(sort_keys_kernel, codes, span_rows, head_size),
        out_shape=(
            jax.ShapeDtypeStruct((total, head_size), jnp.bfloat16),
            jax.ShapeDtypeStruct((total, 2 * head_size), jnp.bfloat16),
            jax.ShapeDtypeStruct((head_size, total), jnp.bfloat16),
            jax.ShapeDtypeStruct((8, LANES), jnp.float32),
        ),
        in_specs=[SCALARS] + [WHOLE] * len(blocks),
        out_specs=(WHOLE,) * 4,
        compiler_params=params(),
        cost_estimate=pl.CostEstimate(
            flops=SORT_FLOPS, bytes_accessed=8 * total * head_size, transcendentals=0
        ),
    )(span_start, *blocks)


def chunk_grads(
    chunk, heads, span_rows, places_ref, q_ref, g_ref, o_ref, lse_ref, keys_ref, values_ref,
    keys_t_ref, total_ref, dq_ref,
):
    half, first, tokens = chunk
    head_size = q_ref.shape[1]
    scale = head_size**-0.5
    to_log2 = math.log2(math.e)
    start = place_of(places_ref, 0, half)
    row_count = tokens * heads
    row_first = (half * span_rows + first) * heads
    rows = slice(row_first, row_first + row_count)
    full_blocks = start // KEY_BLOCK

    q = q_ref[rows, :]
    g = g_ref[...]
    if g.shape[1] == head_size:
        g_wide = jnp.concatenate([g, times(g, o_ref[rows, :])], axis=1)
    else:
        g, g_wide = g[:, :head_size], g
    lse2 = lse_ref[0:1, rows] * to_log2
    dq_ref[...] = jnp.zeros_like(dq_ref)

    def block(base, size, masked):
        base = pl.multiple_of(base, KEY_BLOCK)
        at = pl.ds(base, size)
        scores = lax.dot_general(keys_ref[at, :], q, NT, preferred_element_type=jnp.float32)
        probs = jnp.exp2(scores * (scale * to_log2) - lse2)
        if masked:
            query_row = lax.broadcasted_iota(jnp.int32, (1, row_count), 1)
            query_pos = start + first + query_row // heads
            key_pos = base + lax.broadcasted_iota(jnp.int32, (size, 1), 0)
            probs = jnp.where(key_pos <= query_pos, probs, 0.0)
        centred = lax.dot_general(values_ref[at, :], g_wide, NT, preferred_element_type=jnp.float32)
        grad_scores = (probs * centred).astype(jnp.bfloat16)
        probs_low = probs.astype(jnp.bfloat16)
        total_ref[at, :head_size] += jnp.dot(grad_scores, q, preferred_element_type=jnp.float32)
        total_ref[at, head_size:] += jnp.dot(probs_low, g, preferred_element_type=jnp.float32)
        dq_ref[...] += jnp.dot(keys_t_ref[:, at], grad_scores, preferred_element_type=jnp.float32)

    def dense(index, carry):
        block(index * KEY_BLOCK, KEY_BLOCK, False)
        return carry

    lax.fori_loop(0, full_blocks, dense, 0)
    last = full_blocks * KEY_BLOCK
    short = start - last < KEY_BLOCK // 2

    @pl.when(short)
    def _():
        block(last, KEY_BLOCK // 2, True)

    @pl.when(jnp.logical_not(short))
    def _():
        block(last, KEY_BLOCK, True)


def hand_out(half, count, span_rows, places_ref, total_ref, own_ref, send_refs):
    head_size = total_ref.shape[1] // 2
    scale = head_size**-0.5
    for step, target in enumerate([own_ref, *send_refs]):
        rows = pl.ds(place_of(places_ref, step, half), span_rows)
        target[:, :head_size] = (total_ref[rows, :head_size] * scale).astype(target.dtype)
        target[:, head_size:] = total_ref[rows, head_size:].astype(target.dtype)


def add_terms(term_refs):
    total = term_refs[0][...]
    for term_ref in term_refs[1:]:
        total = total + term_ref[...].astype(jnp.float32)
    return total


def chunk_kernel(
    chunk, heads, span_rows, count, is_first, is_last, hands_out, n_after, q_ref, g_ref, o_ref,
    lse_ref, keys_ref, values_ref, keys_t_ref, places_ref, *refs,
):
    refs = list(refs[n_after:])
    total_in = None if is_first else refs.pop(0)
    total_ref = refs.pop() if is_last else refs.pop(1)
    dq_ref, *handed = refs
    if is_first:
        total_ref[...] = jnp.zeros_like(total_ref)
    else:
        total_ref[...] = total_in[: total_ref.shape[0], :]
    chunk_grads(
        chunk, heads, span_rows, places_ref, q_ref, g_ref, o_ref, lse_ref, keys_ref, values_ref,
        keys_t_ref, total_ref, dq_ref,
    )
    if hands_out:
        hand_out(chunk[0], count, span_rows, places_ref, total_ref, handed[0], handed[1:])


def add_kernel(count, span_rows, head_size, *refs):
    term_refs, upper_ref, (key_ref, value_ref) = refs[:count], refs[count], refs[count + 1 :]
    lower = add_terms(term_refs).astype(jnp.bfloat16)
    for out_ref, columns in ((key_ref, slice(0, head_size)), (value_ref, slice(head_size, None))):
        out_ref[:span_rows, :] = lower[:, columns]
        out_ref[span_rows:, :] = upper_ref[:, columns]


def finish_kernel(count, places, *refs):
    term_refs, refs = refs[:count], refs[count:]
    part_refs, (upper_ref, out_ref, held, sems) = refs[: len(places)], refs[len(places) :]
    scale = out_ref.shape[1] ** -0.5
    copies = []
    for i, (first, part_ref) in enumerate(zip(places, part_refs)):
        rows = pl.ds(first, part_ref.shape[1])
        held[rows, :] = (part_ref[...] * scale).T.astype(jnp.bfloat16)
        copies.append(pltpu.make_async_copy(held.at[rows], out_ref.at[rows], sems.at[i]))
        copies[-1].start()
    upper_ref[...] = add_terms(term_refs).astype(jnp.bfloat16)
    for copy in copies:
        copy.wait()


def finish(terms, parts, places, shape):
    return pl.pallas_call(
        functools.partial(finish_kernel, len(terms), places),
        out_shape=(
            jax.ShapeDtypeStruct(terms[0].shape, jnp.bfloat16),
            jax.ShapeDtypeStruct(shape, jnp.bfloat16),
        ),
        in_specs=[WHOLE] * (len(terms) + len(parts)),
        out_specs=(WHOLE, ANYWHERE),
        scratch_shapes=[
            pltpu.VMEM(shape, jnp.bfloat16),
            pltpu.SemaphoreType.DMA((len(parts),)),
        ],
        compiler_params=params(),
    )(*terms, *parts)


def body(queries, keys, values, outputs, grad_held, lse, span_start):
    count = lax.axis_size("ctx")
    row_count, heads, head_size = queries.shape[1:]
    span_rows = row_count // 2
    total = count * row_count
    chunks = []
    for half, sizes in ((1, UPPER_CHUNKS), (0, LOWER_CHUNKS)):
        chunks += [(half, sum(sizes[:i]), size) for i, size in enumerate(sizes)]

    pieces = cut(grad_held[0], [(half * span_rows + first, size) for half, first, size in chunks])
    grads = [from_behind(pieces[0], "section", -1)]
    pair = jnp.concatenate(lax.optimization_barrier((keys, values, pieces[0]))[:2], axis=0)
    gathered, codes, step = pair, [0], count // 2
    while step:
        held, gathered = gathered, with_partner(gathered, "ctx", step)
        codes = codes + [code ^ step for code in codes]
        if step > 1:
            gathered = stack([held, gathered])
        step //= 2
    for piece, gate in zip(pieces[1:], [None] * (len(pieces) - 2) + [held]):
        if gate is not None:
            piece, _ = lax.optimization_barrier((piece, gate))
        grads.append(from_behind(piece, "section", -1))
    sorted_keys = sort_keys(span_start, [held, gathered], codes, span_rows, head_size)

    q_flat = queries.reshape(row_count * heads, head_size)
    o_flat = outputs.reshape(row_count * heads, head_size)
    lse_flat = lse[0].T.reshape(1, row_count * heads)

    span_wide = (span_rows, 2 * head_size)
    running, received, dq_parts = [], [], []
    for number, chunk in enumerate(chunks):
        half, _, tokens = chunk
        rows = tokens * heads
        is_first, is_last = number == 0, number == len(chunks) - 1
        hands_out = chunk[1] + tokens == span_rows
        after = received[:2] if is_last else []
        if is_last:
            upper_terms = received
        grad = grads[number].reshape(rows, head_size)
        if is_first:
            grad = widen(grad, o_flat, (half * span_rows + chunk[1]) * heads)
        operands = [
            q_flat, grad, o_flat, lse_flat, *sorted_keys, *after,
            *running,
        ]
        total_shape = (total if half else total // 2, 2 * head_size)
        out_shape = [jax.ShapeDtypeStruct((head_size, rows), jnp.float32)]
        if not is_last:
            out_shape.append(jax.ShapeDtypeStruct(total_shape, jnp.float32))
        if hands_out:
            out_shape.append(jax.ShapeDtypeStruct(span_wide, jnp.float32))
            out_shape += [jax.ShapeDtypeStruct(span_wide, jnp.bfloat16)] * (count - 1)
        pairs = rows * (3 * total // 4 if half == 1 else total // 4)
        dq, *handed = pl.pallas_call(
            functools.partial(
                chunk_kernel, chunk, heads, span_rows, count, is_first, is_last, hands_out,
                len(after),
            ),
            out_shape=out_shape,
            in_specs=[WHOLE] * len(operands),
            out_specs=[WHOLE] * len(out_shape),
            scratch_shapes=[pltpu.VMEM(total_shape, jnp.float32)] if is_last else [],
            compiler_params=params(),
            cost_estimate=pl.CostEstimate(
                flops=20 * pairs * head_size, bytes_accessed=2 * 2**20, transcendentals=pairs
            ),
        )(*operands)
        dq_parts.append(dq)
        running = [] if is_last else [handed.pop(0)]
        if hands_out:
            sends = list(enumerate(handed[1:], start=1))
            received = [with_partner(send, "ctx", step) for step, send in reversed(sends)]
            received = [handed[0]] + received[::-1]

    places = [(half * span_rows + first) * heads for half, first, _ in chunks]
    upper_sum, dq = finish(upper_terms, dq_parts, places, q_flat.shape)
    key_out, value_out = pl.pallas_call(
        functools.partial(add_kernel, count, span_rows, head_size),
        out_shape=(jax.ShapeDtypeStruct((row_count, head_size), jnp.bfloat16),) * 2,
        in_specs=[WHOLE] * (count + 1),
        out_specs=(WHOLE,) * 2,
        compiler_params=params(),
    )(*received, upper_sum)
    return (dq.reshape(queries.shape), key_out[None], value_out[None])


def solution(mesh):
    placed = (
        P("section", "ctx", None, None),
        P("section", "ctx", None),
        P("section", "ctx", None),
        P("section", "ctx", None, None),
        P("section", "ctx", None, None),
        P("section", None, "ctx"),
        P(),
    )
    return jax.shard_map(
        body,
        mesh=mesh,
        in_specs=placed,
        out_specs=(
            P("section", "ctx", None, None),
            P("section", "ctx", None),
            P("section", "ctx", None),
        ),
        check_vma=False,
    )
```

```python
import functools
import math

import jax
import jax.numpy as jnp
from jax import lax
from jax.experimental import pallas as pl
from jax.experimental.pallas import tpu as pltpu
from jax.sharding import PartitionSpec as P

KEY_BLOCK = 512
LANES = 128
UPPER_CHUNKS = (64, 64)
LOWER_CHUNKS = (80, 48)
VMEM_LIMIT = 40 * 1024 * 1024
SORT_FLOPS = 10**9
WIDEN_FLOPS = 4 * 10**9

WHOLE = pl.BlockSpec(memory_space=pltpu.VMEM)
SCALARS = pl.BlockSpec(memory_space=pltpu.SMEM)
ANYWHERE = pl.BlockSpec(memory_space=pl.ANY)
NT = (((1,), (1,)), ((), ()))


def from_behind(shard, axis, by):
    length = lax.axis_size(axis)
    return lax.ppermute(shard, axis, [(i, (i + by) % length) for i in range(length)])


def with_partner(shard, axis, step):
    length = lax.axis_size(axis)
    return lax.ppermute(shard, axis, [(i, i ^ step) for i in range(length)])


def params(limit=VMEM_LIMIT):
    return pltpu.CompilerParams(vmem_limit_bytes=limit)


def cut_kernel(cuts, source_ref, *out_refs):
    for (first, size), out_ref in zip(cuts, out_refs):
        out_ref[...] = source_ref[first : first + size]


def cut(source, cuts):
    return pl.pallas_call(
        functools.partial(cut_kernel, cuts),
        out_shape=[
            jax.ShapeDtypeStruct((size, *source.shape[1:]), source.dtype) for _, size in cuts
        ],
        in_specs=[WHOLE],
        out_specs=[WHOLE] * len(cuts),
        compiler_params=params(),
        cost_estimate=pl.CostEstimate(
            flops=0, bytes_accessed=2 * source.size * source.dtype.itemsize, transcendentals=0
        ),
    )(source)


def widen_kernel(rows, g_ref, o_ref, *refs):
    wide_ref = refs[-1]
    head_size = g_ref.shape[1]
    g = g_ref[...]
    wide_ref[:, :head_size] = g
    wide_ref[:, head_size:] = times(g, o_ref[rows, :])


def widen(grad, outputs, first, *others):
    row_count, head_size = grad.shape
    return pl.pallas_call(
        functools.partial(widen_kernel, slice(first, first + row_count)),
        out_shape=jax.ShapeDtypeStruct((row_count, 2 * head_size), grad.dtype),
        in_specs=[WHOLE] * (2 + len(others)),
        out_specs=WHOLE,
        compiler_params=params(),
        cost_estimate=pl.CostEstimate(
            flops=WIDEN_FLOPS, bytes_accessed=grad.size * 8, transcendentals=0
        ),
    )(grad, outputs, *others)


def times(g, o):
    return (g.astype(jnp.float32) * o.astype(jnp.float32)).astype(jnp.bfloat16)


def stack_kernel(*refs):
    *part_refs, out_ref = refs
    first = 0
    for part_ref in part_refs:
        out_ref[first : first + part_ref.shape[0]] = part_ref[...]
        first += part_ref.shape[0]


def stack(parts):
    shape = (sum(part.shape[0] for part in parts), *parts[0].shape[1:])
    return pl.pallas_call(
        stack_kernel,
        out_shape=jax.ShapeDtypeStruct(shape, parts[0].dtype),
        in_specs=[WHOLE] * len(parts),
        out_specs=WHOLE,
        compiler_params=params(),
        cost_estimate=pl.CostEstimate(flops=0, bytes_accessed=2**18, transcendentals=0),
    )(*parts)


def place_of(places_ref, step, half):
    lane = lax.broadcasted_iota(jnp.int32, places_ref.shape, 1)
    place = jnp.max(jnp.where(lane == 2 * step + half, places_ref[...], 0.0))
    return pl.multiple_of(place.astype(jnp.int32), LANES)


def sort_keys_kernel(codes, span_rows, head_size, starts_ref, *refs):
    held_ref, got_ref, keys_ref, values_ref, keys_t_ref, places_ref = refs
    half_count = len(codes) // 2
    blocks = [(ref, 2 * i) for ref in (held_ref, got_ref) for i in range(half_count)]
    me = lax.axis_index("ctx")
    lane = lax.broadcasted_iota(jnp.int32, places_ref.shape, 1)
    places = jnp.zeros(places_ref.shape, jnp.float32)
    values_ref[:, head_size:] = jnp.full(
        (values_ref.shape[0], values_ref.shape[1] - head_size), -1.0, values_ref.dtype
    )
    for (block, at), code in zip(blocks, codes):
        owner = lax.bitwise_xor(me, code)
        for half in range(2):
            start = pl.multiple_of(starts_ref[2 * owner + half], span_rows)
            rows = pl.ds(start, span_rows)
            part = slice(half * span_rows, (half + 1) * span_rows)
            keys = block[at, part, :]
            keys_ref[rows, :] = keys
            values_ref[rows, :head_size] = block[at + 1, part, :]
            keys_t_ref[:, rows] = keys.astype(jnp.float32).T.astype(jnp.bfloat16)
            places = jnp.where(lane == 2 * code + half, start.astype(jnp.float32), places)
    places_ref[...] = places


def sort_keys(span_start, blocks, codes, span_rows, head_size):
    total = len(codes) * 2 * span_rows
    return pl.pallas_call(
        functools.partial(sort_keys_kernel, codes, span_rows, head_size),
        out_shape=(
            jax.ShapeDtypeStruct((total, head_size), jnp.bfloat16),
            jax.ShapeDtypeStruct((total, 2 * head_size), jnp.bfloat16),
            jax.ShapeDtypeStruct((head_size, total), jnp.bfloat16),
            jax.ShapeDtypeStruct((8, LANES), jnp.float32),
        ),
        in_specs=[SCALARS] + [WHOLE] * len(blocks),
        out_specs=(WHOLE,) * 4,
        compiler_params=params(),
        cost_estimate=pl.CostEstimate(
            flops=SORT_FLOPS, bytes_accessed=8 * total * head_size, transcendentals=0
        ),
    )(span_start, *blocks)


def chunk_grads(
    chunk, heads, span_rows, places_ref, q_ref, g_ref, o_ref, lse_ref, keys_ref, values_ref,
    keys_t_ref, total_ref, dq_ref,
):
    half, first, tokens = chunk
    head_size = q_ref.shape[1]
    scale = head_size**-0.5
    to_log2 = math.log2(math.e)
    start = place_of(places_ref, 0, half)
    row_count = tokens * heads
    row_first = (half * span_rows + first) * heads
    rows = slice(row_first, row_first + row_count)
    full_blocks = start // KEY_BLOCK

    q = q_ref[rows, :]
    g = g_ref[...]
    if g.shape[1] == head_size:
        g_wide = jnp.concatenate([g, times(g, o_ref[rows, :])], axis=1)
    else:
        g, g_wide = g[:, :head_size], g
    lse2 = lse_ref[0:1, rows] * to_log2
    dq_ref[...] = jnp.zeros_like(dq_ref)

    def block(base, size, masked):
        base = pl.multiple_of(base, KEY_BLOCK)
        at = pl.ds(base, size)
        scores = lax.dot_general(keys_ref[at, :], q, NT, preferred_element_type=jnp.float32)
        probs = jnp.exp2(scores * (scale * to_log2) - lse2)
        if masked:
            query_row = lax.broadcasted_iota(jnp.int32, (1, row_count), 1)
            query_pos = start + first + query_row // heads
            key_pos = base + lax.broadcasted_iota(jnp.int32, (size, 1), 0)
            probs = jnp.where(key_pos <= query_pos, probs, 0.0)
        centred = lax.dot_general(values_ref[at, :], g_wide, NT, preferred_element_type=jnp.float32)
        grad_scores = (probs * centred).astype(jnp.bfloat16)
        probs_low = probs.astype(jnp.bfloat16)
        total_ref[at, :head_size] += jnp.dot(grad_scores, q, preferred_element_type=jnp.float32)
        total_ref[at, head_size:] += jnp.dot(probs_low, g, preferred_element_type=jnp.float32)
        dq_ref[...] += jnp.dot(keys_t_ref[:, at], grad_scores, preferred_element_type=jnp.float32)

    def dense(index, carry):
        block(index * KEY_BLOCK, KEY_BLOCK, False)
        return carry

    lax.fori_loop(0, full_blocks, dense, 0)
    last = full_blocks * KEY_BLOCK
    short = start - last < KEY_BLOCK // 2

    @pl.when(short)
    def _():
        block(last, KEY_BLOCK // 2, True)

    @pl.when(jnp.logical_not(short))
    def _():
        block(last, KEY_BLOCK, True)


def hand_out(half, count, span_rows, places_ref, total_ref, own_ref, send_refs):
    head_size = total_ref.shape[1] // 2
    scale = head_size**-0.5
    for step, target in enumerate([own_ref, *send_refs]):
        rows = pl.ds(place_of(places_ref, step, half), span_rows)
        target[:, :head_size] = (total_ref[rows, :head_size] * scale).astype(target.dtype)
        target[:, head_size:] = total_ref[rows, head_size:].astype(target.dtype)


def add_terms(term_refs):
    total = term_refs[0][...]
    for term_ref in term_refs[1:]:
        total = total + term_ref[...].astype(jnp.float32)
    return total


def chunk_kernel(
    chunk, heads, span_rows, count, is_first, is_last, hands_out, n_after, q_ref, g_ref, o_ref,
    lse_ref, keys_ref, values_ref, keys_t_ref, places_ref, *refs,
):
    refs = list(refs[n_after:])
    total_in = None if is_first else refs.pop(0)
    total_ref = refs.pop() if is_last else refs.pop(1)
    dq_ref, *handed = refs
    if is_first:
        total_ref[...] = jnp.zeros_like(total_ref)
    else:
        total_ref[...] = total_in[: total_ref.shape[0], :]
    chunk_grads(
        chunk, heads, span_rows, places_ref, q_ref, g_ref, o_ref, lse_ref, keys_ref, values_ref,
        keys_t_ref, total_ref, dq_ref,
    )
    if hands_out:
        hand_out(chunk[0], count, span_rows, places_ref, total_ref, handed[0], handed[1:])


def add_kernel(count, span_rows, head_size, *refs):
    term_refs, upper_ref, (key_ref, value_ref) = refs[:count], refs[count], refs[count + 1 :]
    lower = add_terms(term_refs).astype(jnp.bfloat16)
    for out_ref, columns in ((key_ref, slice(0, head_size)), (value_ref, slice(head_size, None))):
        out_ref[:span_rows, :] = lower[:, columns]
        out_ref[span_rows:, :] = upper_ref[:, columns]


def finish_kernel(count, places, *refs):
    term_refs, refs = refs[:count], refs[count:]
    part_refs, (upper_ref, out_ref, held, sems) = refs[: len(places)], refs[len(places) :]
    scale = out_ref.shape[1] ** -0.5
    copies = []
    for i, (first, part_ref) in enumerate(zip(places, part_refs)):
        rows = pl.ds(first, part_ref.shape[1])
        held[rows, :] = (part_ref[...] * scale).T.astype(jnp.bfloat16)
        copies.append(pltpu.make_async_copy(held.at[rows], out_ref.at[rows], sems.at[i]))
        copies[-1].start()
    upper_ref[...] = add_terms(term_refs).astype(jnp.bfloat16)
    for copy in copies:
        copy.wait()


def finish(terms, parts, places, shape):
    return pl.pallas_call(
        functools.partial(finish_kernel, len(terms), places),
        out_shape=(
            jax.ShapeDtypeStruct(terms[0].shape, jnp.bfloat16),
            jax.ShapeDtypeStruct(shape, jnp.bfloat16),
        ),
        in_specs=[WHOLE] * (len(terms) + len(parts)),
        out_specs=(WHOLE, ANYWHERE),
        scratch_shapes=[
            pltpu.VMEM(shape, jnp.bfloat16),
            pltpu.SemaphoreType.DMA((len(parts),)),
        ],
        compiler_params=params(),
    )(*terms, *parts)


def body(queries, keys, values, outputs, grad_held, lse, span_start):
    count = lax.axis_size("ctx")
    row_count, heads, head_size = queries.shape[1:]
    span_rows = row_count // 2
    total = count * row_count
    chunks = []
    for half, sizes in ((1, UPPER_CHUNKS), (0, LOWER_CHUNKS)):
        chunks += [(half, sum(sizes[:i]), size) for i, size in enumerate(sizes)]

    pieces = cut(grad_held[0], [(half * span_rows + first, size) for half, first, size in chunks])
    grads = [from_behind(pieces[0], "section", -1)]
    pair = jnp.concatenate(lax.optimization_barrier((keys, values, pieces[0]))[:2], axis=0)
    gathered, codes, step = pair, [0], count // 2
    while step:
        held, gathered = gathered, with_partner(gathered, "ctx", step)
        codes = codes + [code ^ step for code in codes]
        if step > 1:
            gathered = stack([held, gathered])
        step //= 2
    for piece, gate in zip(pieces[1:], [None] * (len(pieces) - 2) + [held]):
        if gate is not None:
            piece, _ = lax.optimization_barrier((piece, gate))
        grads.append(from_behind(piece, "section", -1))
    sorted_keys = sort_keys(span_start, [held, gathered], codes, span_rows, head_size)

    q_flat = queries.reshape(row_count * heads, head_size)
    o_flat = outputs.reshape(row_count * heads, head_size)
    lse_flat = lse[0].T.reshape(1, row_count * heads)

    span_wide = (span_rows, 2 * head_size)
    running, received, dq_parts = [], [], []
    for number, chunk in enumerate(chunks):
        half, _, tokens = chunk
        rows = tokens * heads
        is_first, is_last = number == 0, number == len(chunks) - 1
        hands_out = chunk[1] + tokens == span_rows
        after = received[:2] if is_last else []
        if is_last:
            upper_terms = received
        grad = grads[number].reshape(rows, head_size)
        if is_first:
            grad = widen(grad, o_flat, (half * span_rows + chunk[1]) * heads)
        operands = [
            q_flat, grad, o_flat, lse_flat, *sorted_keys, *after,
            *running,
        ]
        total_shape = (total if half else total // 2, 2 * head_size)
        out_shape = [jax.ShapeDtypeStruct((head_size, rows), jnp.float32)]
        if not is_last:
            out_shape.append(jax.ShapeDtypeStruct(total_shape, jnp.float32))
        if hands_out:
            out_shape.append(jax.ShapeDtypeStruct(span_wide, jnp.float32))
            out_shape += [jax.ShapeDtypeStruct(span_wide, jnp.bfloat16)] * (count - 1)
        pairs = rows * (3 * total // 4 if half == 1 else total // 4)
        dq, *handed = pl.pallas_call(
            functools.partial(
                chunk_kernel, chunk, heads, span_rows, count, is_first, is_last, hands_out,
                len(after),
            ),
            out_shape=out_shape,
            in_specs=[WHOLE] * len(operands),
            out_specs=[WHOLE] * len(out_shape),
            scratch_shapes=[pltpu.VMEM(total_shape, jnp.float32)] if is_last else [],
            compiler_params=params(),
            cost_estimate=pl.CostEstimate(
                flops=20 * pairs * head_size, bytes_accessed=2 * 2**20, transcendentals=pairs
            ),
        )(*operands)
        dq_parts.append(dq)
        running = [] if is_last else [handed.pop(0)]
        if hands_out:
            sends = list(enumerate(handed[1:], start=1))
            received = [with_partner(send, "ctx", step) for step, send in reversed(sends)]
            received = [handed[0]] + received[::-1]

    places = [(half * span_rows + first) * heads for half, first, _ in chunks]
    upper_sum, dq = finish(upper_terms, dq_parts, places, q_flat.shape)
    key_out, value_out = pl.pallas_call(
        functools.partial(add_kernel, count, span_rows, head_size),
        out_shape=(jax.ShapeDtypeStruct((row_count, head_size), jnp.bfloat16),) * 2,
        in_specs=[WHOLE] * (count + 1),
        out_specs=(WHOLE,) * 2,
        compiler_params=params(),
    )(*received, upper_sum)
    return (dq.reshape(queries.shape), key_out[None], value_out[None])


def solution(mesh):
    placed = (
        P("section", "ctx", None, None),
        P("section", "ctx", None),
        P("section", "ctx", None),
        P("section", "ctx", None, None),
        P("section", "ctx", None, None),
        P("section", None, "ctx"),
        P(),
    )
    return jax.shard_map(
        body,
        mesh=mesh,
        in_specs=placed,
        out_specs=(
            P("section", "ctx", None, None),
            P("section", "ctx", None),
            P("section", "ctx", None),
        ),
        check_vma=False,
    )
```

```python
import functools
import math

import jax
import jax.numpy as jnp
from jax import lax
from jax.experimental import pallas as pl
from jax.experimental.pallas import tpu as pltpu
from jax.sharding import PartitionSpec as P

KEY_BLOCK = 512
LANES = 128
UPPER_CHUNKS = (64, 64)
LOWER_CHUNKS = (80, 48)
VMEM_LIMIT = 40 * 1024 * 1024
SORT_FLOPS = 10**9
WIDEN_FLOPS = 4 * 10**9

WHOLE = pl.BlockSpec(memory_space=pltpu.VMEM)
SCALARS = pl.BlockSpec(memory_space=pltpu.SMEM)
ANYWHERE = pl.BlockSpec(memory_space=pl.ANY)
NT = (((1,), (1,)), ((), ()))


def from_behind(shard, axis, by):
    length = lax.axis_size(axis)
    return lax.ppermute(shard, axis, [(i, (i + by) % length) for i in range(length)])


def with_partner(shard, axis, step):
    length = lax.axis_size(axis)
    return lax.ppermute(shard, axis, [(i, i ^ step) for i in range(length)])


def params(limit=VMEM_LIMIT):
    return pltpu.CompilerParams(vmem_limit_bytes=limit)


def cut_kernel(cuts, source_ref, *out_refs):
    for (first, size), out_ref in zip(cuts, out_refs):
        out_ref[...] = source_ref[first : first + size]


def cut(source, cuts):
    return pl.pallas_call(
        functools.partial(cut_kernel, cuts),
        out_shape=[
            jax.ShapeDtypeStruct((size, *source.shape[1:]), source.dtype) for _, size in cuts
        ],
        in_specs=[WHOLE],
        out_specs=[WHOLE] * len(cuts),
        compiler_params=params(),
        cost_estimate=pl.CostEstimate(
            flops=0, bytes_accessed=2 * source.size * source.dtype.itemsize, transcendentals=0
        ),
    )(source)


def widen_kernel(rows, g_ref, o_ref, *refs):
    wide_ref = refs[-1]
    head_size = g_ref.shape[1]
    g = g_ref[...]
    wide_ref[:, :head_size] = g
    wide_ref[:, head_size:] = times(g, o_ref[rows, :])


def widen(grad, outputs, first, *others):
    row_count, head_size = grad.shape
    return pl.pallas_call(
        functools.partial(widen_kernel, slice(first, first + row_count)),
        out_shape=jax.ShapeDtypeStruct((row_count, 2 * head_size), grad.dtype),
        in_specs=[WHOLE] * (2 + len(others)),
        out_specs=WHOLE,
        compiler_params=params(),
        cost_estimate=pl.CostEstimate(
            flops=WIDEN_FLOPS, bytes_accessed=grad.size * 8, transcendentals=0
        ),
    )(grad, outputs, *others)


def times(g, o):
    return (g.astype(jnp.float32) * o.astype(jnp.float32)).astype(jnp.bfloat16)


def stack_kernel(*refs):
    *part_refs, out_ref = refs
    first = 0
    for part_ref in part_refs:
        out_ref[first : first + part_ref.shape[0]] = part_ref[...]
        first += part_ref.shape[0]


def stack(parts):
    shape = (sum(part.shape[0] for part in parts), *parts[0].shape[1:])
    return pl.pallas_call(
        stack_kernel,
        out_shape=jax.ShapeDtypeStruct(shape, parts[0].dtype),
        in_specs=[WHOLE] * len(parts),
        out_specs=WHOLE,
        compiler_params=params(),
        cost_estimate=pl.CostEstimate(flops=0, bytes_accessed=2**18, transcendentals=0),
    )(*parts)


def place_of(places_ref, step, half):
    lane = lax.broadcasted_iota(jnp.int32, places_ref.shape, 1)
    place = jnp.max(jnp.where(lane == 2 * step + half, places_ref[...], 0.0))
    return pl.multiple_of(place.astype(jnp.int32), LANES)


def sort_keys_kernel(codes, span_rows, head_size, starts_ref, *refs):
    held_ref, got_ref, keys_ref, values_ref, keys_t_ref, places_ref = refs
    half_count = len(codes) // 2
    blocks = [(ref, 2 * i) for ref in (held_ref, got_ref) for i in range(half_count)]
    me = lax.axis_index("ctx")
    lane = lax.broadcasted_iota(jnp.int32, places_ref.shape, 1)
    places = jnp.zeros(places_ref.shape, jnp.float32)
    values_ref[:, head_size:] = jnp.full(
        (values_ref.shape[0], values_ref.shape[1] - head_size), -1.0, values_ref.dtype
    )
    for (block, at), code in zip(blocks, codes):
        owner = lax.bitwise_xor(me, code)
        for half in range(2):
            start = pl.multiple_of(starts_ref[2 * owner + half], span_rows)
            rows = pl.ds(start, span_rows)
            part = slice(half * span_rows, (half + 1) * span_rows)
            keys = block[at, part, :]
            keys_ref[rows, :] = keys
            values_ref[rows, :head_size] = block[at + 1, part, :]
            keys_t_ref[:, rows] = keys.astype(jnp.float32).T.astype(jnp.bfloat16)
            places = jnp.where(lane == 2 * code + half, start.astype(jnp.float32), places)
    places_ref[...] = places


def sort_keys(span_start, blocks, codes, span_rows, head_size):
    total = len(codes) * 2 * span_rows
    return pl.pallas_call(
        functools.partial(sort_keys_kernel, codes, span_rows, head_size),
        out_shape=(
            jax.ShapeDtypeStruct((total, head_size), jnp.bfloat16),
            jax.ShapeDtypeStruct((total, 2 * head_size), jnp.bfloat16),
            jax.ShapeDtypeStruct((head_size, total), jnp.bfloat16),
            jax.ShapeDtypeStruct((8, LANES), jnp.float32),
        ),
        in_specs=[SCALARS] + [WHOLE] * len(blocks),
        out_specs=(WHOLE,) * 4,
        compiler_params=params(),
        cost_estimate=pl.CostEstimate(
            flops=SORT_FLOPS, bytes_accessed=8 * total * head_size, transcendentals=0
        ),
    )(span_start, *blocks)


def chunk_grads(
    chunk, heads, span_rows, places_ref, q_ref, g_ref, o_ref, lse_ref, keys_ref, values_ref,
    keys_t_ref, total_ref, dq_ref,
):
    half, first, tokens = chunk
    head_size = q_ref.shape[1]
    scale = head_size**-0.5
    to_log2 = math.log2(math.e)
    start = place_of(places_ref, 0, half)
    row_count = tokens * heads
    row_first = (half * span_rows + first) * heads
    rows = slice(row_first, row_first + row_count)
    full_blocks = start // KEY_BLOCK

    q = q_ref[rows, :]
    g = g_ref[...]
    if g.shape[1] == head_size:
        g_wide = jnp.concatenate([g, times(g, o_ref[rows, :])], axis=1)
    else:
        g, g_wide = g[:, :head_size], g
    lse2 = lse_ref[0:1, rows] * to_log2
    dq_ref[...] = jnp.zeros_like(dq_ref)

    def block(base, size, masked):
        base = pl.multiple_of(base, KEY_BLOCK)
        at = pl.ds(base, size)
        scores = lax.dot_general(keys_ref[at, :], q, NT, preferred_element_type=jnp.float32)
        probs = jnp.exp2(scores * (scale * to_log2) - lse2)
        if masked:
            query_row = lax.broadcasted_iota(jnp.int32, (1, row_count), 1)
            query_pos = start + first + query_row // heads
            key_pos = base + lax.broadcasted_iota(jnp.int32, (size, 1), 0)
            probs = jnp.where(key_pos <= query_pos, probs, 0.0)
        centred = lax.dot_general(values_ref[at, :], g_wide, NT, preferred_element_type=jnp.float32)
        grad_scores = (probs * centred).astype(jnp.bfloat16)
        probs_low = probs.astype(jnp.bfloat16)
        total_ref[at, :head_size] += jnp.dot(grad_scores, q, preferred_element_type=jnp.float32)
        total_ref[at, head_size:] += jnp.dot(probs_low, g, preferred_element_type=jnp.float32)
        dq_ref[...] += jnp.dot(keys_t_ref[:, at], grad_scores, preferred_element_type=jnp.float32)

    def dense(index, carry):
        block(index * KEY_BLOCK, KEY_BLOCK, False)
        return carry

    lax.fori_loop(0, full_blocks, dense, 0)
    last = full_blocks * KEY_BLOCK
    short = start - last < KEY_BLOCK // 2

    @pl.when(short)
    def _():
        block(last, KEY_BLOCK // 2, True)

    @pl.when(jnp.logical_not(short))
    def _():
        block(last, KEY_BLOCK, True)


def hand_out(half, count, span_rows, places_ref, total_ref, own_ref, send_refs):
    head_size = total_ref.shape[1] // 2
    scale = head_size**-0.5
    for step, target in enumerate([own_ref, *send_refs]):
        rows = pl.ds(place_of(places_ref, step, half), span_rows)
        target[:, :head_size] = (total_ref[rows, :head_size] * scale).astype(target.dtype)
        target[:, head_size:] = total_ref[rows, head_size:].astype(target.dtype)


def hand_half(half, count, span_rows, places_ref, total_ref, kept_ref, send_ref):
    head_size = total_ref.shape[1] // 2
    scale = head_size**-0.5
    for code in range(count):
        rows = pl.ds(place_of(places_ref, code, half), span_rows)
        target = send_ref if code % 2 else kept_ref
        target[code // 2, :, :head_size] = (total_ref[rows, :head_size] * scale).astype(target.dtype)
        target[code // 2, :, head_size:] = total_ref[rows, head_size:].astype(target.dtype)


def halve_kernel(kept_in_ref, got_ref, kept_ref, send_ref):
    for i in range(kept_in_ref.shape[0]):
        total = kept_in_ref[i] + got_ref[i].astype(jnp.float32)
        target = send_ref if i % 2 else kept_ref
        target[i // 2] = total.astype(target.dtype)


def halve(kept, got):
    shape = (kept.shape[0] // 2, *kept.shape[1:])
    return pl.pallas_call(
        halve_kernel,
        out_shape=(
            jax.ShapeDtypeStruct(shape, jnp.float32),
            jax.ShapeDtypeStruct(shape, jnp.bfloat16),
        ),
        in_specs=[WHOLE] * 2,
        out_specs=(WHOLE,) * 2,
        compiler_params=params(),
    )(kept, got)


def add_terms(term_refs):
    total = term_refs[0][...]
    for term_ref in term_refs[1:]:
        total = total + term_ref[...].astype(jnp.float32)
    return total


def chunk_kernel(
    chunk, heads, span_rows, count, is_first, is_last, hands_out, n_after, q_ref, g_ref, o_ref,
    lse_ref, keys_ref, values_ref, keys_t_ref, places_ref, *refs,
):
    refs = list(refs[n_after:])
    total_in = None if is_first else refs.pop(0)
    total_ref = refs.pop() if is_last else refs.pop(1)
    dq_ref, *handed = refs
    if is_first:
        total_ref[...] = jnp.zeros_like(total_ref)
    else:
        total_ref[...] = total_in[: total_ref.shape[0], :]
    chunk_grads(
        chunk, heads, span_rows, places_ref, q_ref, g_ref, o_ref, lse_ref, keys_ref, values_ref,
        keys_t_ref, total_ref, dq_ref,
    )
    if is_last:
        hand_half(chunk[0], count, span_rows, places_ref, total_ref, *handed)
    elif hands_out:
        hand_out(chunk[0], count, span_rows, places_ref, total_ref, handed[0], handed[1:])


def add_kernel(span_rows, head_size, kept_ref, got_ref, upper_ref, key_ref, value_ref):
    lower = (kept_ref[0] + got_ref[0].astype(jnp.float32)).astype(jnp.bfloat16)
    for out_ref, columns in ((key_ref, slice(0, head_size)), (value_ref, slice(head_size, None))):
        out_ref[:span_rows, :] = lower[:, columns]
        out_ref[span_rows:, :] = upper_ref[:, columns]


def finish_kernel(count, places, *refs):
    term_refs, refs = refs[:count], refs[count:]
    part_refs, (upper_ref, out_ref, held, sems) = refs[: len(places)], refs[len(places) :]
    scale = out_ref.shape[1] ** -0.5
    copies = []
    for i, (first, part_ref) in enumerate(zip(places, part_refs)):
        rows = pl.ds(first, part_ref.shape[1])
        held[rows, :] = (part_ref[...] * scale).T.astype(jnp.bfloat16)
        copies.append(pltpu.make_async_copy(held.at[rows], out_ref.at[rows], sems.at[i]))
        copies[-1].start()
    upper_ref[...] = add_terms(term_refs).astype(jnp.bfloat16)
    for copy in copies:
        copy.wait()


def finish(terms, parts, places, shape):
    return pl.pallas_call(
        functools.partial(finish_kernel, len(terms), places),
        out_shape=(
            jax.ShapeDtypeStruct(terms[0].shape, jnp.bfloat16),
            jax.ShapeDtypeStruct(shape, jnp.bfloat16),
        ),
        in_specs=[WHOLE] * (len(terms) + len(parts)),
        out_specs=(WHOLE, ANYWHERE),
        scratch_shapes=[
            pltpu.VMEM(shape, jnp.bfloat16),
            pltpu.SemaphoreType.DMA((len(parts),)),
        ],
        compiler_params=params(),
    )(*terms, *parts)


def body(queries, keys, values, outputs, grad_held, lse, span_start):
    count = lax.axis_size("ctx")
    row_count, heads, head_size = queries.shape[1:]
    span_rows = row_count // 2
    total = count * row_count
    chunks = []
    for half, sizes in ((1, UPPER_CHUNKS), (0, LOWER_CHUNKS)):
        chunks += [(half, sum(sizes[:i]), size) for i, size in enumerate(sizes)]

    pieces = cut(grad_held[0], [(half * span_rows + first, size) for half, first, size in chunks])
    grads = [from_behind(pieces[0], "section", -1)]
    pair = jnp.concatenate(lax.optimization_barrier((keys, values, pieces[0]))[:2], axis=0)
    gathered, codes, step = pair, [0], count // 2
    while step:
        held, gathered = gathered, with_partner(gathered, "ctx", step)
        codes = codes + [code ^ step for code in codes]
        if step > 1:
            gathered = stack([held, gathered])
        step //= 2
    for piece, gate in zip(pieces[1:], [None] * (len(pieces) - 2) + [held]):
        if gate is not None:
            piece, _ = lax.optimization_barrier((piece, gate))
        grads.append(from_behind(piece, "section", -1))
    sorted_keys = sort_keys(span_start, [held, gathered], codes, span_rows, head_size)

    q_flat = queries.reshape(row_count * heads, head_size)
    o_flat = outputs.reshape(row_count * heads, head_size)
    lse_flat = lse[0].T.reshape(1, row_count * heads)

    span_wide = (span_rows, 2 * head_size)
    running, received, dq_parts = [], [], []
    for number, chunk in enumerate(chunks):
        half, _, tokens = chunk
        rows = tokens * heads
        is_first, is_last = number == 0, number == len(chunks) - 1
        hands_out = chunk[1] + tokens == span_rows
        after = received if is_last else []
        if is_last:
            upper_terms = received
        grad = grads[number].reshape(rows, head_size)
        if is_first:
            grad = widen(grad, o_flat, (half * span_rows + chunk[1]) * heads)
        operands = [
            q_flat, grad, o_flat, lse_flat, *sorted_keys, *after,
            *running,
        ]
        total_shape = (total if half else total // 2, 2 * head_size)
        out_shape = [jax.ShapeDtypeStruct((head_size, rows), jnp.float32)]
        if not is_last:
            out_shape.append(jax.ShapeDtypeStruct(total_shape, jnp.float32))
        if is_last:
            out_shape.append(jax.ShapeDtypeStruct((count // 2, *span_wide), jnp.float32))
            out_shape.append(jax.ShapeDtypeStruct((count // 2, *span_wide), jnp.bfloat16))
        elif hands_out:
            out_shape.append(jax.ShapeDtypeStruct(span_wide, jnp.float32))
            out_shape += [jax.ShapeDtypeStruct(span_wide, jnp.bfloat16)] * (count - 1)
        pairs = rows * (3 * total // 4 if half == 1 else total // 4)
        dq, *handed = pl.pallas_call(
            functools.partial(
                chunk_kernel, chunk, heads, span_rows, count, is_first, is_last, hands_out,
                len(after),
            ),
            out_shape=out_shape,
            in_specs=[WHOLE] * len(operands),
            out_specs=[WHOLE] * len(out_shape),
            scratch_shapes=[pltpu.VMEM(total_shape, jnp.float32)] if is_last else [],
            compiler_params=params(),
            cost_estimate=pl.CostEstimate(
                flops=20 * pairs * head_size, bytes_accessed=2 * 2**20, transcendentals=pairs
            ),
        )(*operands)
        dq_parts.append(dq)
        running = [] if is_last else [handed.pop(0)]
        if is_last:
            kept, send = handed
            got, step = with_partner(send, "ctx", 1), 2
            while step < count:
                kept, send = halve(kept, got)
                got, step = with_partner(send, "ctx", step), 2 * step
        elif hands_out:
            received = [handed[0]] + [
                with_partner(send, "ctx", step) for step, send in enumerate(handed[1:], start=1)
            ]

    places = [(half * span_rows + first) * heads for half, first, _ in chunks]
    upper_sum, dq = finish(upper_terms, dq_parts, places, q_flat.shape)
    key_out, value_out = pl.pallas_call(
        functools.partial(add_kernel, span_rows, head_size),
        out_shape=(jax.ShapeDtypeStruct((row_count, head_size), jnp.bfloat16),) * 2,
        in_specs=[WHOLE] * 3,
        out_specs=(WHOLE,) * 2,
        compiler_params=params(),
    )(kept, got, upper_sum)
    return (dq.reshape(queries.shape), key_out[None], value_out[None])


def solution(mesh):
    placed = (
        P("section", "ctx", None, None),
        P("section", "ctx", None),
        P("section", "ctx", None),
        P("section", "ctx", None, None),
        P("section", "ctx", None, None),
        P("section", None, "ctx"),
        P(),
    )
    return jax.shard_map(
        body,
        mesh=mesh,
        in_specs=placed,
        out_specs=(
            P("section", "ctx", None, None),
            P("section", "ctx", None),
            P("section", "ctx", None),
        ),
        check_vma=False,
    )
```
